32 devices in a mesh: section: 2 (over core), dp: 16 (over z, y, x).
Axes of the slice: x: 2, y: 2, z: 4, core: 2. Of those that a mesh axis runs over, the one named last changes fastest.
Arguments:
- global_ends: bfloat16 [2, 32, 197, 384], P('section', 'dp'), may hold values from -6 to 6
- local_ends: bfloat16 [2, 160, 37, 384], P('section', 'dp'), may hold values from -6 to 6
- global_live: int32 [32], P('dp'), may hold values from 0 to 1, as said below
- local_live: int32 [160], P('dp'), may hold values from 0 to 1, as said below
- ln1_gain: bfloat16 [2, 384], P('section'), may hold values from 0.25 to 1.75
- ln1_bias: bfloat16 [2, 384], P('section'), may hold values from -3 to 3
- qkv_weight: bfloat16 [2, 384, 1152], P('section'), may hold values from -0.3125 to 0.3125
- query_bias: bfloat16 [2, 384], P('section'), may hold values from -3 to 3
- value_bias: bfloat16 [2, 384], P('section'), may hold values from -3 to 3
- proj_weight: bfloat16 [2, 384, 384], P('section'), may hold values from -1.25 to 1.25
- proj_bias: bfloat16 [2, 384], P('section'), may hold values from -3 to 3
- ln2_gain: bfloat16 [2, 384], P('section'), may hold values from 0.25 to 1.75
- ln2_bias: bfloat16 [2, 384], P('section'), may hold values from -3 to 3
- fc1_weight: bfloat16 [2, 384, 1536], P('section'), may hold values from -0.3125 to 0.3125
- fc1_bias: bfloat16 [2, 1536], P('section'), may hold values from -3 to 3
- fc2_weight: bfloat16 [2, 1536, 384], P('section'), may hold values from -0.15625 to 0.15625
- fc2_bias: bfloat16 [2, 384], P('section'), may hold values from -3 to 3
Outputs:
- global_result: bfloat16 [2, 32, 197, 384], P('section', 'dp')
- local_result: bfloat16 [2, 160, 37, 384], P('section', 'dp')
- grad_ln1_gain: float32 [2, 384], P('section')
- grad_ln1_bias: float32 [2, 384], P('section')
- grad_qkv_weight: float32 [2, 384, 1152], P('section')
- grad_query_bias: float32 [2, 384], P('section')
- grad_value_bias: float32 [2, 384], P('section')
- grad_proj_weight: float32 [2, 384, 384], P('section')
- grad_proj_bias: float32 [2, 384], P('section')
- grad_ln2_gain: float32 [2, 384], P('section')
- grad_ln2_bias: float32 [2, 384], P('section')
- grad_fc1_weight: float32 [2, 384, 1536], P('section')
- grad_fc1_bias: float32 [2, 1536], P('section')
- grad_fc2_weight: float32 [2, 1536, 384], P('section')
- grad_fc2_bias: float32 [2, 384], P('section')
The draws below stay inside these ranges and needn't reach their ends.
Inputs may be any that keep to these rules, and one draw needn't show every extreme that they name: `global_live`: device d of dp holds slots d * 2 to (d + 1) * 2 - 1; on some device every global and every local slot is live. `local_live`: device d of dp holds slots d * 10 to (d + 1) * 10 - 1; on some device every global and every local slot is live.
All inputs are finite; a program needn't handle non-finite values.
Results may differ from the reference program's by a relative error of at most 0.015.
Values may be sent and summed in bfloat16 or wider, within the bound.
No kernel may reach another device: no remote copies, remote signals or barrier semaphores. Data moves between devices by JAX's collectives and lax.ppermute only.
A program may use at most 128 MiB of HBM per device.

```python
import jax
import jax.numpy as jnp
from jax import lax

D = 384
HEAD = 64
FF = 1536
GT = 197
LT = 37
GC_DEV = 2
LC_DEV = 10
NG = 32
NL = 160
N_DP = 16


def device_levels(key):
    levels = jax.random.randint(jax.random.fold_in(key, 11), (N_DP,), 1, 5)
    fullest = jax.random.randint(jax.random.fold_in(key, 12), (), 0, N_DP)
    return jnp.where(jnp.arange(N_DP) == fullest, 4, levels)


def live_slots(key, levels, per_device):
    picks = jax.random.randint(key, (N_DP, per_device), 0, 4)
    return (picks < levels[:, None]).astype(jnp.int32).reshape(N_DP * per_device)


def draw_global_live(key, part):
    levels = device_levels(key)
    key = jax.random.fold_in(key, 1)
    return live_slots(key, levels, GC_DEV)


def draw_local_live(key, part):
    levels = device_levels(key)
    key = jax.random.fold_in(key, 2)
    return live_slots(key, levels, LC_DEV)


def level_of(stream_key, extent, pieces, least, top_value):
    factor_of = 1.0
    for position, parts in pieces:
        heights = jax.random.uniform(jax.random.fold_in(jax.random.fold_in(stream_key, 6), position), (parts,), jnp.float32, least / len(pieces), top_value / len(pieces))
        factor_of = factor_of * jnp.repeat(jnp.exp(heights), extent[position] // parts).reshape((-1,) + (1,) * (len(extent) - 1 - position))
    return factor_of


def normal_values(stream_key, extent, width, most, pieces=(), held_as=jnp.bfloat16):
    array = width * jax.random.normal(stream_key, extent, jnp.float32)
    if pieces:
        array = array * level_of(stream_key, extent, pieces, -0.22, 0.18)
    return jnp.clip(array, -most, most).astype(held_as)


def setup_inputs(seed: int = 0) -> dict:
    seeds = jax.random.split(jax.random.key(seed), 18)
    return {
        "global_ends": normal_values(seeds[0], (2, NG, GT, D), 1.0, 6.0, ((0, 2), (1, 16))),
        "local_ends": normal_values(seeds[1], (2, NL, LT, D), 1.0, 6.0, ((0, 2), (1, 16))),
        "global_live": draw_global_live(jax.random.fold_in(seeds[17], 71), 0),
        "local_live": draw_local_live(jax.random.fold_in(seeds[17], 71), 0),
        "ln1_gain": jnp.clip(1.0 + 0.15 * jax.random.normal(seeds[4], (2, D), jnp.float32), 0.25, 1.75).astype(jnp.bfloat16),
        "ln1_bias": normal_values(seeds[5], (2, D), 0.3, 3.0, ((0, 2),)),
        "qkv_weight": normal_values(seeds[6], (2, D, 3 * D), D ** -0.5, 0.3125, ((0, 2),)),
        "query_bias": normal_values(seeds[7], (2, D), 0.5, 3.0, ((0, 2),)),
        "value_bias": normal_values(seeds[8], (2, D), 0.5, 3.0, ((0, 2),)),
        "proj_weight": normal_values(seeds[9], (2, D, D), (D // 16) ** -0.5, 1.25, ((0, 2),)),
        "proj_bias": normal_values(seeds[10], (2, D), 0.3, 3.0, ((0, 2),)),
        "ln2_gain": jnp.clip(1.0 + 0.15 * jax.random.normal(seeds[11], (2, D), jnp.float32), 0.25, 1.75).astype(jnp.bfloat16),
        "ln2_bias": normal_values(seeds[12], (2, D), 0.3, 3.0, ((0, 2),)),
        "fc1_weight": normal_values(seeds[13], (2, D, FF), D ** -0.5, 0.3125, ((0, 2),)),
        "fc1_bias": normal_values(seeds[14], (2, FF), 0.5, 3.0, ((0, 2),)),
        "fc2_weight": normal_values(seeds[15], (2, FF, D), FF ** -0.5, 0.15625, ((0, 2),)),
        "fc2_bias": normal_values(seeds[16], (2, D), 0.3, 3.0, ((0, 2),)),
    }


@jax.custom_vjp
def low(v):
    return lax.optimization_barrier(v.astype(jnp.bfloat16)).astype(jnp.float32)

@jax.custom_vjp
def low_back(v):
    return v

def low_keep(v):
    return (low(v), None)

def low_pass(kept, grad):
    return (grad,)

def back_keep(v):
    return (v, None)

def back_low(kept, grad):
    return (low(grad),)
low.defvjp(low_keep, low_pass)
low_back.defvjp(back_keep, back_low)
EPSILON = 1e-06

def layer_norm(values_in, gain_vector, shift_vector):
    centred = values_in - lax.optimization_barrier(jnp.mean(values_in, axis=-1, keepdims=True))
    spread = lax.optimization_barrier(jnp.mean(centred * centred, axis=-1, keepdims=True))
    return centred * lax.rsqrt(spread + EPSILON) * gain_vector + shift_vector

def project(values_in, matrix):
    return jnp.einsum('csi,io->cso', values_in, matrix, precision=lax.Precision.HIGHEST)

def one_layer(crop_rows, params):
    ln1_gain, ln1_bias, qkv_weight, query_bias, value_bias, proj_weight, proj_bias, ln2_gain, ln2_bias, fc1_weight, fc1_bias, fc2_weight, fc2_bias = params
    crop_count, crop_length, features = crop_rows.shape
    head_count = features // HEAD
    split_shape = (crop_count, crop_length, head_count, HEAD)
    normed = low(layer_norm(crop_rows, ln1_gain, ln1_bias))
    triple = project(normed, qkv_weight)
    queries = low_back(low(triple[..., :features] + query_bias)).reshape(split_shape)
    key_rows = low_back(low(triple[..., features:2 * features])).reshape(split_shape)
    value_rows = low_back(low(triple[..., 2 * features:] + value_bias)).reshape(split_shape)
    scores = low_back(jnp.einsum('cqhe,ckhe->chqk', queries, key_rows, precision=lax.Precision.HIGHEST) * HEAD ** (-0.5))
    soft_weights = low(jax.nn.softmax(scores, axis=-1))
    mixed = jnp.einsum('chqk,ckhe->cqhe', soft_weights, value_rows, precision=lax.Precision.HIGHEST)
    mixed = low_back(low(mixed.reshape(crop_count, crop_length, features)))
    middle = crop_rows + low_back(project(mixed, proj_weight) + proj_bias)
    second_normed = low(layer_norm(middle, ln2_gain, ln2_bias))
    hidden = low_back(project(second_normed, fc1_weight) + fc1_bias)
    active = low(jax.nn.gelu(hidden, approximate=False))
    return middle + (project(active, fc2_weight) + fc2_bias)

def both_layers(params, crop_rows, live_crops):
    first_layer = tuple((weight[0] for weight in params))
    second_layer = tuple((weight[1] for weight in params))
    between = low_back(low(one_layer(crop_rows, first_layer)))
    return one_layer(between, second_layer) * live_crops[:, None, None]

def reference(global_ends, local_ends, global_live, local_live, ln1_gain, ln1_bias, qkv_weight, query_bias, value_bias, proj_weight, proj_bias, ln2_gain, ln2_bias, fc1_weight, fc1_bias, fc2_weight, fc2_bias):
    params = tuple((weight.astype(jnp.float32) for weight in (ln1_gain, ln1_bias, qkv_weight, query_bias, value_bias, proj_weight, proj_bias, ln2_gain, ln2_bias, fc1_weight, fc1_bias, fc2_weight, fc2_bias)))
    start_global = global_ends[0].astype(jnp.float32).reshape(N_DP, GC_DEV, GT, D)
    start_local = local_ends[0].astype(jnp.float32).reshape(N_DP, LC_DEV, LT, D)
    live_global = global_live.astype(jnp.float32).reshape(N_DP, GC_DEV)
    live_local = local_live.astype(jnp.float32).reshape(N_DP, LC_DEV)

    def block_pass(weights_in, crops_global, crops_local, alive_global, alive_local):
        return (both_layers(weights_in, crops_global, alive_global), both_layers(weights_in, crops_local, alive_local))
    checked = jax.checkpoint(block_pass)

    def forward(weights_in, first_global, first_local):

        def scan_step(carried, inputs_block):
            made = checked(weights_in, inputs_block[0], inputs_block[1], inputs_block[2], inputs_block[3])
            return (carried, made)
        unused_carry, results = lax.scan(scan_step, None, (first_global, first_local, live_global, live_local))
        return results
    results, pullback = jax.vjp(forward, params, start_global, start_local)
    cotangent = (global_ends[1].astype(jnp.float32).reshape(N_DP, GC_DEV, GT, D), local_ends[1].astype(jnp.float32).reshape(N_DP, LC_DEV, LT, D))
    gradients, grad_global, grad_local = pullback(cotangent)
    global_result = jnp.stack([grad_global.reshape(NG, GT, D), results[0].reshape(NG, GT, D)]).astype(jnp.bfloat16)
    local_result = jnp.stack([grad_local.reshape(NL, LT, D), results[1].reshape(NL, LT, D)]).astype(jnp.bfloat16)
    return (global_result, local_result, gradients[0], gradients[1], gradients[2], gradients[3], gradients[4], gradients[5], gradients[6], gradients[7], gradients[8], gradients[9], gradients[10], gradients[11], gradients[12])
```

```python
import functools

import jax
import jax.numpy as jnp
from jax import lax
from jax.experimental import pallas as pl
from jax.experimental.pallas import tpu as pltpu
from jax.sharding import PartitionSpec as P

HEAD = 64
GT = 197
LT = 37
WIDTH = 384
FF = 1536
SEQ = 208
ROWS = 2 * SEQ
SLOT = 40
LOCALS = 5
VECS = 16
BLOCKS = 12
HALF_ROWS = BLOCKS // 2 * WIDTH
EPSILON = 1e-06
MASKED = -1e30
LN1G, LN1B, QB, VB, PB, LN2G, LN2B, F2B, F1B = range(9)
VMEM_LIMIT = 56 * 1024 * 1024
BF16 = jnp.bfloat16
F32 = jnp.float32
ANY = pl.BlockSpec(memory_space=pl.ANY)
VMEM = pl.BlockSpec(memory_space=pltpu.VMEM)
SMEM = pl.BlockSpec(memory_space=pltpu.SMEM)


def mm(left, right):
    return jnp.dot(left, right, preferred_element_type=F32)


def mm_right_t(left, right):
    return lax.dot_general(left, right, (((1,), (1,)), ((), ())), preferred_element_type=F32)


def mm_left_t(left, right):
    return lax.dot_general(left, right, (((0,), (0,)), ((), ())), preferred_element_type=F32)


def normalise(values_in):
    centred = values_in - jnp.mean(values_in, axis=-1, keepdims=True)
    scale = lax.rsqrt(jnp.mean(centred * centred, axis=-1, keepdims=True) + EPSILON)
    return centred * scale, scale


def normalise_back(unit, scale, grad_rows, gain):
    e = grad_rows * gain
    return scale * (
        e
        - jnp.mean(e, axis=-1, keepdims=True)
        - unit * jnp.mean(e * unit, axis=-1, keepdims=True)
    )


def seq_rows(seq):
    return pl.ds(pl.multiple_of(seq * SEQ, 16), SEQ)


def column(block):
    return slice(block * WIDTH, (block + 1) * WIDTH)


def row_sum(values_in):
    return jnp.sum(values_in, axis=0, keepdims=True)


def pack_kernel(glive, llive, g, l, *refs):
    vecs, (keep, send, rows, tail) = refs[:9], refs[9:]
    core = lax.axis_index("section")
    tail[...] = jnp.zeros_like(tail)
    for i, vec in enumerate(vecs[:8]):
        tail[i : i + 1, :] = vec[...].astype(F32)
    for i in range(FF // WIDTH):
        tail[F1B + i : F1B + i + 1, :] = vecs[8][:, column(i)].astype(F32)
    tail_low = tail[...].astype(BF16)
    rows[...] = jnp.zeros_like(rows)
    for out, half in ((keep, core), (send, 1 - core)):
        live = jnp.where(core == 1, glive[half], 1).astype(F32)
        rows[:GT, :] = g[half].astype(F32) * live
        for j in range(LOCALS):
            live = jnp.where(core == 1, llive[half * LOCALS + j], 1).astype(F32)
            rows[SEQ + j * SLOT : SEQ + j * SLOT + LT, :] = l[half * LOCALS + j].astype(F32) * live
        out[:ROWS, :] = rows[...].astype(BF16)
        out[ROWS:, :] = tail_low


def fill_masks(masks):
    row = lax.broadcasted_iota(jnp.int32, (SEQ, SEQ), 0)
    col = lax.broadcasted_iota(jnp.int32, (SEQ, SEQ), 1)
    masks[0] = jnp.where(col < GT, 0.0, MASKED)
    inside = jnp.zeros((SEQ, SEQ), jnp.bool_)
    for j in range(LOCALS):
        inside = inside | (
            (row >= j * SLOT)
            & (row < (j + 1) * SLOT)
            & (col >= j * SLOT)
            & (col < j * SLOT + LT)
        )
    masks[1] = jnp.where(inside, 0.0, MASKED)


def head_lanes():
    lane = lax.broadcasted_iota(jnp.int32, (SEQ, 2 * HEAD), 1)
    return (lane < HEAD, lane >= HEAD)


def only(mask, values_in):
    return jnp.where(mask, values_in, jnp.zeros_like(values_in))


def attention_forward(x, vec, masks, qkv_w, proj_w, n1, qkv, probs, mixed, middle):
    def body(seq, carry):
        rows = seq_rows(seq)
        x_rows = x[rows, :].astype(F32)
        unit, _ = normalise(x_rows)
        normed = (unit * vec[LN1G : LN1G + 1, :] + vec[LN1B : LN1B + 1, :]).astype(BF16)
        n1[rows, :] = normed
        for part in range(3):
            value = mm(normed, qkv_w[:, column(part)])
            if part == 0:
                value = (value + vec[QB : QB + 1, :]).astype(BF16) * BF16(HEAD**-0.5)
            if part == 2:
                value = value + vec[VB : VB + 1, :]
            qkv[rows, column(part)] = value.astype(BF16)
        lanes = head_lanes()
        mask = masks[seq]
        for pair in range(3):
            q = qkv[rows, pair * 128 : pair * 128 + 128]
            k = qkv[rows, WIDTH + pair * 128 : WIDTH + pair * 128 + 128]
            v = qkv[rows, 2 * WIDTH + pair * 128 : 2 * WIDTH + pair * 128 + 128]
            total = None
            for a in range(2):
                s = mm_right_t(only(lanes[a], q), k) + mask
                e = jnp.exp(s - jnp.max(s, axis=-1, keepdims=True))
                p = (e * (1.0 / jnp.sum(e, axis=-1, keepdims=True))).astype(BF16)
                probs[seq * 6 + pair * 2 + a] = p
                part = mm(p, only(lanes[a], v))
                total = part if total is None else total + part
            mixed[rows, pair * 128 : pair * 128 + 128] = total.astype(BF16)
        middle[rows, :] = x_rows + (mm(mixed[rows, :], proj_w[...]) + vec[PB : PB + 1, :])
        return carry

    lax.fori_loop(0, 2, body, 0)


def mlp_forward(vec, fc1_w, fc2_w, middle, n2, slope, active, result):
    def body(seq, carry):
        rows = seq_rows(seq)
        unit, _ = normalise(middle[rows, :])
        normed = (unit * vec[LN2G : LN2G + 1, :] + vec[LN2B : LN2B + 1, :]).astype(BF16)
        n2[rows, :] = normed
        for part in range(FF // WIDTH):
            hidden = mm(normed, fc1_w[:, column(part)]) + vec[F1B + part : F1B + part + 1, :]
            cdf = 0.5 + 0.5 * lax.erf(hidden * (0.5**0.5))
            active[rows, column(part)] = (hidden * cdf).astype(BF16)
            density = jnp.exp(hidden * hidden * -0.5) * 0.3989422804014327
            slope[rows, column(part)] = (cdf + hidden * density).astype(BF16)
        y = middle[rows, :] + (mm(active[rows, :], fc2_w[...]) + vec[F2B : F2B + 1, :])
        result[rows, :] = y.astype(BF16)
        return carry

    lax.fori_loop(0, 2, body, 0)


def mlp_backward(vec, fc1_w, fc2_w, middle, n2, slope, active, dy, dh, dmid, da, sums, emit):
    def body(seq, carry):
        rows = seq_rows(seq)
        dy_rows = dy[rows, :]
        for part in range(FF // WIDTH):
            dactive = mm_right_t(dy_rows, fc2_w[column(part), :])
            low = (slope[rows, column(part)].astype(F32) * dactive).astype(BF16)
            dh[rows, column(part)] = low
            sums[F1B + part : F1B + part + 1, :] += row_sum(low.astype(F32))
        dn2 = mm_right_t(dh[rows, :], fc1_w[...])
        unit, scale = normalise(middle[rows, :])
        dy_wide = dy_rows.astype(F32)
        grad = dy_wide + normalise_back(unit, scale, dn2, vec[LN2G : LN2G + 1, :])
        dmid[rows, :] = grad
        low = grad.astype(BF16)
        da[rows, :] = low
        sums[LN2G : LN2G + 1, :] += row_sum(dn2 * unit)
        sums[LN2B : LN2B + 1, :] += row_sum(dn2)
        sums[F2B : F2B + 1, :] += row_sum(dy_wide)
        sums[PB : PB + 1, :] += row_sum(low.astype(F32))
        return carry

    lax.fori_loop(0, 2, body, 0)
    for part in range(FF // WIDTH):
        emit(part, mm_left_t(active[:, column(part)], dy[:ROWS, :]))
    for part in range(FF // WIDTH):
        emit(4 + part, mm_left_t(n2[...], dh[:, column(part)]))


def attention_backward(
    x, vec, qkv_w, proj_w, n1, qkv, probs, mixed, dmid, da, dt, sums, emit, result
):
    def body(seq, carry):
        rows = seq_rows(seq)
        dmixed = mm_right_t(da[rows, :], proj_w[...]).astype(BF16)
        lanes = head_lanes()
        for pair in range(3):
            q = qkv[rows, pair * 128 : pair * 128 + 128]
            k = qkv[rows, WIDTH + pair * 128 : WIDTH + pair * 128 + 128]
            v = qkv[rows, 2 * WIDTH + pair * 128 : 2 * WIDTH + pair * 128 + 128]
            dm = dmixed[:, pair * 128 : pair * 128 + 128]
            dq = dk = dv = None
            for a in range(2):
                dm_a = only(lanes[a], dm)
                p = probs[seq * 6 + pair * 2 + a]
                dp = mm_right_t(dm_a, v)
                p_wide = p.astype(F32)
                ds = p_wide * (dp - jnp.sum(dp * p_wide, axis=-1, keepdims=True))
                ds = ds.astype(BF16)
                parts = (
                    mm(ds, only(lanes[a], k)),
                    mm_left_t(ds, only(lanes[a], q)),
                    mm_left_t(p, dm_a),
                )
                if a == 0:
                    dq, dk, dv = parts
                else:
                    dq, dk, dv = dq + parts[0], dk + parts[1], dv + parts[2]
            dq = (dq * HEAD**-0.5).astype(BF16)
            dv = dv.astype(BF16)
            here = slice(pair * 128, pair * 128 + 128)
            dt[rows, pair * 128 : pair * 128 + 128] = dq
            dt[rows, WIDTH + pair * 128 : WIDTH + pair * 128 + 128] = dk.astype(BF16)
            dt[rows, 2 * WIDTH + pair * 128 : 2 * WIDTH + pair * 128 + 128] = dv
            sums[QB : QB + 1, here] += row_sum(dq.astype(F32))
            sums[VB : VB + 1, here] += row_sum(dv.astype(F32))
        dn1 = mm_right_t(dt[rows, :], qkv_w[...])
        unit, scale = normalise(x[rows, :].astype(F32))
        grad = dmid[rows, :] + normalise_back(unit, scale, dn1, vec[LN1G : LN1G + 1, :])
        result[rows, :] = grad.astype(BF16)
        sums[LN1G : LN1G + 1, :] += row_sum(dn1 * unit)
        sums[LN1B : LN1B + 1, :] += row_sum(dn1)
        return carry

    lax.fori_loop(0, 2, body, 0)
    emit(8, mm_left_t(mixed[...], da[...]))
    for part in range(3):
        emit(9 + part, mm_left_t(n1[...], dt[:, column(part)]))


def make_emit(grads, core):
    def emit(block, value):
        half = block % 2
        place = block // 2
        grads[half ^ core, place * WIDTH : (place + 1) * WIDTH, :] = value.astype(BF16)

    return emit


def start_all(copies):
    for copy in copies:
        copy.start()


def wait_all(copies):
    for copy in copies:
        copy.wait()


def forward_kernel(*refs):
    (
        keep, recv, qkv_own, proj_own, fc1_own, fc2_own,
        qkv_got, proj_got, fc1_got, fc2_got,
        n1_out, qkv_out, probs_out, mixed_out, middle_out, n2_out, slope_out, active_out,
        result_out, dx_out, keep_out, send_out,
        pack, qkv_w, proj_w, fc1_w, fc2_w, vec, masks, between,
        n1, qkv, probs, mixed, middle, n2, slope, active,
        result, dh, dmid, da, dt, dx, sums, grads, in_sem, out_sem,
    ) = refs
    core = lax.axis_index("section")
    other = 1 - core
    own = (keep, qkv_own, proj_own, fc1_own, fc2_own)
    got = (recv, qkv_got, proj_got, fc1_got, fc2_got)
    held = (pack, qkv_w, proj_w, fc1_w, fc2_w)

    def loads(sources, layer):
        return [
            pltpu.make_async_copy(source, place.at[layer], in_sem.at[layer, i])
            for i, (source, place) in enumerate(zip(sources, held))
        ]

    start_all(loads(own, core))
    start_all(loads(got, other))
    fill_masks(masks)
    sums[...] = jnp.zeros_like(sums)
    wait_all(loads(own, 0))
    for layer in range(2):
        if layer == 1:
            wait_all(loads(own, 1)[:1])
        vec[layer] = pack[layer, ROWS:, :].astype(F32)
    saves = []
    for layer in range(2):
        if layer == 1:
            wait_all(loads(own, 1)[1:])
        x = pack.at[0] if layer == 0 else between
        attention_forward(
            x, vec.at[layer], masks, qkv_w.at[layer], proj_w.at[layer],
            n1.at[layer], qkv.at[layer], probs.at[layer], mixed.at[layer], middle.at[layer],
        )
        mlp_forward(
            vec.at[layer], fc1_w.at[layer], fc2_w.at[layer], middle.at[layer], n2.at[layer],
            slope.at[layer], active.at[layer], between if layer == 0 else result,
        )
        if layer == 0:
            pairs = (
                (n1, n1_out), (qkv, qkv_out), (probs, probs_out), (mixed, mixed_out),
                (middle, middle_out), (n2, n2_out), (slope, slope_out), (active, active_out),
            )
            saves = [
                pltpu.make_async_copy(source.at[0], place, out_sem.at[i])
                for i, (source, place) in enumerate(pairs)
            ]
            start_all(saves)
    result_copy = pltpu.make_async_copy(result, result_out, out_sem.at[8])
    result_copy.start()
    emit = make_emit(grads, core)
    mlp_backward(
        vec.at[1], fc1_w.at[1], fc2_w.at[1], middle.at[1], n2.at[1], slope.at[1], active.at[1],
        pack.at[1], dh, dmid, da, sums, emit,
    )
    attention_backward(
        between, vec.at[1], qkv_w.at[1], proj_w.at[1], n1.at[1], qkv.at[1], probs.at[1],
        mixed.at[1], dmid, da, dt, sums, emit, dx,
    )
    for place in range(2):
        grads[place, HALF_ROWS:, :] = sums[...].astype(BF16)
    last = [
        pltpu.make_async_copy(dx, dx_out, out_sem.at[9]),
        pltpu.make_async_copy(grads.at[0], keep_out, out_sem.at[10]),
        pltpu.make_async_copy(grads.at[1], send_out, out_sem.at[11]),
    ]
    start_all(last)
    wait_all(saves + [result_copy] + last)


def backward_kernel(*refs):
    (
        keep, recv, qkv_own, proj_own, fc1_own, fc2_own,
        qkv_got, proj_got, fc1_got, fc2_got,
        n1_in, qkv_in, probs_in, mixed_in, middle_in, n2_in, slope_in, active_in, dx_in, out_in,
        rows_keep, rows_send, keep_out, send_out,
        pack, qkv_w, proj_w, fc1_w, fc2_w, vec,
        n1, qkv, probs, mixed, middle, n2, slope, active, dy,
        dh, dmid, da, dt, dx, sums, grads, in_sem, out_sem,
    ) = refs
    core = lax.axis_index("section")
    own = (keep, qkv_own, proj_own, fc1_own, fc2_own)
    got = (recv, qkv_got, proj_got, fc1_got, fc2_got)
    held = (pack, qkv_w, proj_w, fc1_w, fc2_w)

    def loads(sources):
        return [
            pltpu.make_async_copy(source, place, in_sem.at[i])
            for i, (source, place) in enumerate(zip(sources, held))
        ]

    saved = (
        (middle_in, middle), (slope_in, slope), (active_in, active), (n2_in, n2), (dx_in, dy),
        (n1_in, n1), (qkv_in, qkv), (probs_in, probs), (mixed_in, mixed),
    )
    saved = [
        pltpu.make_async_copy(source, place, in_sem.at[5 + i])
        for i, (source, place) in enumerate(saved)
    ]

    @pl.when(core == 0)
    def _():
        start_all(loads(own))
        pltpu.make_async_copy(out_in, rows_send, out_sem.at[0]).start()

    @pl.when(core == 1)
    def _():
        start_all(loads(got))
        pltpu.make_async_copy(out_in, rows_keep, out_sem.at[0]).start()

    start_all(saved)
    sums[...] = jnp.zeros_like(sums)
    wait_all(loads(own))
    wait_all(saved[:5])
    vec[...] = pack[ROWS:, :].astype(F32)
    emit = make_emit(grads, core)
    mlp_backward(
        vec, fc1_w, fc2_w, middle, n2, slope, active, dy, dh, dmid, da, sums, emit
    )
    wait_all(saved[5:])
    attention_backward(
        pack, vec, qkv_w, proj_w, n1, qkv, probs, mixed, dmid, da, dt, sums, emit, dx
    )
    for place in range(2):
        grads[place, HALF_ROWS:, :] = sums[...].astype(BF16)
    last = [
        pltpu.make_async_copy(grads.at[0], keep_out, out_sem.at[2]),
        pltpu.make_async_copy(grads.at[1], send_out, out_sem.at[3]),
    ]
    start_all(last)

    @pl.when(core == 0)
    def _():
        pltpu.make_async_copy(dx, rows_keep, out_sem.at[1]).start()

    @pl.when(core == 1)
    def _():
        pltpu.make_async_copy(dx, rows_send, out_sem.at[1]).start()

    wait_all(last)
    pltpu.make_async_copy(dx, rows_keep, out_sem.at[1]).wait()
    pltpu.make_async_copy(out_in, rows_send, out_sem.at[0]).wait()


def rows_kernel(glive, llive, keep, recv, g_out, l_out, wide):
    core = lax.axis_index("section")
    for source, half in ((keep, core), (recv, 1 - core)):
        wide[...] = source[...].astype(F32)
        live = jnp.where(core == 1, glive[half], 1).astype(F32)
        g_out[half] = (wide[:GT, :] * live).astype(BF16)
        for j in range(LOCALS):
            live = jnp.where(core == 1, llive[half * LOCALS + j], 1).astype(F32)
            piece = wide[SEQ + j * SLOT : SEQ + j * SLOT + LT, :]
            l_out[half * LOCALS + j] = (piece * live).astype(BF16)


def grads_kernel(*refs):
    (
        half_a, half_b, got_a, got_b, sums_a, sums_b,
        ln1g, ln1b, qkv, qb, vb, proj, pb, ln2g, ln2b, fc1, fc1b, fc2, fc2b,
        halves, sums, sem,
    ) = refs
    core = lax.axis_index("section")

    def copies(own, got, vectors, first):
        return [
            pltpu.make_async_copy(own, halves.at[first], sem.at[0]),
            pltpu.make_async_copy(got, halves.at[1 - first], sem.at[1]),
            pltpu.make_async_copy(vectors, sums, sem.at[2]),
        ]

    @pl.when(core == 0)
    def _():
        start_all(copies(half_a, got_a, sums_a, 0))

    @pl.when(core == 1)
    def _():
        start_all(copies(half_b, got_b, sums_b, 1))

    wait_all(copies(half_a, got_a, sums_a, 0))

    def block(index):
        place = index // 2
        return halves[index % 2, place * WIDTH : (place + 1) * WIDTH, :].astype(F32)

    for part in range(4):
        fc2[0, column(part), :] = block(part)
        fc1[0, :, column(part)] = block(4 + part)
    proj[0] = block(8)
    for part in range(3):
        qkv[0, :, column(part)] = block(9 + part)
    for out, row in (
        (ln1g, LN1G), (ln1b, LN1B), (qb, QB), (vb, VB), (pb, PB), (ln2g, LN2G), (ln2b, LN2B),
        (fc2b, F2B),
    ):
        out[...] = sums[row : row + 1, :]
    for part in range(4):
        fc1b[:, column(part)] = sums[F1B + part : F1B + part + 1, :]


def shape(*dims, dtype=BF16):
    return jax.ShapeDtypeStruct(dims, dtype)


def call(kernel, outs, in_specs, out_specs, scratch=(), flops=0, moved=0):
    return pl.pallas_call(
        kernel,
        out_shape=outs,
        in_specs=in_specs,
        out_specs=out_specs,
        scratch_shapes=list(scratch),
        compiler_params=pltpu.CompilerParams(vmem_limit_bytes=VMEM_LIMIT),
        cost_estimate=pl.CostEstimate(flops=flops, bytes_accessed=moved, transcendentals=0),
    )


CHUNK = 48


def add_rows(out, start_out, left, right, start, count):
    def step(i, carry):
        here = pl.ds(pl.multiple_of(start + i * CHUNK, 16), CHUNK)
        there = pl.ds(pl.multiple_of(start_out + i * CHUNK, 16), CHUNK)
        out[there, :] = (left[here, :].astype(F32) + right[here, :].astype(F32)).astype(BF16)
        return carry

    lax.fori_loop(0, count // CHUNK, step, 0, unroll=2)


def add_tail(outs, start_out, left, right, start):
    here = slice(start, start + VECS)
    tail = (left[here, :].astype(F32) + right[here, :].astype(F32)).astype(BF16)
    for out in outs:
        out[start_out : start_out + VECS, :] = tail


def position():
    dp = lax.axis_index("dp")
    return dp % 2, dp // 2 % 2, dp // 4


def bit_of(step):
    x, y, _ = position()
    core = lax.axis_index("section")
    return jnp.where(core == step, x, y)


def halve_kernel(step, count, keep, recv, keep_out, send_out):
    bit = bit_of(step)
    half = count // 2
    add_rows(send_out, 0, keep, recv, (1 - bit) * half, half)
    add_rows(keep_out, 0, keep, recv, bit * half, half)
    add_tail((keep_out, send_out), half, keep, recv, count)


def quarter_kernel(count, keep, recv, keep_out, *send_outs):
    _, _, z = position()
    part = count // 4
    for k, out in enumerate((keep_out,) + send_outs):
        add_rows(out, 0, keep, recv, lax.rem(z + k, 4) * part, part)
    add_tail((keep_out,) + send_outs, part, keep, recv, count)


def total_kernel(count, keep, a, b, c, total_out, sums_out, tails):
    _, _, z = position()

    def step(i, carry):
        here = pl.ds(pl.multiple_of(i * CHUNK, 16), CHUNK)
        total = keep[here, :].astype(F32) + a[here, :].astype(F32)
        total = total + b[here, :].astype(F32) + c[here, :].astype(F32)
        total_out[here, :] = total.astype(BF16)
        return carry

    lax.fori_loop(0, count // CHUNK, step, 0)
    for k, ref in enumerate((keep, a, b, c)):
        tails[lax.rem(z + 4 - k, 4)] = ref[count : count + VECS, :].astype(F32)
    sums_out[...] = tails[0] + tails[1] + tails[2] + tails[3]


def join_kernel(which, count, *refs):
    parts, out = refs[:-1], refs[-1]
    if which == "z":
        _, _, first = position()
    else:
        first = bit_of(which)
    size = len(parts)
    for k, ref in enumerate(parts):
        place = lax.rem(first + size - k, size) * count
        out[pl.ds(pl.multiple_of(place, 16), count), :] = ref[...]


def flat_pairs(move):
    pairs = []
    for core in range(2):
        for dp in range(16):
            x, y, z = dp % 2, dp // 2 % 2, dp // 4
            to_core, to_x, to_y, to_z = move(core, x, y, z)
            pairs.append((core * 16 + dp, to_core * 16 + to_z * 4 + to_y * 2 + to_x))
    return pairs


def exchange(values_in, step):
    def move(core, x, y, z):
        return (core, 1 - x, y, z) if core == step else (core, x, 1 - y, z)

    return lax.ppermute(values_in, ("section", "dp"), flat_pairs(move))


def forward_z(values_in, by):
    return lax.ppermute(
        values_in,
        ("section", "dp"),
        flat_pairs(lambda core, x, y, z: (core, x, y, (z + by) % 4)),
    )


def reduce_everywhere(keep, recv, count):
    tail = VECS
    for step in range(2):
        half = count // 2
        keep, send = call(
            functools.partial(halve_kernel, step, count),
            [shape(half + tail, WIDTH)] * 2,
            [VMEM] * 2,
            [VMEM] * 2,
            moved=6 * count * WIDTH,
        )(keep, recv)
        recv = exchange(send, step)
        count = half
    part = count // 4
    keep, *sends = call(
        functools.partial(quarter_kernel, count),
        [shape(part + tail, WIDTH)] * 4,
        [VMEM] * 2,
        [VMEM] * 4,
        moved=6 * count * WIDTH,
    )(keep, recv)
    recvs = [forward_z(send, k + 1) for k, send in enumerate(sends)]
    total, sums = call(
        functools.partial(total_kernel, part),
        [shape(part, WIDTH), shape(tail, WIDTH, dtype=F32)],
        [VMEM] * 4,
        [VMEM] * 2,
        [pltpu.VMEM((4, tail, WIDTH), F32)],
        moved=6 * count * WIDTH,
    )(keep, *recvs)
    parts = [total] + [forward_z(total, k) for k in range(1, 4)]
    whole = None
    for which in ("z", 1, 0):
        rows = parts[0].shape[0]
        whole = call(
            functools.partial(join_kernel, which, rows),
            shape(rows * len(parts), WIDTH),
            [VMEM] * len(parts),
            VMEM,
            moved=4 * rows * len(parts) * WIDTH,
        )(*parts)
        if which != "z" and which == 0:
            break
        parts = [whole, exchange(whole, 1 if which == "z" else 0)]
    return whole, sums


def plain_reduce(keep, recv, count):
    total = lax.psum(keep.astype(F32) + recv.astype(F32), "dp")
    return total[:count].astype(BF16), total[count:]


def swap(values_in):
    return lax.ppermute(values_in, "section", [(0, 1), (1, 0)])


def on_device(dp_size, global_ends, local_ends, global_live, local_live, *weights):
    (
        ln1_gain, ln1_bias, qkv_weight, query_bias, value_bias, proj_weight, proj_bias,
        ln2_gain, ln2_bias, fc1_weight, fc1_bias, fc2_weight, fc2_bias,
    ) = weights
    matrices = tuple(w[0] for w in (qkv_weight, proj_weight, fc1_weight, fc2_weight))
    got = tuple(swap(w) for w in matrices)
    vectors = (
        ln1_gain, ln1_bias, query_bias, value_bias, proj_bias, ln2_gain, ln2_bias, fc2_bias,
        fc1_bias,
    )
    keep, send = call(
        pack_kernel,
        [shape(ROWS + VECS, WIDTH)] * 2,
        [SMEM] * 2 + [VMEM] * 11,
        [VMEM] * 2,
        [pltpu.VMEM((ROWS, WIDTH), F32), pltpu.VMEM((VECS, WIDTH), F32)],
        moved=2000000,
    )(global_live, local_live, global_ends[0], local_ends[0], *vectors)
    recv = swap(send)
    grad_rows = HALF_ROWS + VECS
    saved_shapes = [
        shape(ROWS, WIDTH),
        shape(ROWS, 3 * WIDTH),
        shape(12, SEQ, SEQ),
        shape(ROWS, WIDTH),
        shape(ROWS, WIDTH, dtype=F32),
        shape(ROWS, WIDTH),
        shape(ROWS, FF),
        shape(ROWS, FF),
    ]
    weight_shapes = [(WIDTH, 3 * WIDTH), (WIDTH, WIDTH), (WIDTH, FF), (FF, WIDTH)]
    work = [
        pltpu.VMEM((ROWS, FF), BF16),
        pltpu.VMEM((ROWS, WIDTH), F32),
        pltpu.VMEM((ROWS, WIDTH), BF16),
        pltpu.VMEM((ROWS, 3 * WIDTH), BF16),
        pltpu.VMEM((ROWS, WIDTH), BF16),
        pltpu.VMEM((VECS, WIDTH), F32),
        pltpu.VMEM((2, grad_rows, WIDTH), BF16),
    ]
    *saved, result, dx, keep_b, send_b = call(
        forward_kernel,
        saved_shapes + [shape(ROWS, WIDTH)] * 2 + [shape(grad_rows, WIDTH)] * 2,
        [ANY] * 10,
        [ANY] * 12,
        [pltpu.VMEM((2, ROWS + VECS, WIDTH), BF16)]
        + [pltpu.VMEM((2,) + dims, BF16) for dims in weight_shapes]
        + [
            pltpu.VMEM((2, VECS, WIDTH), F32),
            pltpu.VMEM((2, SEQ, SEQ), F32),
            pltpu.VMEM((ROWS, WIDTH), BF16),
        ]
        + [pltpu.VMEM((2,) + s.shape, s.dtype) for s in saved_shapes]
        + [pltpu.VMEM((ROWS, WIDTH), BF16)]
        + work
        + [pltpu.SemaphoreType.DMA((2, 5)), pltpu.SemaphoreType.DMA((12,))],
        flops=6000000000,
        moved=20000000,
    )(keep, recv, *matrices, *got)
    recv_b = swap(send_b)
    rows_keep, rows_send, keep_a, send_a = call(
        backward_kernel,
        [shape(ROWS, WIDTH)] * 2 + [shape(grad_rows, WIDTH)] * 2,
        [ANY] * 20,
        [ANY] * 4,
        [pltpu.VMEM((ROWS + VECS, WIDTH), BF16)]
        + [pltpu.VMEM(dims, BF16) for dims in weight_shapes]
        + [pltpu.VMEM((VECS, WIDTH), F32)]
        + [pltpu.VMEM(s.shape, s.dtype) for s in saved_shapes]
        + [pltpu.VMEM((ROWS, WIDTH), BF16)]
        + work
        + [pltpu.SemaphoreType.DMA((14,)), pltpu.SemaphoreType.DMA((4,))],
        flops=3000000000,
        moved=15000000,
    )(keep, recv, *matrices, *got, *saved, dx, result)
    recv_a = swap(send_a)
    rows_recv = swap(rows_send)
    reduce = reduce_everywhere if dp_size == 16 else plain_reduce
    half_b, sums_b = reduce(keep_b, recv_b, HALF_ROWS)
    got_b = lax.ppermute(half_b, "section", [(0, 1)])
    half_a, sums_a = reduce(keep_a, recv_a, HALF_ROWS)
    got_a = lax.ppermute(half_a, "section", [(1, 0)])
    global_out, local_out = call(
        rows_kernel,
        [shape(*global_ends.shape[1:]), shape(*local_ends.shape[1:])],
        [SMEM] * 2 + [VMEM] * 2,
        [VMEM] * 2,
        [pltpu.VMEM((ROWS, WIDTH), F32)],
        moved=2000000,
    )(global_live, local_live, rows_keep, rows_recv)
    gradients = call(
        grads_kernel,
        [shape(*w.shape, dtype=F32) for w in weights],
        [ANY] * 6,
        [VMEM] * 13,
        [
            pltpu.VMEM((2, HALF_ROWS, WIDTH), BF16),
            pltpu.VMEM((VECS, WIDTH), F32),
            pltpu.SemaphoreType.DMA((3,)),
        ],
        moved=12000000,
    )(half_a, half_b, got_a, got_b, sums_a, sums_b)
    return (global_out[None], local_out[None]) + tuple(gradients)


def solution(mesh):
    matrix, vector = P("section", None, None), P("section", None)
    weights = (
        vector, vector, matrix, vector, vector, matrix, vector,
        vector, vector, matrix, vector, matrix, vector,
    )
    rows = P("section", "dp", None, None)
    return jax.shard_map(
        functools.partial(on_device, mesh.shape["dp"]),
        mesh=mesh,
        in_specs=(rows, rows, P("dp"), P("dp")) + weights,
        out_specs=(rows, rows) + weights,
        check_vma=False,
    )
```

```python
import functools

import jax
import jax.numpy as jnp
from jax import lax
from jax.experimental import pallas as pl
from jax.experimental.pallas import tpu as pltpu
from jax.sharding import PartitionSpec as P

HEAD = 64
GT = 197
LT = 37
WIDTH = 384
FF = 1536
SEQ = 208
ROWS = 2 * SEQ
SLOT = 40
LOCALS = 5
VECS = 16
EPSILON = 1e-06
MASKED = -1e30
ORDER = "b1c2d3j4jJjJjJjrJjJ5J76p8q"
DIMS_B = ((0, 1, 2, 3), (1, 0, 2, 3))
DIMS_A = ((0, 1, 2, 3), (1, 0, 2, 3))
PART_ROWS = {"m": 4 * WIDTH, "a": 2 * WIDTH}
COST = 10000000000
PACK_COST = 10
KA_VMEM = 12
KB_VMEM = 12
LN1G, LN1B, QB, VB, PB, LN2G, LN2B, F2B, F1B = range(9)
LIVE = 12
BF16 = jnp.bfloat16
F32 = jnp.float32
ANY = pl.BlockSpec(memory_space=pl.ANY)
VMEM = pl.BlockSpec(memory_space=pltpu.VMEM)
HBM = pl.BlockSpec(memory_space=pltpu.HBM)


def mm(left, right):
    return jnp.dot(left, right, preferred_element_type=F32)


def mm_right_t(left, right):
    return lax.dot_general(left, right, (((1,), (1,)), ((), ())), preferred_element_type=F32)


def mm_left_t(left, right):
    return lax.dot_general(left, right, (((0,), (0,)), ((), ())), preferred_element_type=F32)


def normalise(values_in):
    centred = values_in - jnp.mean(values_in, axis=-1, keepdims=True)
    scale = lax.rsqrt(jnp.mean(centred * centred, axis=-1, keepdims=True) + EPSILON)
    return centred * scale, scale


def normalise_back(unit, scale, grad_rows, gain):
    e = grad_rows * gain
    return scale * (
        e
        - jnp.mean(e, axis=-1, keepdims=True)
        - unit * jnp.mean(e * unit, axis=-1, keepdims=True)
    )


def seq_rows(seq):
    return pl.ds(pl.multiple_of(seq * SEQ, 16), SEQ)


def column(block):
    return slice(block * WIDTH, (block + 1) * WIDTH)


def row_sum(values_in):
    return jnp.sum(values_in, axis=0, keepdims=True)


def live_flag(tail, index):
    lane = lax.broadcasted_iota(jnp.int32, (1, WIDTH), 1)
    flags = tail[LIVE : LIVE + 1, :]
    return jnp.sum(jnp.where(lane == index, flags, 0.0), axis=1, keepdims=True)


def pack_kernel(g, l, tail, keep, send, rows):
    core = lax.axis_index("section")
    rows[...] = jnp.zeros_like(rows)
    tail_low = tail[...].astype(BF16)
    for out, half in ((keep, core), (send, 1 - core)):
        live = jnp.where(core == 1, live_flag(tail, half), 1.0)
        rows[:GT, :] = g[half].astype(F32) * live
        for j in range(LOCALS):
            crop = half * LOCALS + j
            live = jnp.where(core == 1, live_flag(tail, 2 + crop), 1.0)
            rows[SEQ + j * SLOT : SEQ + j * SLOT + LT, :] = l[crop].astype(F32) * live
        out[:ROWS, :] = rows[...].astype(BF16)
        out[ROWS:, :] = tail_low


def fill_masks(masks):
    row = lax.broadcasted_iota(jnp.int32, (SEQ, SEQ), 0)
    col = lax.broadcasted_iota(jnp.int32, (SEQ, SEQ), 1)
    masks[0] = jnp.where(col < GT, 0.0, MASKED)
    inside = jnp.zeros((SEQ, SEQ), jnp.bool_)
    for j in range(LOCALS):
        inside = inside | (
            (row >= j * SLOT)
            & (row < (j + 1) * SLOT)
            & (col >= j * SLOT)
            & (col < j * SLOT + LT)
        )
    masks[1] = jnp.where(inside, 0.0, MASKED)


def head_lanes():
    lane = lax.broadcasted_iota(jnp.int32, (SEQ, 2 * HEAD), 1)
    return (lane < HEAD, lane >= HEAD)


def only(mask, values_in):
    return jnp.where(mask, values_in, jnp.zeros_like(values_in))


def attention_forward(x, vec, masks, qkv_w, proj_w, n1, qkv, probs, mixed, middle):
    def body(seq, carry):
        rows = seq_rows(seq)
        x_rows = x[rows, :].astype(F32)
        unit, _ = normalise(x_rows)
        normed = (unit * vec[LN1G : LN1G + 1, :] + vec[LN1B : LN1B + 1, :]).astype(BF16)
        n1[rows, :] = normed
        for part in range(3):
            value = mm(normed, qkv_w[:, column(part)])
            if part == 0:
                value = (value + vec[QB : QB + 1, :]).astype(BF16) * BF16(HEAD**-0.5)
            if part == 2:
                value = value + vec[VB : VB + 1, :]
            qkv[rows, column(part)] = value.astype(BF16)
        lanes = head_lanes()
        mask = masks[seq]
        for pair in range(3):
            q = qkv[rows, pair * 128 : pair * 128 + 128]
            k = qkv[rows, WIDTH + pair * 128 : WIDTH + pair * 128 + 128]
            v = qkv[rows, 2 * WIDTH + pair * 128 : 2 * WIDTH + pair * 128 + 128]
            total = None
            for a in range(2):
                s = mm_right_t(only(lanes[a], q), k) + mask
                e = jnp.exp(s - jnp.max(s, axis=-1, keepdims=True))
                p = (e * (1.0 / jnp.sum(e, axis=-1, keepdims=True))).astype(BF16)
                probs[seq * 6 + pair * 2 + a] = p
                part = mm(p, only(lanes[a], v))
                total = part if total is None else total + part
            mixed[rows, pair * 128 : pair * 128 + 128] = total.astype(BF16)
        middle[rows, :] = x_rows + (mm(mixed[rows, :], proj_w[...]) + vec[PB : PB + 1, :])
        return carry

    lax.fori_loop(0, 2, body, 0)


def mlp_forward(vec, fc1_w, fc2_w, middle, n2, slope, active, result):
    def body(seq, carry):
        rows = seq_rows(seq)
        unit, _ = normalise(middle[rows, :])
        normed = (unit * vec[LN2G : LN2G + 1, :] + vec[LN2B : LN2B + 1, :]).astype(BF16)
        n2[rows, :] = normed
        for part in range(FF // WIDTH):
            hidden = mm(normed, fc1_w[:, column(part)]) + vec[F1B + part : F1B + part + 1, :]
            cdf = 0.5 + 0.5 * lax.erf(hidden * (0.5**0.5))
            active[rows, column(part)] = (hidden * cdf).astype(BF16)
            density = jnp.exp(hidden * hidden * -0.5) * 0.3989422804014327
            slope[rows, column(part)] = (cdf + hidden * density).astype(BF16)
        y = middle[rows, :] + (mm(active[rows, :], fc2_w[...]) + vec[F2B : F2B + 1, :])
        result[rows, :] = y.astype(BF16)
        return carry

    lax.fori_loop(0, 2, body, 0)


def mlp_backward(vec, fc1_w, fc2_w, middle, n2, slope, active, dy, dh, dmid, da, sums, emit):
    def body(seq, carry):
        rows = seq_rows(seq)
        dy_rows = dy[rows, :]
        for part in range(FF // WIDTH):
            dactive = mm_right_t(dy_rows, fc2_w[column(part), :])
            low = (slope[rows, column(part)].astype(F32) * dactive).astype(BF16)
            dh[rows, column(part)] = low
            sums[F1B + part : F1B + part + 1, :] += row_sum(low.astype(F32))
        dn2 = mm_right_t(dh[rows, :], fc1_w[...])
        unit, scale = normalise(middle[rows, :])
        dy_wide = dy_rows.astype(F32)
        grad = dy_wide + normalise_back(unit, scale, dn2, vec[LN2G : LN2G + 1, :])
        dmid[rows, :] = grad
        low = grad.astype(BF16)
        da[rows, :] = low
        sums[LN2G : LN2G + 1, :] += row_sum(dn2 * unit)
        sums[LN2B : LN2B + 1, :] += row_sum(dn2)
        sums[F2B : F2B + 1, :] += row_sum(dy_wide)
        sums[PB : PB + 1, :] += row_sum(low.astype(F32))
        return carry

    lax.fori_loop(0, 2, body, 0)
    for part in range(FF // WIDTH):
        emit(part, mm_left_t(active[:, column(part)], dy[:ROWS, :]))
    for part in range(FF // WIDTH):
        emit(4 + part, mm_left_t(n2[...], dh[:, column(part)]))


def attention_backward(
    x, vec, qkv_w, proj_w, n1, qkv, probs, mixed, dmid, da, dt, sums, emit, result
):
    def body(seq, carry):
        rows = seq_rows(seq)
        dmixed = mm_right_t(da[rows, :], proj_w[...]).astype(BF16)
        lanes = head_lanes()
        for pair in range(3):
            q = qkv[rows, pair * 128 : pair * 128 + 128]
            k = qkv[rows, WIDTH + pair * 128 : WIDTH + pair * 128 + 128]
            v = qkv[rows, 2 * WIDTH + pair * 128 : 2 * WIDTH + pair * 128 + 128]
            dm = dmixed[:, pair * 128 : pair * 128 + 128]
            dq = dk = dv = None
            for a in range(2):
                dm_a = only(lanes[a], dm)
                p = probs[seq * 6 + pair * 2 + a]
                dp = mm_right_t(dm_a, v)
                p_wide = p.astype(F32)
                ds = p_wide * (dp - jnp.sum(dp * p_wide, axis=-1, keepdims=True))
                ds = ds.astype(BF16)
                parts = (
                    mm(ds, only(lanes[a], k)),
                    mm_left_t(ds, only(lanes[a], q)),
                    mm_left_t(p, dm_a),
                )
                if a == 0:
                    dq, dk, dv = parts
                else:
                    dq, dk, dv = dq + parts[0], dk + parts[1], dv + parts[2]
            dq = (dq * HEAD**-0.5).astype(BF16)
            dv = dv.astype(BF16)
            here = slice(pair * 128, pair * 128 + 128)
            dt[rows, pair * 128 : pair * 128 + 128] = dq
            dt[rows, WIDTH + pair * 128 : WIDTH + pair * 128 + 128] = dk.astype(BF16)
            dt[rows, 2 * WIDTH + pair * 128 : 2 * WIDTH + pair * 128 + 128] = dv
            sums[QB : QB + 1, here] += row_sum(dq.astype(F32))
            sums[VB : VB + 1, here] += row_sum(dv.astype(F32))
        dn1 = mm_right_t(dt[rows, :], qkv_w[...])
        unit, scale = normalise(x[rows, :].astype(F32))
        grad = dmid[rows, :] + normalise_back(unit, scale, dn1, vec[LN1G : LN1G + 1, :])
        result[rows, :] = grad.astype(BF16)
        sums[LN1G : LN1G + 1, :] += row_sum(dn1 * unit)
        sums[LN1B : LN1B + 1, :] += row_sum(dn1)
        return carry

    lax.fori_loop(0, 2, body, 0)
    emit(8, mm_left_t(mixed[...], da[...]))
    for part in range(3):
        emit(9 + part, mm_left_t(n1[...], dt[:, column(part)]))


def make_emit(keep, send, core, first, blocks):
    def emit(block, value):
        half, place = block % 2, (block - first) // 2
        rows = slice(place * WIDTH, (place + 1) * WIDTH)
        low = value.astype(BF16)

        @pl.when(core == half)
        def _():
            keep[rows, :] = low

        @pl.when(core != half)
        def _():
            send[rows, :] = low

    return emit


def start_all(copies):
    for copy in copies:
        copy.start()


def wait_all(copies):
    for copy in copies:
        copy.wait()


def forward_kernel(*refs):
    own, got = refs[:1] + refs[2:6], refs[1:2] + refs[6:10]
    (
        pack, qkv_w, proj_w, fc1_w, fc2_w, vec, between,
        n1, qkv, probs, mixed, middle, n2, slope, active, result,
        dmid, da, sums, keep_out, send_out,
        masks, dh, in_sem,
    ) = refs[10:]
    core = lax.axis_index("section")
    other = 1 - core
    held = (pack, qkv_w, proj_w, fc1_w, fc2_w)

    def load(sources, layer, i):
        return pltpu.make_async_copy(sources[i], held[i].at[layer], in_sem.at[layer, i])

    for i in range(5):
        load(own, core, i).start()
        load(got, other, i).start()
    fill_masks(masks)
    sums[...] = jnp.zeros_like(sums)
    for layer in range(2):
        load(own, layer, 0).wait()
        vec[layer] = pack[layer, ROWS:, :].astype(F32)
    for layer in range(2):
        for i in (1, 2):
            load(own, layer, i).wait()
        x = pack.at[0] if layer == 0 else between
        attention_forward(
            x, vec.at[layer], masks, qkv_w.at[layer], proj_w.at[layer],
            n1.at[layer], qkv.at[layer], probs.at[layer], mixed.at[layer], middle.at[layer],
        )
        for i in (3, 4):
            load(own, layer, i).wait()
        mlp_forward(
            vec.at[layer], fc1_w.at[layer], fc2_w.at[layer], middle.at[layer], n2.at[layer],
            slope.at[layer], active.at[layer], between if layer == 0 else result,
        )
    mlp_backward(
        vec.at[1], fc1_w.at[1], fc2_w.at[1], middle.at[1], n2.at[1], slope.at[1], active.at[1],
        pack.at[1], dh, dmid, da, sums, make_emit(keep_out, send_out, core, 0, 8),
    )


def attention_backward_kernel(layer, *refs):
    (
        x, vec, qkv_w, proj_w, n1, qkv, probs, mixed, dmid, da, sums_in,
        dx, keep_out, send_out, dt, sums,
    ) = refs
    core = lax.axis_index("section")
    sums[...] = sums_in[...]
    attention_backward(
        x, vec.at[layer], qkv_w.at[layer], proj_w.at[layer], n1.at[layer], qkv.at[layer],
        probs.at[layer], mixed.at[layer], dmid, da, dt, sums,
        make_emit(keep_out, send_out, core, 8, 4), dx,
    )
    keep_out[2 * WIDTH :, :] = sums[...].astype(BF16)
    send_out[2 * WIDTH :, :] = sums[...].astype(BF16)


def last_backward_kernel(*refs):
    pack, result, rows_keep, rows_send, dx = refs[0], refs[11], refs[12], refs[13], refs[-1]
    attention_backward_kernel(
        0, pack.at[0], *refs[1:11], dx, refs[14], refs[15], refs[16], refs[17]
    )
    core = lax.axis_index("section")

    @pl.when(core == 0)
    def _():
        rows_keep[...] = dx[...]
        rows_send[...] = result[...]

    @pl.when(core == 1)
    def _():
        rows_keep[...] = result[...]
        rows_send[...] = dx[...]


def mlp_backward_kernel(*refs):
    (
        vec, fc1_w, fc2_w, middle, n2, slope, active, dy, dmid, da, sums, keep_out, send_out, dh,
    ) = refs
    core = lax.axis_index("section")
    sums[...] = jnp.zeros_like(sums)
    mlp_backward(
        vec.at[0], fc1_w.at[0], fc2_w.at[0], middle.at[0], n2.at[0], slope.at[0], active.at[0],
        dy, dh, dmid, da, sums, make_emit(keep_out, send_out, core, 0, 8),
    )


def rows_kernel(tails, keep, recv, g_out, l_out, wide):
    core = lax.axis_index("section")
    tail = tails.at[0]
    for source, half in ((keep, core), (recv, 1 - core)):
        wide[...] = source[...].astype(F32)
        live = jnp.where(core == 1, live_flag(tail, half), 1.0)
        g_out[half] = (wide[:GT, :] * live).astype(BF16)
        for j in range(LOCALS):
            crop = half * LOCALS + j
            live = jnp.where(core == 1, live_flag(tail, 2 + crop), 1.0)
            piece = wide[SEQ + j * SLOT : SEQ + j * SLOT + LT, :]
            l_out[crop] = (piece * live).astype(BF16)


def out_block(own, got, index):
    core = lax.axis_index("section")
    place = index // 2
    rows = slice(place * WIDTH, (place + 1) * WIDTH)
    return jnp.where(core == index % 2, own[rows, :], got[rows, :]).astype(F32)


def write_blocks(own, got, places, held, sem):
    copies = []
    for i, place in enumerate(places):
        held[i] = out_block(own, got, i)
        copies.append(pltpu.make_async_copy(held.at[i], place, sem.at[i]))
        copies[-1].start()
    return copies


def mlp_out_kernel(own, got, fc1, fc2, held, sem):
    places = [fc2.at[0, column(part), :] for part in range(4)]
    places += [fc1.at[0, :, column(part)] for part in range(4)]
    wait_all(write_blocks(own, got, places, held, sem))


def attention_out_kernel(*refs):
    (
        own, got, sums_a, sums_b,
        ln1g, ln1b, qkv, qb, vb, proj, pb, ln2g, ln2b, fc1b, fc2b, held, sem,
    ) = refs
    places = [proj.at[0]] + [qkv.at[0, :, column(part)] for part in range(3)]
    copies = write_blocks(own, got, places, held, sem)
    core = lax.axis_index("section")
    sums = jnp.where(core == 0, sums_a[...], sums_b[...])
    for out, row in (
        (ln1g, LN1G), (ln1b, LN1B), (qb, QB), (vb, VB), (pb, PB), (ln2g, LN2G), (ln2b, LN2B),
        (fc2b, F2B),
    ):
        out[...] = sums[row : row + 1, :]
    for part in range(4):
        fc1b[:, column(part)] = sums[F1B + part : F1B + part + 1, :]
    wait_all(copies)


def shape(*dims, dtype=BF16):
    return jax.ShapeDtypeStruct(dims, dtype)


class Ordered:
    def __init__(self):
        self.last = None

    def __call__(
        self, name, kernel, outs, in_specs, out_specs, scratch=(), vmem=8, cost=1
    ):
        before = [] if self.last is None else [self.last]
        count = len(in_specs)

        def body(*refs):
            kernel(*refs[:count], *refs[count + len(before) :])

        def run(*args):
            results = pl.pallas_call(
                body,
                out_shape=outs,
                name=name,
                in_specs=list(in_specs) + [ANY] * len(before),
                out_specs=out_specs,
                scratch_shapes=list(scratch),
                compiler_params=pltpu.CompilerParams(vmem_limit_bytes=vmem * 1024 * 1024),
                cost_estimate=pl.CostEstimate(
                    flops=cost * COST, bytes_accessed=0, transcendentals=0
                ),
            )(*args, *before)
            self.last = results[-1]
            return results

        return run


CHUNK = 48


def add_rows(out, start_out, left, right, start, count):
    def step(i, carry):
        here = pl.ds(pl.multiple_of(start + i * CHUNK, 16), CHUNK)
        there = pl.ds(pl.multiple_of(start_out + i * CHUNK, 16), CHUNK)
        out[there, :] = (left[here, :].astype(F32) + right[here, :].astype(F32)).astype(BF16)
        return carry

    lax.fori_loop(0, count // CHUNK, step, 0, unroll=2)


def add_tail(outs, start_out, left, right, start):
    if left.shape[0] == start:
        return
    here = slice(start, start + VECS)
    tail = (left[here, :].astype(F32) + right[here, :].astype(F32)).astype(BF16)
    for out in outs:
        out[start_out : start_out + VECS, :] = tail


def bit_of(dims, step):
    dp = lax.axis_index("dp")
    core = lax.axis_index("section")
    return jnp.where(core == 0, dp >> dims[0][step] & 1, dp >> dims[1][step] & 1)


def halve_kernel(dims, step, counts, *refs):
    sources, (keep_out, send_out) = refs[:-2], refs[-2:]
    bit = bit_of(dims, step)
    place = 0
    for count, keep, recv in zip(counts, sources[::2], sources[1::2]):
        half = count // 2
        add_rows(send_out, place, keep, recv, (1 - bit) * half, half)
        add_rows(keep_out, place, keep, recv, bit * half, half)
        place += half
    for count, keep, recv in zip(counts, sources[::2], sources[1::2]):
        add_tail((keep_out, send_out), place, keep, recv, count)


def sum_kernel(count, keep, recv, out):
    add_rows(out, 0, keep, recv, 0, count)
    add_tail((out,), count, keep, recv, count)


def total_kernel(count, own, recv, total_out, sums_out):
    add_rows(total_out, 0, own, recv, 0, count)
    sums_out[...] = own[count:, :].astype(F32) + recv[count:, :].astype(F32)


def join_rows(out, own, recv, bit, start, count):
    for ref, half in ((own, bit), (recv, 1 - bit)):
        out[pl.ds(pl.multiple_of(half * count, 16), count), :] = ref[start : start + count, :]


def join_kernel(dims, step, counts, own, recv, *outs):
    bit = bit_of(dims, step)
    start = 0
    for count, out in zip(counts, outs):
        join_rows(out, own, recv, bit, start, count)
        start += count


def last_join_kernel(dims, own, recv, other, mine, send, whole):
    join_rows(whole, own, recv, bit_of(dims, 0), 0, own.shape[0])
    core = lax.axis_index("section")

    @pl.when(core == 0)
    def _():
        mine[...] = whole[...]
        send[...] = other[...]

    @pl.when(core == 1)
    def _():
        mine[...] = other[...]
        send[...] = whole[...]


def exchange(values_in, dims, step):
    pairs = [
        (core * 16 + dp, core * 16 + (dp ^ 1 << dims[core][step]))
        for core in range(2)
        for dp in range(16)
    ]
    return lax.ppermute(values_in, ("section", "dp"), pairs)


class Reduction:
    def __init__(self, name, call, dims):
        self.name, self.call, self.dims = name, call, dims
        self.sources, self.wholes = {}, {}
        self.joint = self.run_joint()

    def add(self, part, keep, send):
        self.sources[part] = (keep, swap(send))

    def halve(self, step, label, counts, tail, sources):
        rows = sum(counts) // 2 + tail
        keep, send = self.call(
            f"{self.name}_halve{label}",
            functools.partial(halve_kernel, self.dims, step, counts),
            [shape(rows, WIDTH)] * 2,
            [VMEM] * len(sources),
            [VMEM] * 2,
        )(*sources)
        return keep, exchange(send, self.dims, step)

    def first(self, part):
        keep, recv = self.sources[part]
        count = PART_ROWS[part]
        tail = keep.shape[0] - count
        self.sources[part] = self.halve(0, f"0{part}", [count], tail, [keep, recv])

    def run_joint(self):
        counts = [PART_ROWS[part] // 2 for part in "ma"]
        sources = self.sources["m"] + self.sources["a"]
        keep, recv = self.halve(1, "1", counts, VECS, sources)
        yield
        count = sum(counts) // 2
        keep, recv = self.halve(2, "2", [count], VECS, [keep, recv])
        yield
        count //= 2
        (own,) = self.call(
            f"{self.name}_sum",
            functools.partial(sum_kernel, count),
            [shape(count + VECS, WIDTH)],
            [VMEM] * 2,
            [VMEM],
        )(keep, recv)
        recv = exchange(own, self.dims, 3)
        yield
        whole, self.sums = self.call(
            f"{self.name}_total",
            functools.partial(total_kernel, count),
            [shape(count, WIDTH), shape(VECS, WIDTH, dtype=F32)],
            [VMEM] * 2,
            [VMEM] * 2,
        )(own, recv)
        recv = exchange(whole, self.dims, 2)
        yield
        (whole,) = self.join(2, [count], whole, recv)
        recv = exchange(whole, self.dims, 1)
        yield
        wholes = self.join(1, [n // 2 for n in counts], whole, recv)
        for part, whole in zip("ma", wholes):
            self.wholes[part] = (whole, exchange(whole, self.dims, 0))
        yield

    def join(self, step, counts, own, recv):
        return self.call(
            f"{self.name}_join{step}",
            functools.partial(join_kernel, self.dims, step, counts),
            [shape(2 * count, WIDTH) for count in counts],
            [VMEM] * 2,
            [VMEM] * len(counts),
        )(own, recv)

    def last(self, part):
        own, recv = self.wholes[part]
        (self.wholes[part],) = self.join(0, [own.shape[0]], own, recv)

    def last_sorted(self, part, other):
        own, recv = self.wholes[part]
        mine, send = self.call(
            f"{self.name}_last_{part}",
            functools.partial(last_join_kernel, self.dims),
            [shape(PART_ROWS[part], WIDTH)] * 2,
            [VMEM] * 3,
            [VMEM] * 2,
            [pltpu.VMEM((PART_ROWS[part], WIDTH), BF16)],
        )(own, recv, other.wholes[part])
        return mine, swap(send)


class PlainReduction(Reduction):
    def first(self, part):
        keep, recv = self.sources[part]
        total = lax.psum(keep.astype(F32) + recv.astype(F32), "dp")
        self.wholes[part] = total[: PART_ROWS[part]].astype(BF16)
        self.sums = total[PART_ROWS[part] :]

    def run_joint(self):
        yield from [None] * 6

    def last(self, part):
        pass

    def last_sorted(self, part, other):
        leading = lax.axis_index("section") == 0
        pair = (self.wholes[part], other.wholes[part])
        return jnp.where(leading, *pair), swap(jnp.where(leading, *pair[::-1]))


def swap(values_in):
    return lax.ppermute(values_in, "section", [(0, 1), (1, 0)])


def on_device(dp_size, global_ends, local_ends, global_live, local_live, *weights):
    (
        ln1_gain, ln1_bias, qkv_weight, query_bias, value_bias, proj_weight, proj_bias,
        ln2_gain, ln2_bias, fc1_weight, fc1_bias, fc2_weight, fc2_bias,
    ) = weights
    matrices = tuple(w[0] for w in (qkv_weight, proj_weight, fc1_weight, fc2_weight))
    got = tuple(swap(w) for w in matrices)
    vectors = (
        ln1_gain, ln1_bias, query_bias, value_bias, proj_bias, ln2_gain, ln2_bias, fc2_bias,
        fc1_bias,
    )
    flags = jnp.concatenate([global_live, local_live]).astype(F32)
    tail = jnp.concatenate(
        [vector.reshape(-1, WIDTH).astype(F32) for vector in vectors]
        + [jnp.pad(flags, (0, WIDTH - flags.shape[0]))[None]]
    )
    tail = jnp.pad(tail, ((0, VECS - tail.shape[0]), (0, 0)))
    call = Ordered()
    keep, send = call(
        "pack",
        pack_kernel,
        [shape(ROWS + VECS, WIDTH)] * 2,
        [VMEM] * 3,
        [VMEM] * 2,
        [pltpu.VMEM((ROWS, WIDTH), F32)],
        cost=PACK_COST,
    )(global_ends[0], local_ends[0], tail)
    recv = swap(send)
    weight_shapes = [(WIDTH, 3 * WIDTH), (WIDTH, WIDTH), (WIDTH, FF), (FF, WIDTH)]
    rows_low, rows_wide = shape(ROWS, WIDTH), shape(ROWS, WIDTH, dtype=F32)
    sums_shape = shape(VECS, WIDTH, dtype=F32)
    mlp_pair = [shape(4 * WIDTH, WIDTH)] * 2
    attention_pair = [shape(2 * WIDTH + VECS, WIDTH)] * 2
    outs = (
        [shape(2, ROWS + VECS, WIDTH)]
        + [shape(2, *dims) for dims in weight_shapes]
        + [
            shape(2, VECS, WIDTH, dtype=F32),
            rows_low,
            shape(2, ROWS, WIDTH),
            shape(2, ROWS, 3 * WIDTH),
            shape(2, 12, SEQ, SEQ),
            shape(2, ROWS, WIDTH),
            shape(2, ROWS, WIDTH, dtype=F32),
            shape(2, ROWS, WIDTH),
            shape(2, ROWS, FF),
            shape(2, ROWS, FF),
            rows_low,
            rows_wide,
            rows_low,
            sums_shape,
        ]
        + mlp_pair
    )
    (
        pack, qkv_w, proj_w, fc1_w, fc2_w, vec, between,
        n1, qkv, probs, mixed, middle, n2, slope, active, result,
        dmid, da, sums, keep_1, send_1,
    ) = call(
        "forward",
        forward_kernel,
        outs,
        [HBM] * 10,
        [VMEM] * len(outs),
        [
            pltpu.VMEM((2, SEQ, SEQ), F32),
            pltpu.VMEM((ROWS, FF), BF16),
            pltpu.SemaphoreType.DMA((2, 5)),
        ],
        vmem=KA_VMEM,
    )(keep, recv, *matrices, *got)
    reduction = Reduction if dp_size == 16 else PlainReduction
    layer_a = reduction("a", call, DIMS_A)
    layer_b = reduction("b", call, DIMS_B)
    layer_b.add("m", keep_1, send_1)
    wide_work = [pltpu.VMEM((ROWS, 3 * WIDTH), BF16), pltpu.VMEM((VECS, WIDTH), F32)]
    held = {}

    def back_b_attention():
        held["dx"], keep, send = call(
            "back_b_attention",
            functools.partial(attention_backward_kernel, 1),
            [rows_low] + attention_pair,
            [VMEM] * 11,
            [VMEM] * 3,
            wide_work,
            vmem=KB_VMEM,
        )(between, vec, qkv_w, proj_w, n1, qkv, probs, mixed, dmid, da, sums)
        layer_b.add("a", keep, send)

    def back_a_mlp():
        *held["mlp"], keep, send = call(
            "back_a_mlp",
            mlp_backward_kernel,
            [rows_wide, rows_low, sums_shape] + mlp_pair,
            [VMEM] * 8,
            [VMEM] * 5,
            [pltpu.VMEM((ROWS, FF), BF16)],
            vmem=KB_VMEM,
        )(vec, fc1_w, fc2_w, middle, n2, slope, active, held["dx"])
        layer_a.add("m", keep, send)

    def back_a_attention():
        held["rows"], rows_send, keep, send = call(
            "back_a_attention",
            last_backward_kernel,
            [rows_low] * 2 + attention_pair,
            [VMEM] * 12,
            [VMEM] * 4,
            wide_work + [pltpu.VMEM((ROWS, WIDTH), BF16)],
            vmem=KB_VMEM,
        )(pack, vec, qkv_w, proj_w, n1, qkv, probs, mixed, *held["mlp"], result)
        layer_a.add("a", keep, send)
        held["rows_got"] = swap(rows_send)

    def rows_out():
        held["rows_out"] = call(
            "rows_out",
            rows_kernel,
            [shape(*global_ends.shape[1:]), shape(*local_ends.shape[1:])],
            [VMEM] * 3,
            [VMEM] * 2,
            [pltpu.VMEM((ROWS, WIDTH), F32)],
        )(vec, held["rows"], held["rows_got"])

    def grad(w):
        return shape(*w.shape, dtype=F32)

    def last_sorted(part):
        held[part] = layer_a.last_sorted(part, layer_b)

    def mlp_out():
        held["mlp_out"] = call(
            "mlp_out",
            mlp_out_kernel,
            [grad(fc1_weight), grad(fc2_weight)],
            [VMEM] * 2,
            [ANY] * 2,
            [pltpu.VMEM((8, WIDTH, WIDTH), F32), pltpu.SemaphoreType.DMA((8,))],
            vmem=16,
        )(*held["m"])

    def attention_out():
        wanted = (
            ln1_gain, ln1_bias, qkv_weight, query_bias, value_bias, proj_weight,
            proj_bias, ln2_gain, ln2_bias, fc1_bias, fc2_bias,
        )
        held["attention_out"] = call(
            "attention_out",
            attention_out_kernel,
            [grad(w) for w in wanted],
            [VMEM] * 4,
            [ANY if w.ndim == 3 else VMEM for w in wanted],
            [pltpu.VMEM((4, WIDTH, WIDTH), F32), pltpu.SemaphoreType.DMA((4,))],
        )(*held["a"], layer_a.sums, layer_b.sums)

    actions = {
        "b": back_b_attention, "c": back_a_mlp, "d": back_a_attention,
        "r": rows_out, "p": mlp_out, "q": attention_out,
        "1": lambda: layer_b.first("m"), "2": lambda: layer_b.first("a"),
        "3": lambda: layer_a.first("m"), "4": lambda: layer_a.first("a"),
        "j": lambda: next(layer_b.joint), "J": lambda: next(layer_a.joint),
        "5": lambda: layer_b.last("m"), "6": lambda: layer_b.last("a"),
        "7": lambda: last_sorted("m"), "8": lambda: last_sorted("a"),
    }
    for name in ORDER:
        actions[name]()
    global_out, local_out = held["rows_out"]
    grad_fc1, grad_fc2 = held["mlp_out"]
    (
        grad_ln1_gain, grad_ln1_bias, grad_qkv, grad_query_bias, grad_value_bias, grad_proj,
        grad_proj_bias, grad_ln2_gain, grad_ln2_bias, grad_fc1_bias, grad_fc2_bias,
    ) = held["attention_out"]
    return (
        global_out[None], local_out[None],
        grad_ln1_gain, grad_ln1_bias, grad_qkv, grad_query_bias, grad_value_bias, grad_proj,
        grad_proj_bias, grad_ln2_gain, grad_ln2_bias, grad_fc1, grad_fc1_bias, grad_fc2,
        grad_fc2_bias,
    )


def solution(mesh):
    matrix, vector = P("section", None, None), P("section", None)
    weights = (
        vector, vector, matrix, vector, vector, matrix, vector,
        vector, vector, matrix, vector, matrix, vector,
    )
    rows = P("section", "dp", None, None)
    return jax.shard_map(
        functools.partial(on_device, mesh.shape["dp"]),
        mesh=mesh,
        in_specs=(rows, rows, P("dp"), P("dp")) + weights,
        out_specs=(rows, rows) + weights,
        check_vma=False,
    )
```

```python
import functools

import jax
import jax.numpy as jnp
from jax import lax
from jax.experimental import pallas as pl
from jax.experimental.pallas import tpu as pltpu
from jax.sharding import PartitionSpec as P

HEAD = 64
GT = 197
LT = 37
WIDTH = 384
FF = 1536
SEQ = 208
ROWS = 2 * SEQ
SLOT = 40
LOCALS = 5
VECS = 16
EPSILON = 1e-06
MASKED = -1e30
CHUNK_FF = 768
ORDER = "bwcxywdywzywzyxzwxzwyxzwyxzrxyxzWYXZpq"
DIMS = {
    "bm": ((0, 1, 2, 3), (2, 0, 1, 3)),
    "ba": ((2, 0, 1, 3), (2, 1, 0, 3)),
    "am": ((0, 1, 2, 3), (1, 2, 0, 3)),
    "aa": ((0, 1, 2, 3), (1, 0, 2, 3)),
}
PART_ROWS = {"m": 4 * WIDTH, "a": 2 * WIDTH}
COST = 30000000000
PACK_COST = 10
KA_VMEM = 12
KB_VMEM = 12
LN1G, LN1B, QB, VB, PB, LN2G, LN2B, F2B, F1B = range(9)
LIVE = 12
BF16 = jnp.bfloat16
F32 = jnp.float32
ANY = pl.BlockSpec(memory_space=pl.ANY)
VMEM = pl.BlockSpec(memory_space=pltpu.VMEM)
HBM = pl.BlockSpec(memory_space=pltpu.HBM)


def mm(left, right):
    return jnp.dot(left, right, preferred_element_type=F32)


def mm_right_t(left, right):
    return lax.dot_general(left, right, (((1,), (1,)), ((), ())), preferred_element_type=F32)


def mm_left_t(left, right):
    return lax.dot_general(left, right, (((0,), (0,)), ((), ())), preferred_element_type=F32)


def normalise(values_in):
    centred = values_in - jnp.mean(values_in, axis=-1, keepdims=True)
    scale = lax.rsqrt(jnp.mean(centred * centred, axis=-1, keepdims=True) + EPSILON)
    return centred * scale, scale


def normalise_back(unit, scale, grad_rows, gain):
    e = grad_rows * gain
    return scale * (
        e
        - jnp.mean(e, axis=-1, keepdims=True)
        - unit * jnp.mean(e * unit, axis=-1, keepdims=True)
    )


def seq_rows(seq):
    return pl.ds(pl.multiple_of(seq * SEQ, 16), SEQ)


def column(block):
    return slice(block * WIDTH, (block + 1) * WIDTH)


def wide(part):
    return slice(part * CHUNK_FF, (part + 1) * CHUNK_FF)


def row_sum(values_in):
    return jnp.sum(values_in, axis=0, keepdims=True)


def live_flag(tail, index):
    lane = lax.broadcasted_iota(jnp.int32, (1, WIDTH), 1)
    flags = tail[LIVE : LIVE + 1, :]
    return jnp.sum(jnp.where(lane == index, flags, 0.0), axis=1, keepdims=True)


def pack_kernel(g, l, tail, keep, send, rows):
    core = lax.axis_index("section")
    rows[...] = jnp.zeros_like(rows)
    tail_low = tail[...].astype(BF16)
    for out, half in ((keep, core), (send, 1 - core)):
        live = jnp.where(core == 1, live_flag(tail, half), 1.0)
        rows[:GT, :] = g[half].astype(F32) * live
        for j in range(LOCALS):
            crop = half * LOCALS + j
            live = jnp.where(core == 1, live_flag(tail, 2 + crop), 1.0)
            rows[SEQ + j * SLOT : SEQ + j * SLOT + LT, :] = l[crop].astype(F32) * live
        out[:ROWS, :] = rows[...].astype(BF16)
        out[ROWS:, :] = tail_low


def fill_masks(masks):
    key = lax.broadcasted_iota(jnp.int32, (SEQ, SEQ), 0)
    query = lax.broadcasted_iota(jnp.int32, (SEQ, SEQ), 1)
    masks[0] = jnp.where(key < GT, 0.0, MASKED)
    inside = jnp.zeros((SEQ, SEQ), jnp.bool_)
    for j in range(LOCALS):
        inside = inside | (
            (query >= j * SLOT)
            & (query < (j + 1) * SLOT)
            & (key >= j * SLOT)
            & (key < j * SLOT + LT)
        )
    masks[1] = jnp.where(inside, 0.0, MASKED)


def head_lanes():
    lane = lax.broadcasted_iota(jnp.int32, (SEQ, 2 * HEAD), 1)
    return (lane < HEAD, lane >= HEAD)


def only(mask, values_in):
    return jnp.where(mask, values_in, jnp.zeros_like(values_in))


def attention_forward(x, vec, masks, qkv_w, proj_w, n1, qkv, probs, mixed, middle):
    def body(seq, carry):
        rows = seq_rows(seq)
        x_rows = x[rows, :].astype(F32)
        unit, _ = normalise(x_rows)
        normed = (unit * vec[LN1G : LN1G + 1, :] + vec[LN1B : LN1B + 1, :]).astype(BF16)
        n1[rows, :] = normed
        triple = mm(normed, qkv_w[...])
        query = (triple[:, :WIDTH] + vec[QB : QB + 1, :]).astype(BF16) * BF16(HEAD**-0.5)
        qkv[rows, :WIDTH] = query
        qkv[rows, column(1)] = triple[:, column(1)].astype(BF16)
        qkv[rows, column(2)] = (triple[:, column(2)] + vec[VB : VB + 1, :]).astype(BF16)
        lanes = head_lanes()
        mask = masks[seq]
        for pair in range(3):
            q = qkv[rows, pair * 128 : pair * 128 + 128]
            k = qkv[rows, WIDTH + pair * 128 : WIDTH + pair * 128 + 128]
            v = qkv[rows, 2 * WIDTH + pair * 128 : 2 * WIDTH + pair * 128 + 128]
            total = None
            for a in range(2):
                s = mm_right_t(only(lanes[a], k), q) + mask
                e = jnp.exp(s - jnp.max(s, axis=0, keepdims=True))
                p = (e * (1.0 / jnp.sum(e, axis=0, keepdims=True))).astype(BF16)
                probs[seq * 6 + pair * 2 + a] = p
                part = mm_left_t(p, only(lanes[a], v))
                total = part if total is None else total + part
            mixed[rows, pair * 128 : pair * 128 + 128] = total.astype(BF16)
        middle[rows, :] = x_rows + (mm(mixed[rows, :], proj_w[...]) + vec[PB : PB + 1, :])
        return carry

    lax.fori_loop(0, 2, body, 0, unroll=True)


def wide_bias(vec, part):
    rows = CHUNK_FF // 128
    pieces = []
    for i in range(part * rows, (part + 1) * rows):
        row, lane = F1B + i * 128 // WIDTH, i * 128 % WIDTH
        pieces.append(vec[row : row + 1, lane : lane + 128])
    return jnp.concatenate(pieces, axis=1)


def mlp_forward(vec, fc1_w, fc2_w, middle, n2, slope, active, result):
    def body(seq, carry):
        rows = seq_rows(seq)
        unit, _ = normalise(middle[rows, :])
        normed = (unit * vec[LN2G : LN2G + 1, :] + vec[LN2B : LN2B + 1, :]).astype(BF16)
        n2[rows, :] = normed
        for part in range(FF // CHUNK_FF):
            hidden = mm(normed, fc1_w[:, wide(part)]) + wide_bias(vec, part)
            cdf = 0.5 + 0.5 * lax.erf(hidden * (0.5**0.5))
            active[rows, wide(part)] = (hidden * cdf).astype(BF16)
            density = jnp.exp(hidden * hidden * -0.5) * 0.3989422804014327
            slope[rows, wide(part)] = (cdf + hidden * density).astype(BF16)
        y = middle[rows, :] + (mm(active[rows, :], fc2_w[...]) + vec[F2B : F2B + 1, :])
        result[rows, :] = y.astype(BF16)
        return carry

    lax.fori_loop(0, 2, body, 0, unroll=True)


def mlp_backward(vec, fc1_w, fc2_w, middle, n2, slope, active, dy, dh, dmid, da, sums, emit):
    def body(seq, carry):
        rows = seq_rows(seq)
        dy_rows = dy[rows, :]
        for part in range(FF // WIDTH):
            dactive = mm_right_t(dy_rows, fc2_w[column(part), :])
            low = (slope[rows, column(part)].astype(F32) * dactive).astype(BF16)
            dh[rows, column(part)] = low
            sums[F1B + part : F1B + part + 1, :] += row_sum(low.astype(F32))
        dn2 = mm_right_t(dh[rows, :], fc1_w[...])
        unit, scale = normalise(middle[rows, :])
        dy_wide = dy_rows.astype(F32)
        grad = dy_wide + normalise_back(unit, scale, dn2, vec[LN2G : LN2G + 1, :])
        dmid[rows, :] = grad
        low = grad.astype(BF16)
        da[rows, :] = low
        sums[LN2G : LN2G + 1, :] += row_sum(dn2 * unit)
        sums[LN2B : LN2B + 1, :] += row_sum(dn2)
        sums[F2B : F2B + 1, :] += row_sum(dy_wide)
        sums[PB : PB + 1, :] += row_sum(low.astype(F32))
        return carry

    lax.fori_loop(0, 2, body, 0, unroll=True)
    for part in range(FF // WIDTH):
        emit(part, mm_left_t(active[:, column(part)], dy[:ROWS, :]))
    for part in range(2):
        value = mm_left_t(n2[...], dh[:, part * 2 * WIDTH : (part + 1) * 2 * WIDTH])
        emit(4 + 2 * part, value[:, :WIDTH])
        emit(5 + 2 * part, value[:, WIDTH:])


def attention_backward(
    x, vec, qkv_w, proj_w, n1, qkv, probs, mixed, dmid, da, dt, sums, emit, result
):
    def body(seq, carry):
        rows = seq_rows(seq)
        dmixed = mm_right_t(da[rows, :], proj_w[...]).astype(BF16)
        lanes = head_lanes()
        for pair in range(3):
            q = qkv[rows, pair * 128 : pair * 128 + 128]
            k = qkv[rows, WIDTH + pair * 128 : WIDTH + pair * 128 + 128]
            v = qkv[rows, 2 * WIDTH + pair * 128 : 2 * WIDTH + pair * 128 + 128]
            dm = dmixed[:, pair * 128 : pair * 128 + 128]
            dq = dk = dv = None
            for a in range(2):
                dm_a = only(lanes[a], dm)
                p = probs[seq * 6 + pair * 2 + a]
                dp = mm_right_t(only(lanes[a], v), dm)
                p_wide = p.astype(F32)
                ds = p_wide * (dp - jnp.sum(dp * p_wide, axis=0, keepdims=True))
                ds = ds.astype(BF16)
                parts = (
                    mm_left_t(ds, only(lanes[a], k)),
                    mm(ds, only(lanes[a], q)),
                    mm(p, dm_a),
                )
                if a == 0:
                    dq, dk, dv = parts
                else:
                    dq, dk, dv = dq + parts[0], dk + parts[1], dv + parts[2]
            dq = (dq * HEAD**-0.5).astype(BF16)
            dv = dv.astype(BF16)
            here = slice(pair * 128, pair * 128 + 128)
            dt[rows, pair * 128 : pair * 128 + 128] = dq
            dt[rows, WIDTH + pair * 128 : WIDTH + pair * 128 + 128] = dk.astype(BF16)
            dt[rows, 2 * WIDTH + pair * 128 : 2 * WIDTH + pair * 128 + 128] = dv
            sums[QB : QB + 1, here] += row_sum(dq.astype(F32))
            sums[VB : VB + 1, here] += row_sum(dv.astype(F32))
        dn1 = mm_right_t(dt[rows, :], qkv_w[...])
        unit, scale = normalise(x[rows, :].astype(F32))
        grad = dmid[rows, :] + normalise_back(unit, scale, dn1, vec[LN1G : LN1G + 1, :])
        result[rows, :] = grad.astype(BF16)
        sums[LN1G : LN1G + 1, :] += row_sum(dn1 * unit)
        sums[LN1B : LN1B + 1, :] += row_sum(dn1)
        return carry

    lax.fori_loop(0, 2, body, 0, unroll=True)
    emit(8, mm_left_t(mixed[...], da[...]))
    value = mm_left_t(n1[...], dt[...])
    for part in range(3):
        emit(9 + part, value[:, column(part)])


def make_emit(keep, send, core, first, blocks):
    def emit(block, value):
        half, place = block % 2, (block - first) // 2
        rows = slice(place * WIDTH, (place + 1) * WIDTH)
        low = value.astype(BF16)

        @pl.when(core == half)
        def _():
            keep[rows, :] = low

        @pl.when(core != half)
        def _():
            send[rows, :] = low

    return emit


def start_all(copies):
    for copy in copies:
        copy.start()


def wait_all(copies):
    for copy in copies:
        copy.wait()


def forward_kernel(*refs):
    own, got = refs[:1] + refs[2:6], refs[1:2] + refs[6:10]
    (
        pack, qkv_w, proj_w, fc1_w, fc2_w, vec, between,
        n1, qkv, probs, mixed, middle, n2, slope, active, result,
        dmid, da, sums, keep_out, send_out,
        masks, dh, in_sem,
    ) = refs[10:]
    core = lax.axis_index("section")
    other = 1 - core
    held = (pack, qkv_w, proj_w, fc1_w, fc2_w)

    def load(sources, layer, i):
        return pltpu.make_async_copy(sources[i], held[i].at[layer], in_sem.at[layer, i])

    for i in range(5):
        load(own, core, i).start()
        load(got, other, i).start()
    fill_masks(masks)
    sums[...] = jnp.zeros_like(sums)
    for layer in range(2):
        load(own, layer, 0).wait()
        vec[layer] = pack[layer, ROWS:, :].astype(F32)
    for layer in range(2):
        for i in (1, 2):
            load(own, layer, i).wait()
        x = pack.at[0] if layer == 0 else between
        attention_forward(
            x, vec.at[layer], masks, qkv_w.at[layer], proj_w.at[layer],
            n1.at[layer], qkv.at[layer], probs.at[layer], mixed.at[layer], middle.at[layer],
        )
        for i in (3, 4):
            load(own, layer, i).wait()
        mlp_forward(
            vec.at[layer], fc1_w.at[layer], fc2_w.at[layer], middle.at[layer], n2.at[layer],
            slope.at[layer], active.at[layer], between if layer == 0 else result,
        )
    mlp_backward(
        vec.at[1], fc1_w.at[1], fc2_w.at[1], middle.at[1], n2.at[1], slope.at[1], active.at[1],
        pack.at[1], dh, dmid, da, sums, make_emit(keep_out, send_out, core, 0, 8),
    )


def attention_backward_kernel(layer, *refs):
    (
        x, vec, qkv_w, proj_w, n1, qkv, probs, mixed, dmid, da, sums_in,
        dx, keep_out, send_out, dt, sums,
    ) = refs
    core = lax.axis_index("section")
    sums[...] = sums_in[...]
    attention_backward(
        x, vec.at[layer], qkv_w.at[layer], proj_w.at[layer], n1.at[layer], qkv.at[layer],
        probs.at[layer], mixed.at[layer], dmid, da, dt, sums,
        make_emit(keep_out, send_out, core, 8, 4), dx,
    )
    keep_out[2 * WIDTH :, :] = sums[...].astype(BF16)
    send_out[2 * WIDTH :, :] = sums[...].astype(BF16)


def last_backward_kernel(*refs):
    pack, result, rows_keep, rows_send, dx = refs[0], refs[11], refs[12], refs[13], refs[-1]
    attention_backward_kernel(
        0, pack.at[0], *refs[1:11], dx, refs[14], refs[15], refs[16], refs[17]
    )
    core = lax.axis_index("section")

    @pl.when(core == 0)
    def _():
        rows_keep[...] = dx[...]
        rows_send[...] = result[...]

    @pl.when(core == 1)
    def _():
        rows_keep[...] = result[...]
        rows_send[...] = dx[...]


def mlp_backward_kernel(*refs):
    (
        vec, fc1_w, fc2_w, middle, n2, slope, active, dy, dmid, da, sums, keep_out, send_out, dh,
    ) = refs
    core = lax.axis_index("section")
    sums[...] = jnp.zeros_like(sums)
    mlp_backward(
        vec.at[0], fc1_w.at[0], fc2_w.at[0], middle.at[0], n2.at[0], slope.at[0], active.at[0],
        dy, dh, dmid, da, sums, make_emit(keep_out, send_out, core, 0, 8),
    )


def rows_kernel(tails, keep, recv, g_out, l_out, wide):
    core = lax.axis_index("section")
    tail = tails.at[0]
    for source, half in ((keep, core), (recv, 1 - core)):
        wide[...] = source[...].astype(F32)
        live = jnp.where(core == 1, live_flag(tail, half), 1.0)
        g_out[half] = (wide[:GT, :] * live).astype(BF16)
        for j in range(LOCALS):
            crop = half * LOCALS + j
            live = jnp.where(core == 1, live_flag(tail, 2 + crop), 1.0)
            piece = wide[SEQ + j * SLOT : SEQ + j * SLOT + LT, :]
            l_out[crop] = (piece * live).astype(BF16)


def out_block(own, got, index):
    core = lax.axis_index("section")
    place = index // 2
    rows = slice(place * WIDTH, (place + 1) * WIDTH)
    return jnp.where(core == index % 2, own[rows, :], got[rows, :]).astype(F32)


def write_blocks(own, got, places, held, sem):
    copies = []
    for i, place in enumerate(places):
        held[i] = out_block(own, got, i)
        copies.append(pltpu.make_async_copy(held.at[i], place, sem.at[i]))
        copies[-1].start()
    return copies


def mlp_out_kernel(own, got, fc1, fc2, held, sem):
    places = [fc2.at[0, column(part), :] for part in range(4)]
    places += [fc1.at[0, :, column(part)] for part in range(4)]
    wait_all(write_blocks(own, got, places, held, sem))


def attention_out_kernel(*refs):
    (
        own, got, sums_a, sums_b,
        ln1g, ln1b, qkv, qb, vb, proj, pb, ln2g, ln2b, fc1b, fc2b, held, sem,
    ) = refs
    places = [proj.at[0]] + [qkv.at[0, :, column(part)] for part in range(3)]
    copies = write_blocks(own, got, places, held, sem)
    core = lax.axis_index("section")
    sums = jnp.where(core == 0, sums_a[...], sums_b[...])
    for out, row in (
        (ln1g, LN1G), (ln1b, LN1B), (qb, QB), (vb, VB), (pb, PB), (ln2g, LN2G), (ln2b, LN2B),
        (fc2b, F2B),
    ):
        out[...] = sums[row : row + 1, :]
    for part in range(4):
        fc1b[:, column(part)] = sums[F1B + part : F1B + part + 1, :]
    wait_all(copies)


def shape(*dims, dtype=BF16):
    return jax.ShapeDtypeStruct(dims, dtype)


class Ordered:
    def __init__(self):
        self.last = None

    def __call__(
        self, name, kernel, outs, in_specs, out_specs, scratch=(), vmem=8, cost=1
    ):
        before = [] if self.last is None else [self.last]
        count = len(in_specs)

        def body(*refs):
            kernel(*refs[:count], *refs[count + len(before) :])

        def run(*args):
            results = pl.pallas_call(
                body,
                out_shape=outs,
                name=name,
                in_specs=list(in_specs) + [ANY] * len(before),
                out_specs=out_specs,
                scratch_shapes=list(scratch),
                compiler_params=pltpu.CompilerParams(vmem_limit_bytes=vmem * 1024 * 1024),
                cost_estimate=pl.CostEstimate(
                    flops=cost * COST, bytes_accessed=0, transcendentals=0
                ),
            )(*args, *before)
            self.last = results[-1]
            return results

        return run


CHUNK = 48


def add_rows(out, start_out, left, right, start, count):
    def step(i, carry):
        here = pl.ds(pl.multiple_of(start + i * CHUNK, 16), CHUNK)
        there = pl.ds(pl.multiple_of(start_out + i * CHUNK, 16), CHUNK)
        out[there, :] = (left[here, :].astype(F32) + right[here, :].astype(F32)).astype(BF16)
        return carry

    lax.fori_loop(0, count // CHUNK, step, 0, unroll=2)


def add_tail(outs, start_out, left, right, start):
    if left.shape[0] == start:
        return
    here = slice(start, start + VECS)
    tail = (left[here, :].astype(F32) + right[here, :].astype(F32)).astype(BF16)
    for out in outs:
        out[start_out : start_out + VECS, :] = tail


def bit_of(dims, step):
    dp = lax.axis_index("dp")
    core = lax.axis_index("section")
    return jnp.where(core == 0, dp >> dims[0][step] & 1, dp >> dims[1][step] & 1)


def halve_kernel(dims, step, count, keep, recv, keep_out, send_out):
    bit = bit_of(dims, step)
    half = count // 2
    add_rows(send_out, 0, keep, recv, (1 - bit) * half, half)
    add_rows(keep_out, 0, keep, recv, bit * half, half)
    add_tail((keep_out, send_out), half, keep, recv, count)


def sum_kernel(count, keep, recv, out):
    add_rows(out, 0, keep, recv, 0, count)
    add_tail((out,), count, keep, recv, count)


def total_kernel(count, own, recv, total_out, *sums_out):
    add_rows(total_out, 0, own, recv, 0, count)
    for out in sums_out:
        out[...] = own[count:, :].astype(F32) + recv[count:, :].astype(F32)


def join_rows(out, own, recv, bit):
    count = own.shape[0]
    for ref, half in ((own, bit), (recv, 1 - bit)):
        out[pl.ds(pl.multiple_of(half * count, 16), count), :] = ref[...]


def join_kernel(dims, step, own, recv, out):
    join_rows(out, own, recv, bit_of(dims, step))


def last_join_kernel(dims, own, recv, other, mine, send, whole):
    join_rows(whole, own, recv, bit_of(dims, 0))
    core = lax.axis_index("section")

    @pl.when(core == 0)
    def _():
        mine[...] = whole[...]
        send[...] = other[...]

    @pl.when(core == 1)
    def _():
        mine[...] = other[...]
        send[...] = whole[...]


def exchange(values_in, dims, step):
    pairs = [
        (core * 16 + dp, core * 16 + (dp ^ 1 << dims[core][step]))
        for core in range(2)
        for dp in range(16)
    ]
    return lax.ppermute(values_in, ("section", "dp"), pairs)


class Reduction:
    def __init__(self, name, call, dims, keep, send, count):
        self.name, self.call, self.dims = name, call, dims
        self.keep, self.recv, self.count = keep, swap(send), count
        self.steps = self.run(count, keep.shape[0] - count)

    def kernel(self, label, body, rows, *args):
        outs = [shape(n, WIDTH) for n in rows]
        return self.call(
            f"{self.name}_{label}", body, outs, [VMEM] * len(args), [VMEM] * len(outs)
        )(*args)

    def run(self, count, tail):
        keep, recv = self.keep, self.recv
        for step in range(3):
            body = functools.partial(halve_kernel, self.dims, step, count)
            count //= 2
            keep, send = self.kernel(f"halve{step}", body, [count + tail] * 2, keep, recv)
            recv = exchange(send, self.dims, step)
            yield
        body = functools.partial(sum_kernel, count)
        (own,) = self.kernel("sum", body, [count + tail], keep, recv)
        recv = exchange(own, self.dims, 3)
        yield
        whole, *sums = self.call(
            f"{self.name}_total",
            functools.partial(total_kernel, count),
            [shape(count, WIDTH)] + [shape(tail, WIDTH, dtype=F32)] * bool(tail),
            [VMEM] * 2,
            [VMEM] * (1 + bool(tail)),
        )(own, recv)
        self.sums = sums
        for step in (2, 1, 0):
            recv = exchange(whole, self.dims, step)
            self.pair = (whole, recv)
            yield
            if step:
                body = functools.partial(join_kernel, self.dims, step)
                (whole,) = self.kernel(f"join{step}", body, [2 * whole.shape[0]], whole, recv)

    def advance(self):
        next(self.steps)

    def last(self):
        body = functools.partial(join_kernel, self.dims, 0)
        (self.whole,) = self.kernel("join0", body, [self.count], *self.pair)

    def last_sorted(self, other):
        mine, send = self.call(
            f"{self.name}_last",
            functools.partial(last_join_kernel, self.dims),
            [shape(self.count, WIDTH)] * 2,
            [VMEM] * 3,
            [VMEM] * 2,
            [pltpu.VMEM((self.count, WIDTH), BF16)],
        )(*self.pair, other.whole)
        return mine, swap(send)


class PlainReduction(Reduction):
    def advance(self):
        pass

    def last(self):
        total = lax.psum(self.keep.astype(F32) + self.recv.astype(F32), "dp")
        self.whole = total[: self.count].astype(BF16)
        self.sums = [total[self.count :]] * (total.shape[0] > self.count)

    def last_sorted(self, other):
        self.last()
        leading = lax.axis_index("section") == 0
        pair = (self.whole, other.whole)
        return jnp.where(leading, *pair), swap(jnp.where(leading, *pair[::-1]))


def swap(values_in):
    return lax.ppermute(values_in, "section", [(0, 1), (1, 0)])


def on_device(dp_size, global_ends, local_ends, global_live, local_live, *weights):
    (
        ln1_gain, ln1_bias, qkv_weight, query_bias, value_bias, proj_weight, proj_bias,
        ln2_gain, ln2_bias, fc1_weight, fc1_bias, fc2_weight, fc2_bias,
    ) = weights
    matrices = tuple(w[0] for w in (qkv_weight, proj_weight, fc1_weight, fc2_weight))
    got = tuple(swap(w) for w in matrices)
    vectors = (
        ln1_gain, ln1_bias, query_bias, value_bias, proj_bias, ln2_gain, ln2_bias, fc2_bias,
        fc1_bias,
    )
    flags = jnp.concatenate([global_live, local_live]).astype(F32)
    tail = jnp.concatenate(
        [vector.reshape(-1, WIDTH).astype(F32) for vector in vectors]
        + [jnp.pad(flags, (0, WIDTH - flags.shape[0]))[None]]
    )
    tail = jnp.pad(tail, ((0, VECS - tail.shape[0]), (0, 0)))
    call = Ordered()
    keep, send = call(
        "pack",
        pack_kernel,
        [shape(ROWS + VECS, WIDTH)] * 2,
        [VMEM] * 3,
        [VMEM] * 2,
        [pltpu.VMEM((ROWS, WIDTH), F32)],
        cost=PACK_COST,
    )(global_ends[0], local_ends[0], tail)
    recv = swap(send)
    weight_shapes = [(WIDTH, 3 * WIDTH), (WIDTH, WIDTH), (WIDTH, FF), (FF, WIDTH)]
    rows_low, rows_wide = shape(ROWS, WIDTH), shape(ROWS, WIDTH, dtype=F32)
    sums_shape = shape(VECS, WIDTH, dtype=F32)
    mlp_pair = [shape(4 * WIDTH, WIDTH)] * 2
    attention_pair = [shape(2 * WIDTH + VECS, WIDTH)] * 2
    outs = (
        [shape(2, ROWS + VECS, WIDTH)]
        + [shape(2, *dims) for dims in weight_shapes]
        + [
            shape(2, VECS, WIDTH, dtype=F32),
            rows_low,
            shape(2, ROWS, WIDTH),
            shape(2, ROWS, 3 * WIDTH),
            shape(2, 12, SEQ, SEQ),
            shape(2, ROWS, WIDTH),
            shape(2, ROWS, WIDTH, dtype=F32),
            shape(2, ROWS, WIDTH),
            shape(2, ROWS, FF),
            shape(2, ROWS, FF),
            rows_low,
            rows_wide,
            rows_low,
            sums_shape,
        ]
        + mlp_pair
    )
    (
        pack, qkv_w, proj_w, fc1_w, fc2_w, vec, between,
        n1, qkv, probs, mixed, middle, n2, slope, active, result,
        dmid, da, sums, keep_1, send_1,
    ) = call(
        "forward",
        forward_kernel,
        outs,
        [HBM] * 10,
        [VMEM] * len(outs),
        [
            pltpu.VMEM((2, SEQ, SEQ), F32),
            pltpu.VMEM((ROWS, FF), BF16),
            pltpu.SemaphoreType.DMA((2, 5)),
        ],
        vmem=KA_VMEM,
    )(keep, recv, *matrices, *got)
    reduction = Reduction if dp_size == 16 else PlainReduction
    chains, held = {}, {}

    def begin(name, keep, send):
        count = PART_ROWS[name[1]]
        chains[name] = reduction(name, call, DIMS[name], keep, send, count)

    begin("bm", keep_1, send_1)
    wide_work = [pltpu.VMEM((ROWS, 3 * WIDTH), BF16), pltpu.VMEM((VECS, WIDTH), F32)]
    def back_b_attention():
        held["dx"], keep, send = call(
            "back_b_attention",
            functools.partial(attention_backward_kernel, 1),
            [rows_low] + attention_pair,
            [VMEM] * 11,
            [VMEM] * 3,
            wide_work,
            vmem=KB_VMEM,
        )(between, vec, qkv_w, proj_w, n1, qkv, probs, mixed, dmid, da, sums)
        begin("ba", keep, send)

    def back_a_mlp():
        *held["mlp"], keep, send = call(
            "back_a_mlp",
            mlp_backward_kernel,
            [rows_wide, rows_low, sums_shape] + mlp_pair,
            [VMEM] * 8,
            [VMEM] * 5,
            [pltpu.VMEM((ROWS, FF), BF16)],
            vmem=KB_VMEM,
        )(vec, fc1_w, fc2_w, middle, n2, slope, active, held["dx"])
        begin("am", keep, send)

    def back_a_attention():
        held["rows"], rows_send, keep, send = call(
            "back_a_attention",
            last_backward_kernel,
            [rows_low] * 2 + attention_pair,
            [VMEM] * 12,
            [VMEM] * 4,
            wide_work + [pltpu.VMEM((ROWS, WIDTH), BF16)],
            vmem=KB_VMEM,
        )(pack, vec, qkv_w, proj_w, n1, qkv, probs, mixed, *held["mlp"], result)
        begin("aa", keep, send)
        held["rows_got"] = swap(rows_send)

    def rows_out():
        held["rows_out"] = call(
            "rows_out",
            rows_kernel,
            [shape(*global_ends.shape[1:]), shape(*local_ends.shape[1:])],
            [VMEM] * 3,
            [VMEM] * 2,
            [pltpu.VMEM((ROWS, WIDTH), F32)],
        )(vec, held["rows"], held["rows_got"])

    def grad(w):
        return shape(*w.shape, dtype=F32)

    def last_sorted(part):
        held[part] = chains["a" + part].last_sorted(chains["b" + part])

    def mlp_out():
        held["mlp_out"] = call(
            "mlp_out",
            mlp_out_kernel,
            [grad(fc1_weight), grad(fc2_weight)],
            [VMEM] * 2,
            [ANY] * 2,
            [pltpu.VMEM((8, WIDTH, WIDTH), F32), pltpu.SemaphoreType.DMA((8,))],
            vmem=16,
        )(*held["m"])

    def attention_out():
        wanted = (
            ln1_gain, ln1_bias, qkv_weight, query_bias, value_bias, proj_weight,
            proj_bias, ln2_gain, ln2_bias, fc1_bias, fc2_bias,
        )
        held["attention_out"] = call(
            "attention_out",
            attention_out_kernel,
            [grad(w) for w in wanted],
            [VMEM] * 4,
            [ANY if w.ndim == 3 else VMEM for w in wanted],
            [pltpu.VMEM((4, WIDTH, WIDTH), F32), pltpu.SemaphoreType.DMA((4,))],
        )(*held["a"], *chains["aa"].sums, *chains["ba"].sums)

    actions = {
        "b": back_b_attention, "c": back_a_mlp, "d": back_a_attention,
        "r": rows_out, "p": mlp_out, "q": attention_out,
        "w": lambda: chains["bm"].advance(), "x": lambda: chains["ba"].advance(),
        "y": lambda: chains["am"].advance(), "z": lambda: chains["aa"].advance(),
        "W": lambda: chains["bm"].last(), "X": lambda: chains["ba"].last(),
        "Y": lambda: last_sorted("m"), "Z": lambda: last_sorted("a"),
    }
    for name in ORDER:
        actions[name]()
    global_out, local_out = held["rows_out"]
    grad_fc1, grad_fc2 = held["mlp_out"]
    (
        grad_ln1_gain, grad_ln1_bias, grad_qkv, grad_query_bias, grad_value_bias, grad_proj,
        grad_proj_bias, grad_ln2_gain, grad_ln2_bias, grad_fc1_bias, grad_fc2_bias,
    ) = held["attention_out"]
    return (
        global_out[None], local_out[None],
        grad_ln1_gain, grad_ln1_bias, grad_qkv, grad_query_bias, grad_value_bias, grad_proj,
        grad_proj_bias, grad_ln2_gain, grad_ln2_bias, grad_fc1, grad_fc1_bias, grad_fc2,
        grad_fc2_bias,
    )


def solution(mesh):
    matrix, vector = P("section", None, None), P("section", None)
    weights = (
        vector, vector, matrix, vector, vector, matrix, vector,
        vector, vector, matrix, vector, matrix, vector,
    )
    rows = P("section", "dp", None, None)
    return jax.shard_map(
        functools.partial(on_device, mesh.shape["dp"]),
        mesh=mesh,
        in_specs=(rows, rows, P("dp"), P("dp")) + weights,
        out_specs=(rows, rows) + weights,
        check_vma=False,
    )
```

```python
import functools

import jax
import jax.numpy as jnp
from jax import lax
from jax.experimental import pallas as pl
from jax.experimental.pallas import tpu as pltpu
from jax.sharding import PartitionSpec as P

HEAD = 64
GT = 197
LT = 37
WIDTH = 384
FF = 1536
SEQ = 208
ROWS = 2 * SEQ
SLOT = 40
LOCALS = 5
VECS = 16
EPSILON = 1e-06
MASKED = -1e30
CHUNK_FF = 768
ORDER = "bcwxydwzxwywxzywyzwyxwzxyzWxzyxzrYXZpq"
DIMS = {
    "bm": ((0, 1, 2, 3), (1, 2, 0, 3)),
    "ba": ((1, 2, 0, 3), (2, 1, 0, 3)),
    "am": ((0, 2, 1, 3), (2, 1, 0, 3)),
    "aa": ((0, 1, 2, 3), (1, 2, 0, 3)),
}
PART_ROWS = {"m": 4 * WIDTH, "a": 2 * WIDTH}
COST = 10000000000
PACK_COST = 10
PACK_VMEM = 55
FIRST_VMEM = 8
KA_VMEM = 16
OUT_VMEM = 8
ROWS_VMEM = 8
LAST_VMEM = 8
KB_VMEM = 12
LN1G, LN1B, QB, VB, PB, LN2G, LN2B, F2B, F1B = range(9)
LIVE = 12
PROJ = ROWS + VECS
PACKED = PROJ + WIDTH
BF16 = jnp.bfloat16
F32 = jnp.float32
ANY = pl.BlockSpec(memory_space=pl.ANY)
VMEM = pl.BlockSpec(memory_space=pltpu.VMEM)
SMEM = pl.BlockSpec(memory_space=pltpu.SMEM)


def mm(left, right):
    return jnp.dot(left, right, preferred_element_type=F32)


def mm_right_t(left, right):
    return lax.dot_general(left, right, (((1,), (1,)), ((), ())), preferred_element_type=F32)


def mm_left_t(left, right):
    return lax.dot_general(left, right, (((0,), (0,)), ((), ())), preferred_element_type=F32)


def normalise(values_in):
    centred = values_in - jnp.mean(values_in, axis=-1, keepdims=True)
    scale = lax.rsqrt(jnp.mean(centred * centred, axis=-1, keepdims=True) + EPSILON)
    return centred * scale, scale


def normalise_back(unit, scale, grad_rows, gain):
    e = grad_rows * gain
    return scale * (
        e
        - jnp.mean(e, axis=-1, keepdims=True)
        - unit * jnp.mean(e * unit, axis=-1, keepdims=True)
    )


def seq_rows(seq):
    return pl.ds(pl.multiple_of(seq * SEQ, 16), SEQ)


def column(block):
    return slice(block * WIDTH, (block + 1) * WIDTH)


def wide(part):
    return slice(part * CHUNK_FF, (part + 1) * CHUNK_FF)


def row_sum(values_in):
    return jnp.sum(values_in, axis=0, keepdims=True)


def live_flag(vec, index):
    lane = lax.broadcasted_iota(jnp.int32, (1, WIDTH), 1)
    flags = vec[LIVE : LIVE + 1, :]
    return jnp.sum(jnp.where(lane == index, flags, 0.0), axis=1, keepdims=True)


def pack_kernel(*refs):
    sources, (keep, send), held = refs[:12], refs[12:14], refs[14:26]
    rows, tail, sem = refs[26:]
    g, l, proj, vecs = held[0], held[1], held[2], held[3:]
    copies = [
        pltpu.make_async_copy(source, place, sem.at[i])
        for i, (source, place) in enumerate(zip(sources, held))
    ]
    start_all(copies)
    core = lax.axis_index("section")
    rows[...] = jnp.zeros_like(rows)
    tail[...] = jnp.zeros_like(tail)
    wait_all(copies)
    for i, vec in enumerate(vecs[:8]):
        tail[i : i + 1, :] = vec[...].astype(F32)
    for i in range(FF // WIDTH):
        tail[F1B + i : F1B + i + 1, :] = vecs[8][:, column(i)].astype(F32)
    crops = g[...].astype(F32)
    for out, half in ((keep, core), (send, 1 - core)):
        rows[:GT, :] = jnp.where(half == 0, crops[:, 0, :], crops[:, 1, :])
        for j in range(LOCALS):
            rows[SEQ + j * SLOT : SEQ + j * SLOT + LT, :] = l[half * LOCALS + j].astype(F32)
        out[:ROWS, :] = rows[...].astype(BF16)
        out[ROWS:PROJ, :] = tail[...].astype(BF16)
        out[PROJ:, :] = proj[...]


def crop_of(axis):
    dims = (SEQ, 1) if axis == 0 else (1, SEQ)
    row = lax.broadcasted_iota(jnp.int32, dims, axis)
    crop = jnp.zeros(dims, jnp.int32)
    for j in range(1, LOCALS + 1):
        crop += (row >= j * SLOT).astype(jnp.int32)
    return crop, (crop < LOCALS) & (row - crop * SLOT < LT)


def head_lanes():
    lane = lax.broadcasted_iota(jnp.int32, (SEQ, 2 * HEAD), 1)
    return (lane < HEAD, lane >= HEAD)


def only(mask, values_in):
    return jnp.where(mask, values_in, jnp.zeros_like(values_in))


def attention_forward(x, vec, masks, qkv_w, proj_w, n1, qkv, probs, mixed, middle):
    def body(seq, carry):
        rows = seq_rows(seq)
        x_rows = x[rows, :].astype(F32)
        unit, _ = normalise(x_rows)
        normed = (unit * vec[LN1G : LN1G + 1, :] + vec[LN1B : LN1B + 1, :]).astype(BF16)
        n1[rows, :] = normed
        triple = mm(normed, qkv_w[...])
        query = (triple[:, :WIDTH] + vec[QB : QB + 1, :]).astype(BF16) * BF16(HEAD**-0.5)
        qkv[rows, :WIDTH] = query
        qkv[rows, column(1)] = triple[:, column(1)].astype(BF16)
        qkv[rows, column(2)] = (triple[:, column(2)] + vec[VB : VB + 1, :]).astype(BF16)
        lanes = head_lanes()
        mask = masks[seq]
        for pair in range(3):
            q = qkv[rows, pair * 128 : pair * 128 + 128]
            k = qkv[rows, WIDTH + pair * 128 : WIDTH + pair * 128 + 128]
            v = qkv[rows, 2 * WIDTH + pair * 128 : 2 * WIDTH + pair * 128 + 128]
            total = None
            for a in range(2):
                s = mm_right_t(only(lanes[a], k), q) + mask
                e = jnp.exp(s - jnp.max(s, axis=0, keepdims=True))
                p = (e * (1.0 / jnp.sum(e, axis=0, keepdims=True))).astype(BF16)
                probs[seq * 6 + pair * 2 + a] = p
                part = mm_left_t(p, only(lanes[a], v))
                total = part if total is None else total + part
            mixed[rows, pair * 128 : pair * 128 + 128] = total.astype(BF16)
        middle[rows, :] = x_rows + (mm(mixed[rows, :], proj_w[...]) + vec[PB : PB + 1, :])
        return carry

    lax.fori_loop(0, 2, body, 0, unroll=True)


def wide_bias(vec, part):
    rows = CHUNK_FF // 128
    pieces = []
    for i in range(part * rows, (part + 1) * rows):
        row, lane = F1B + i * 128 // WIDTH, i * 128 % WIDTH
        pieces.append(vec[row : row + 1, lane : lane + 128])
    return jnp.concatenate(pieces, axis=1)


def mlp_forward(vec, fc1_w, fc2_w, middle, n2, slope, active, result):
    def body(seq, carry):
        rows = seq_rows(seq)
        unit, _ = normalise(middle[rows, :])
        normed = (unit * vec[LN2G : LN2G + 1, :] + vec[LN2B : LN2B + 1, :]).astype(BF16)
        n2[rows, :] = normed
        for part in range(FF // CHUNK_FF):
            hidden = mm(normed, fc1_w[:, wide(part)]) + wide_bias(vec, part)
            cdf = 0.5 + 0.5 * lax.erf(hidden * (0.5**0.5))
            active[rows, wide(part)] = (hidden * cdf).astype(BF16)
            density = jnp.exp(hidden * hidden * -0.5) * 0.3989422804014327
            slope[rows, wide(part)] = (cdf + hidden * density).astype(BF16)
        y = middle[rows, :] + (mm(active[rows, :], fc2_w[...]) + vec[F2B : F2B + 1, :])
        result[rows, :] = y.astype(BF16)
        return carry

    lax.fori_loop(0, 2, body, 0, unroll=True)


def mlp_backward(vec, fc1_w, fc2_w, middle, n2, slope, active, dy, dh, dmid, da, sums, emit):
    def body(seq, carry):
        rows = seq_rows(seq)
        dy_rows = dy[rows, :]
        for part in range(FF // WIDTH):
            dactive = mm_right_t(dy_rows, fc2_w[column(part), :])
            low = (slope[rows, column(part)].astype(F32) * dactive).astype(BF16)
            dh[rows, column(part)] = low
            sums[F1B + part : F1B + part + 1, :] += row_sum(low.astype(F32))
        dn2 = mm_right_t(dh[rows, :], fc1_w[...])
        unit, scale = normalise(middle[rows, :])
        dy_wide = dy_rows.astype(F32)
        grad = dy_wide + normalise_back(unit, scale, dn2, vec[LN2G : LN2G + 1, :])
        dmid[rows, :] = grad
        low = grad.astype(BF16)
        da[rows, :] = low
        sums[LN2G : LN2G + 1, :] += row_sum(dn2 * unit)
        sums[LN2B : LN2B + 1, :] += row_sum(dn2)
        sums[F2B : F2B + 1, :] += row_sum(dy_wide)
        sums[PB : PB + 1, :] += row_sum(low.astype(F32))
        return carry

    lax.fori_loop(0, 2, body, 0, unroll=True)
    for pair in range(2):
        parts = (column(2 * pair), column(2 * pair + 1))
        emit(pair, *(mm_left_t(active[:, part], dy[:ROWS, :]) for part in parts))
    for part in range(2):
        value = mm_left_t(n2[...], dh[:, part * 2 * WIDTH : (part + 1) * 2 * WIDTH])
        emit(2 + part, value[:, :WIDTH], value[:, WIDTH:])


def attention_backward(
    x, vec, qkv_w, proj_w, n1, qkv, probs, mixed, dmid, da, dt, sums, emit, result
):
    def body(seq, carry):
        rows = seq_rows(seq)
        dmixed = mm_right_t(da[rows, :], proj_w[...]).astype(BF16)
        lanes = head_lanes()
        for pair in range(3):
            q = qkv[rows, pair * 128 : pair * 128 + 128]
            k = qkv[rows, WIDTH + pair * 128 : WIDTH + pair * 128 + 128]
            v = qkv[rows, 2 * WIDTH + pair * 128 : 2 * WIDTH + pair * 128 + 128]
            dm = dmixed[:, pair * 128 : pair * 128 + 128]
            dq = dk = dv = None
            for a in range(2):
                dm_a = only(lanes[a], dm)
                p = probs[seq * 6 + pair * 2 + a]
                dp = mm_right_t(only(lanes[a], v), dm)
                p_wide = p.astype(F32)
                ds = p_wide * (dp - jnp.sum(dp * p_wide, axis=0, keepdims=True))
                ds = ds.astype(BF16)
                parts = (
                    mm_left_t(ds, only(lanes[a], k)),
                    mm(ds, only(lanes[a], q)),
                    mm(p, dm_a),
                )
                if a == 0:
                    dq, dk, dv = parts
                else:
                    dq, dk, dv = dq + parts[0], dk + parts[1], dv + parts[2]
            dq = (dq * HEAD**-0.5).astype(BF16)
            dv = dv.astype(BF16)
            here = slice(pair * 128, pair * 128 + 128)
            dt[rows, pair * 128 : pair * 128 + 128] = dq
            dt[rows, WIDTH + pair * 128 : WIDTH + pair * 128 + 128] = dk.astype(BF16)
            dt[rows, 2 * WIDTH + pair * 128 : 2 * WIDTH + pair * 128 + 128] = dv
            sums[QB : QB + 1, here] += row_sum(dq.astype(F32))
            sums[VB : VB + 1, here] += row_sum(dv.astype(F32))
        dn1 = mm_right_t(dt[rows, :], qkv_w[...])
        unit, scale = normalise(x[rows, :].astype(F32))
        grad = dmid[rows, :] + normalise_back(unit, scale, dn1, vec[LN1G : LN1G + 1, :])
        result[rows, :] = grad.astype(BF16)
        sums[LN1G : LN1G + 1, :] += row_sum(dn1 * unit)
        sums[LN1B : LN1B + 1, :] += row_sum(dn1)
        return carry

    lax.fori_loop(0, 2, body, 0, unroll=True)
    value = mm_left_t(n1[...], dt[...])
    emit(0, mm_left_t(mixed[...], da[...]), value[:, column(0)])
    emit(1, value[:, column(1)], value[:, column(2)])


def make_emit(keep, send, core):
    def emit(pair, first, second):
        rows = slice(pair * WIDTH, (pair + 1) * WIDTH)
        first, second = first.astype(BF16), second.astype(BF16)
        keep[rows, :] = jnp.where(core == 0, first, second)
        send[rows, :] = jnp.where(core == 0, second, first)

    return emit


def start_all(copies):
    for copy in copies:
        copy.start()


def wait_all(copies):
    for copy in copies:
        copy.wait()


def hold_flags(glive, llive, vec, dy):
    core = lax.axis_index("section")
    lane = lax.broadcasted_iota(jnp.int32, (1, WIDTH), 1)
    flags = jnp.zeros((1, WIDTH), F32)
    for i in range(2):
        flags = jnp.where(lane == i, glive[i].astype(F32), flags)
    for i in range(2 * LOCALS):
        flags = jnp.where(lane == 2 + i, llive[i].astype(F32), flags)
    vec[LIVE : LIVE + 1, :] = flags
    crop, _ = crop_of(0)
    live = jnp.zeros((SEQ, 1), F32)
    for j in range(LOCALS):
        live = jnp.where(crop == j, llive[core * LOCALS + j].astype(F32), live)
    dy[:SEQ, :] = (dy[:SEQ, :].astype(F32) * glive[core].astype(F32)).astype(BF16)
    dy[SEQ:ROWS, :] = (dy[SEQ:ROWS, :].astype(F32) * live).astype(BF16)


def sort_by_core(own, got, first, second):
    core = lax.axis_index("section")
    first[...] = jnp.where(core == 0, own[...], got[...])
    second[...] = jnp.where(core == 0, got[...], own[...])


def settle_kernel(_, own, got, masks, qkv_w):
    key = lax.broadcasted_iota(jnp.int32, (SEQ, SEQ), 0)
    masks[0] = jnp.where(key < GT, 0.0, MASKED)
    key_crop, true_key = crop_of(0)
    query_crop, _ = crop_of(1)
    masks[1] = jnp.where(jnp.where(true_key, key_crop, -1) == query_crop, 0.0, MASKED)
    sort_by_core(own, got, qkv_w.at[0], qkv_w.at[1])


def first_attention_kernel(*refs):
    (
        glive, llive, keep, recv, qkv_w, masks,
        pack, vec, n1, qkv, probs, mixed, middle,
    ) = refs
    sort_by_core(keep, recv, pack.at[0], pack.at[1])
    for layer in range(2):
        vec[layer] = pack[layer, ROWS:PROJ, :].astype(F32)
    hold_flags(glive, llive, vec.at[0], pack.at[1])
    attention_forward(
        pack.at[0], vec.at[0], masks, qkv_w.at[0], pack.at[0, pl.ds(PROJ, WIDTH)],
        n1, qkv, probs, mixed, middle,
    )


def forward_kernel(*refs):
    (
        fc1_own, fc2_own, fc1_got, fc2_got, pack, qkv_w, vec, masks, middle_a,
        fc1_a, fc2_a, between, result, n2_a, slope_a, active_a,
        n1_b, qkv_b, probs_b, mixed_b, dmid, da, sums, keep_out, send_out,
        fc1_b, fc2_b, middle_b, n2_b, slope_b, active_b, dh,
    ) = refs
    core = lax.axis_index("section")
    sort_by_core(fc1_own, fc1_got, fc1_a, fc1_b)
    sort_by_core(fc2_own, fc2_got, fc2_a, fc2_b)
    sums[...] = jnp.zeros_like(sums)
    mlp_forward(vec.at[0], fc1_a, fc2_a, middle_a, n2_a, slope_a, active_a, between)
    attention_forward(
        between, vec.at[1], masks, qkv_w.at[1], pack.at[1, pl.ds(PROJ, WIDTH)],
        n1_b, qkv_b, probs_b, mixed_b, middle_b,
    )
    mlp_forward(vec.at[1], fc1_b, fc2_b, middle_b, n2_b, slope_b, active_b, result)
    mlp_backward(
        vec.at[1], fc1_b, fc2_b, middle_b, n2_b, slope_b, active_b, pack.at[1], dh, dmid, da,
        sums, make_emit(keep_out, send_out, core),
    )


def attention_backward_kernel(layer, *refs):
    (
        x, pack, vec, qkv_w, n1, qkv, probs, mixed, dmid, da, sums_in,
        dx, keep_out, send_out, dt, sums,
    ) = refs
    core = lax.axis_index("section")
    sums[...] = sums_in[...]
    attention_backward(
        x, vec.at[layer], qkv_w.at[layer], pack.at[layer, pl.ds(PROJ, WIDTH)], n1, qkv, probs,
        mixed, dmid, da, dt, sums, make_emit(keep_out, send_out, core), dx,
    )
    keep_out[2 * WIDTH :, :] = sums[...].astype(BF16)
    send_out[2 * WIDTH :, :] = sums[...].astype(BF16)


def last_backward_kernel(*refs):
    pack, result, rows_keep, rows_send, dx = refs[0], refs[10], refs[11], refs[12], refs[-1]
    attention_backward_kernel(0, pack.at[0], *refs[:10], dx, *refs[13:17])
    core = lax.axis_index("section")

    rows_keep[...] = jnp.where(core == 0, dx[...], result[...])
    rows_send[...] = jnp.where(core == 0, result[...], dx[...])


def mlp_backward_kernel(*refs):
    (
        _, vec, fc1_w, fc2_w, middle, n2, slope, active, dy,
        dmid, da, sums, keep_out, send_out, dh,
    ) = refs
    core = lax.axis_index("section")
    sums[...] = jnp.zeros_like(sums)
    mlp_backward(
        vec.at[0], fc1_w, fc2_w, middle, n2, slope, active, dy, dh, dmid, da, sums, make_emit(keep_out, send_out, core),
    )


def rows_kernel(vec, keep, recv, g_out, l_out, mark, wide, g, l, sem):
    mark[...] = jnp.zeros_like(mark)
    core = lax.axis_index("section")
    globals_live = []
    for source, half in ((keep, core), (recv, 1 - core)):
        wide[...] = source[...].astype(F32)
        live = jnp.where(core == 1, live_flag(vec.at[0], half), 1.0)
        globals_live.append(wide[:GT, :] * live)
        for j in range(LOCALS):
            crop = half * LOCALS + j
            live = jnp.where(core == 1, live_flag(vec.at[0], 2 + crop), 1.0)
            piece = wide[SEQ + j * SLOT : SEQ + j * SLOT + LT, :]
            l[crop] = (piece * live).astype(BF16)
    g[:, 0, :] = jnp.where(core == 0, *globals_live).astype(BF16)
    g[:, 1, :] = jnp.where(core == 1, *globals_live).astype(BF16)
    copies = [
        pltpu.make_async_copy(g, g_out, sem.at[0]),
        pltpu.make_async_copy(l, l_out, sem.at[1]),
    ]
    start_all(copies)
    wait_all(copies)


def out_block(own, got, index):
    core = lax.axis_index("section")
    place = index // 2
    rows = slice(place * WIDTH, (place + 1) * WIDTH)
    return jnp.where(core == index % 2, own[rows, :], got[rows, :]).astype(F32)


def write_blocks(own, got, places, held, sem):
    copies = []
    for i, place in enumerate(places):
        held[i] = out_block(own, got, i)
        copies.append(pltpu.make_async_copy(held.at[i], place, sem.at[i]))
        copies[-1].start()
    return copies


def mlp_out_kernel(own, got, fc1, fc2, mark, held, sem):
    mark[...] = jnp.zeros_like(mark)
    places = [fc2.at[0, column(part), :] for part in range(4)]
    places += [fc1.at[0, :, column(part)] for part in range(4)]
    wait_all(write_blocks(own, got, places, held, sem))


def attention_out_kernel(*refs):
    (
        own, got, sums_a, sums_b,
        ln1g, ln1b, qkv, qb, vb, proj, pb, ln2g, ln2b, fc1b, fc2b, held, sem,
    ) = refs
    places = [proj.at[0]] + [qkv.at[0, :, column(part)] for part in range(3)]
    copies = write_blocks(own, got, places, held, sem)
    core = lax.axis_index("section")
    sums = jnp.where(core == 0, sums_a[...], sums_b[...])
    for out, row in (
        (ln1g, LN1G), (ln1b, LN1B), (qb, QB), (vb, VB), (pb, PB), (ln2g, LN2G), (ln2b, LN2B),
        (fc2b, F2B),
    ):
        out[...] = sums[row : row + 1, :]
    for part in range(4):
        fc1b[:, column(part)] = sums[F1B + part : F1B + part + 1, :]
    wait_all(copies)


def shape(*dims, dtype=BF16):
    return jax.ShapeDtypeStruct(dims, dtype)


MARK = shape(8, 128, dtype=F32)


class Ordered:
    def __init__(self):
        self.last = None

    def __call__(
        self, name, kernel, outs, in_specs, out_specs, scratch=(), vmem=8, cost=1, mark=0
    ):
        before = [] if self.last is None else [self.last]
        count = len(in_specs)

        def body(*refs):
            kernel(*refs[:count], *refs[count + len(before) :])

        def run(*args):
            results = pl.pallas_call(
                body,
                out_shape=outs,
                name=name,
                in_specs=list(in_specs) + [ANY] * len(before),
                out_specs=out_specs,
                scratch_shapes=list(scratch),
                compiler_params=pltpu.CompilerParams(vmem_limit_bytes=int(vmem * 1024 * 1024)),
                cost_estimate=pl.CostEstimate(
                    flops=cost * COST, bytes_accessed=0, transcendentals=0
                ),
            )(*args, *before)
            self.last = results[mark]
            return results

        return run


CHUNK = 48


def add_rows(out, start_out, left, right, start, count):
    def step(i, carry):
        here = pl.ds(pl.multiple_of(start + i * CHUNK, 16), CHUNK)
        there = pl.ds(pl.multiple_of(start_out + i * CHUNK, 16), CHUNK)
        out[there, :] = (left[here, :].astype(F32) + right[here, :].astype(F32)).astype(BF16)
        return carry

    lax.fori_loop(0, count // CHUNK, step, 0, unroll=2)


def add_tail(outs, start_out, left, right, start):
    if left.shape[0] == start:
        return
    here = slice(start, start + VECS)
    tail = (left[here, :].astype(F32) + right[here, :].astype(F32)).astype(BF16)
    for out in outs:
        out[start_out : start_out + VECS, :] = tail


def bit_of(dims, step):
    dp = lax.axis_index("dp")
    core = lax.axis_index("section")
    return jnp.where(core == 0, dp >> dims[0][step] & 1, dp >> dims[1][step] & 1)


def halve_kernel(dims, step, count, keep, recv, keep_out, send_out):
    bit = bit_of(dims, step)
    half = count // 2
    add_rows(send_out, 0, keep, recv, (1 - bit) * half, half)
    add_rows(keep_out, 0, keep, recv, bit * half, half)
    add_tail((keep_out, send_out), half, keep, recv, count)


def sum_kernel(count, keep, recv, out):
    add_rows(out, 0, keep, recv, 0, count)
    add_tail((out,), count, keep, recv, count)


def total_kernel(count, own, recv, total_out, *sums_out):
    add_rows(total_out, 0, own, recv, 0, count)
    for out in sums_out:
        out[...] = own[count:, :].astype(F32) + recv[count:, :].astype(F32)


def join_rows(out, own, recv, bit):
    count = own.shape[0]
    for ref, half in ((own, bit), (recv, 1 - bit)):
        out[pl.ds(pl.multiple_of(half * count, 16), count), :] = ref[...]


def join_kernel(dims, step, own, recv, out):
    join_rows(out, own, recv, bit_of(dims, step))


def last_join_kernel(dims, own, recv, other, mine, send, whole):
    join_rows(whole, own, recv, bit_of(dims, 0))
    core = lax.axis_index("section")

    @pl.when(core == 0)
    def _():
        mine[...] = whole[...]
        send[...] = other[...]

    @pl.when(core == 1)
    def _():
        mine[...] = other[...]
        send[...] = whole[...]


def exchange(values_in, dims, step):
    pairs = [
        (core * 16 + dp, core * 16 + (dp ^ 1 << dims[core][step]))
        for core in range(2)
        for dp in range(16)
    ]
    return lax.ppermute(values_in, ("section", "dp"), pairs)


class Reduction:
    def __init__(self, name, call, dims, keep, send, count):
        self.name, self.call, self.dims = name, call, dims
        self.keep, self.recv, self.count = keep, swap(send), count
        self.steps = self.run(count, keep.shape[0] - count)

    def kernel(self, label, body, rows, *args):
        outs = [shape(n, WIDTH) for n in rows]
        return self.call(
            f"{self.name}_{label}", body, outs, [VMEM] * len(args), [VMEM] * len(outs)
        )(*args)

    def run(self, count, tail):
        keep, recv = self.keep, self.recv
        for step in range(3):
            body = functools.partial(halve_kernel, self.dims, step, count)
            count //= 2
            keep, send = self.kernel(f"halve{step}", body, [count + tail] * 2, keep, recv)
            recv = exchange(send, self.dims, step)
            yield
        body = functools.partial(sum_kernel, count)
        (own,) = self.kernel("sum", body, [count + tail], keep, recv)
        recv = exchange(own, self.dims, 3)
        yield
        whole, *sums = self.call(
            f"{self.name}_total",
            functools.partial(total_kernel, count),
            [shape(count, WIDTH)] + [shape(tail, WIDTH, dtype=F32)] * bool(tail),
            [VMEM] * 2,
            [VMEM] * (1 + bool(tail)),
        )(own, recv)
        self.sums = sums
        for step in (2, 1, 0):
            recv = exchange(whole, self.dims, step)
            self.pair = (whole, recv)
            yield
            if step:
                body = functools.partial(join_kernel, self.dims, step)
                (whole,) = self.kernel(f"join{step}", body, [2 * whole.shape[0]], whole, recv)

    def advance(self):
        next(self.steps)

    def last(self):
        assert 2 * self.pair[0].shape[0] == self.count
        body = functools.partial(join_kernel, self.dims, 0)
        (self.whole,) = self.kernel("join0", body, [self.count], *self.pair)

    def last_sorted(self, other):
        assert 2 * self.pair[0].shape[0] == self.count
        mine, send = self.call(
            f"{self.name}_last",
            functools.partial(last_join_kernel, self.dims),
            [shape(self.count, WIDTH)] * 2,
            [VMEM] * 3,
            [VMEM] * 2,
            [pltpu.VMEM((self.count, WIDTH), BF16)],
        )(*self.pair, other.whole)
        return mine, swap(send)


class PlainReduction(Reduction):
    def advance(self):
        pass

    def last(self):
        total = lax.psum(self.keep.astype(F32) + self.recv.astype(F32), "dp")
        self.whole = total[: self.count].astype(BF16)
        self.sums = [total[self.count :]] * (total.shape[0] > self.count)

    def last_sorted(self, other):
        self.last()
        leading = lax.axis_index("section") == 0
        pair = (self.whole, other.whole)
        return jnp.where(leading, *pair), swap(jnp.where(leading, *pair[::-1]))


def swap(values_in):
    return lax.ppermute(values_in, "section", [(0, 1), (1, 0)])


def on_device(dp_size, global_ends, local_ends, global_live, local_live, *weights):
    (
        ln1_gain, ln1_bias, qkv_weight, query_bias, value_bias, proj_weight, proj_bias,
        ln2_gain, ln2_bias, fc1_weight, fc1_bias, fc2_weight, fc2_bias,
    ) = weights
    qkv_own, fc1_own, fc2_own = (w[0] for w in (qkv_weight, fc1_weight, fc2_weight))
    qkv_got = swap(qkv_own)
    vectors = (
        ln1_gain, ln1_bias, query_bias, value_bias, proj_bias, ln2_gain, ln2_bias, fc2_bias,
        fc1_bias,
    )
    call = Ordered()
    packed = [global_ends[0].transpose(1, 0, 2), local_ends[0], proj_weight[0], *vectors]
    keep, send = call(
        "pack",
        pack_kernel,
        [shape(PACKED, WIDTH)] * 2,
        [ANY] * len(packed),
        [VMEM] * 2,
        [pltpu.VMEM(v.shape, BF16) for v in packed]
        + [
            pltpu.VMEM((ROWS, WIDTH), F32),
            pltpu.VMEM((VECS, WIDTH), F32),
            pltpu.SemaphoreType.DMA((len(packed),)),
        ],
        vmem=PACK_VMEM,
        cost=PACK_COST,
    )(*packed)
    recv = swap(send)
    fc1_own, fc2_own, _ = lax.optimization_barrier((fc1_own, fc2_own, send))
    fc1_got, fc2_got = swap(fc1_own), swap(fc2_own)
    rows_low, rows_wide = shape(ROWS, WIDTH), shape(ROWS, WIDTH, dtype=F32)
    hidden_low = shape(ROWS, FF)
    triple_low = shape(ROWS, 3 * WIDTH)
    weights_low = [shape(WIDTH, FF), shape(FF, WIDTH)]
    sums_shape = shape(VECS, WIDTH, dtype=F32)
    mlp_pair = [shape(4 * WIDTH, WIDTH)] * 2
    attention_pair = [shape(2 * WIDTH + VECS, WIDTH)] * 2
    attention_saved = [rows_low, triple_low, shape(12, SEQ, SEQ), rows_low]
    mlp_saved = [rows_wide, rows_low, hidden_low, hidden_low]
    masks_shape = shape(2, SEQ, SEQ, dtype=F32)
    masks, qkv_w = call(
        "settle",
        settle_kernel,
        [masks_shape, shape(2, WIDTH, 3 * WIDTH)],
        [VMEM] * 3,
        [VMEM] * 2,
    )(keep, qkv_own, qkv_got)
    outs = [shape(2, PACKED, WIDTH), shape(2, VECS, WIDTH, dtype=F32)]
    outs += attention_saved + [rows_wide]
    pack, vec, n1_a, qkv_a, probs_a, mixed_a, middle_a = call(
        "first_attention",
        first_attention_kernel,
        outs,
        [SMEM] * 2 + [VMEM] * 4,
        [VMEM] * len(outs),
        vmem=FIRST_VMEM,
        mark=1,
    )(global_live, local_live, keep, recv, qkv_w, masks)
    outs = weights_low + [rows_low] * 2 + mlp_saved[1:] + attention_saved
    outs += [rows_wide, rows_low, sums_shape] + mlp_pair
    (
        fc1_a, fc2_a, between, result, n2_a, slope_a, active_a,
        n1_b, qkv_b, probs_b, mixed_b, dmid, da, sums, keep_1, send_1,
    ) = call(
        "forward",
        forward_kernel,
        outs,
        [VMEM] * 9,
        [VMEM] * len(outs),
        [pltpu.VMEM(held.shape, held.dtype) for held in weights_low + mlp_saved]
        + [pltpu.VMEM((ROWS, FF), BF16)],
        vmem=KA_VMEM,
        mark=13,
    )(fc1_own, fc2_own, fc1_got, fc2_got, pack, qkv_w, vec, masks, middle_a)
    reduction = Reduction if dp_size == 16 else PlainReduction
    chains, held = {}, {}

    def begin(name, keep, send):
        count = PART_ROWS[name[1]]
        chains[name] = reduction(name, call, DIMS[name], keep, send, count)

    begin("bm", keep_1, send_1)
    wide_work = [pltpu.VMEM((ROWS, 3 * WIDTH), BF16), pltpu.VMEM((VECS, WIDTH), F32)]
    def back_b_attention():
        held["dx"], keep, send = call(
            "back_b_attention",
            functools.partial(attention_backward_kernel, 1),
            [rows_low] + attention_pair,
            [VMEM] * 11,
            [VMEM] * 3,
            wide_work,
            vmem=KB_VMEM,
        )(between, pack, vec, qkv_w, n1_b, qkv_b, probs_b, mixed_b, dmid, da, sums)
        begin("ba", keep, send)

    def back_a_mlp():
        *held["mlp"], keep, send = call(
            "back_a_mlp",
            mlp_backward_kernel,
            [rows_wide, rows_low, sums_shape] + mlp_pair,
            [VMEM] * 9,
            [VMEM] * 5,
            [pltpu.VMEM((ROWS, FF), BF16)],
            vmem=KB_VMEM,
        )(pack, vec, fc1_a, fc2_a, middle_a, n2_a, slope_a, active_a, held["dx"])
        begin("am", keep, send)

    def back_a_attention():
        held["rows"], rows_send, keep, send = call(
            "back_a_attention",
            last_backward_kernel,
            [rows_low] * 2 + attention_pair,
            [VMEM] * 11,
            [VMEM] * 4,
            wide_work + [pltpu.VMEM((ROWS, WIDTH), BF16)],
            vmem=KB_VMEM,
        )(pack, vec, qkv_w, n1_a, qkv_a, probs_a, mixed_a, *held["mlp"], result)
        begin("aa", keep, send)
        held["rows_got"] = swap(rows_send)

    def rows_out():
        ends = [shape(GT, global_ends.shape[1], WIDTH), shape(*local_ends.shape[1:])]
        held["rows_out"] = call(
            "rows_out",
            rows_kernel,
            ends + [MARK],
            [VMEM] * 3,
            [ANY] * 2 + [VMEM],
            [pltpu.VMEM((ROWS, WIDTH), F32)]
            + [pltpu.VMEM(end.shape, BF16) for end in ends]
            + [pltpu.SemaphoreType.DMA((2,))],
            vmem=ROWS_VMEM,
            mark=2,
        )(vec, held["rows"], held["rows_got"])

    def grad(w):
        return shape(*w.shape, dtype=F32)

    def last_sorted(part):
        held[part] = chains["a" + part].last_sorted(chains["b" + part])

    def mlp_out():
        held["mlp_out"] = call(
            "mlp_out",
            mlp_out_kernel,
            [grad(fc1_weight), grad(fc2_weight), MARK],
            [VMEM] * 2,
            [ANY] * 2 + [VMEM],
            [pltpu.VMEM((8, WIDTH, WIDTH), F32), pltpu.SemaphoreType.DMA((8,))],
            vmem=OUT_VMEM,
            mark=2,
        )(*held["m"])

    def attention_out():
        wanted = (
            ln1_gain, ln1_bias, qkv_weight, query_bias, value_bias, proj_weight,
            proj_bias, ln2_gain, ln2_bias, fc1_bias, fc2_bias,
        )
        held["attention_out"] = call(
            "attention_out",
            attention_out_kernel,
            [grad(w) for w in wanted],
            [VMEM] * 4,
            [ANY if w.ndim == 3 else VMEM for w in wanted],
            [pltpu.VMEM((4, WIDTH, WIDTH), F32), pltpu.SemaphoreType.DMA((4,))],
            vmem=LAST_VMEM,
        )(*held["a"], *chains["aa"].sums, *chains["ba"].sums)

    actions = {
        "b": back_b_attention, "c": back_a_mlp, "d": back_a_attention,
        "r": rows_out, "p": mlp_out, "q": attention_out,
        "w": lambda: chains["bm"].advance(), "x": lambda: chains["ba"].advance(),
        "y": lambda: chains["am"].advance(), "z": lambda: chains["aa"].advance(),
        "W": lambda: chains["bm"].last(), "X": lambda: chains["ba"].last(),
        "Y": lambda: last_sorted("m"), "Z": lambda: last_sorted("a"),
    }
    for name in ORDER:
        actions[name]()
    global_out, local_out, _ = held["rows_out"]
    grad_fc1, grad_fc2, _ = held["mlp_out"]
    (
        grad_ln1_gain, grad_ln1_bias, grad_qkv, grad_query_bias, grad_value_bias, grad_proj,
        grad_proj_bias, grad_ln2_gain, grad_ln2_bias, grad_fc1_bias, grad_fc2_bias,
    ) = held["attention_out"]
    return (
        global_out.transpose(1, 0, 2)[None], local_out[None],
        grad_ln1_gain, grad_ln1_bias, grad_qkv, grad_query_bias, grad_value_bias, grad_proj,
        grad_proj_bias, grad_ln2_gain, grad_ln2_bias, grad_fc1, grad_fc1_bias, grad_fc2,
        grad_fc2_bias,
    )


def solution(mesh):
    matrix, vector = P("section", None, None), P("section", None)
    weights = (
        vector, vector, matrix, vector, vector, matrix, vector,
        vector, vector, matrix, vector, matrix, vector,
    )
    rows = P("section", "dp", None, None)
    return jax.shard_map(
        functools.partial(on_device, mesh.shape["dp"]),
        mesh=mesh,
        in_specs=(rows, rows, P("dp"), P("dp")) + weights,
        out_specs=(rows, rows) + weights,
        check_vma=False,
    )
```

```python
import functools

import jax
import jax.numpy as jnp
from jax import lax
from jax.experimental import pallas as pl
from jax.experimental.pallas import tpu as pltpu
from jax.sharding import PartitionSpec as P

HEAD = 64
GT = 197
LT = 37
WIDTH = 384
FF = 1536
SEQ = 208
ROWS = 2 * SEQ
SLOT = 40
LOCALS = 5
VECS = 16
EPSILON = 1e-06
MASKED = -1e30
CHUNK_FF = 768
ORDER = "bcwxydwzxywwxzywyzwyxwzxyzWxzyxzrYXZpq"
DIMS = {
    "bm": ((0, 1, 2, 3), (1, 2, 0, 3)),
    "ba": ((1, 2, 0, 3), (2, 1, 0, 3)),
    "am": ((0, 2, 1, 3), (2, 1, 0, 3)),
    "aa": ((0, 1, 2, 3), (1, 2, 0, 3)),
}
PART_ROWS = {"m": 4 * WIDTH, "a": 2 * WIDTH}
COST = 26214400000
PACK_COST = 10
COSTS = {"bm_halve1": 0.5, "bm_sum": 0.001, "aa_halve0": 0.013, "ba_halve1": 0.002, "bm_halve2": 0.006, "back_a_attention": 0.5, "am_halve1": 0.005, "ba_halve2": 0.001, "aa_halve1": 0.5, "am_halve2": 0.025, "bm_total": 0.125, "am_sum": 0.5, "aa_halve2": 0.125, "bm_join2": 0.125, "am_total": 0.25, "ba_sum": 0.125, "bm_join1": 0.25, "aa_sum": 0.062, "ba_total": 0.02, "am_join2": 0.125, "aa_total": 0.1, "bm_join0": 0.125, "ba_join2": 0.125, "aa_join2": 0.125, "am_join1": 0.25, "ba_join1": 0.013, "aa_join1": 0.125, "back_b_attention": 0.5}
PACK_VMEM = 55
FIRST_VMEM = 8
KA_VMEM = 16
OUT_VMEM = 8
ROWS_VMEM = 8
LAST_VMEM = 8
KB_VMEM = 12
LN1G, LN1B, QB, VB, PB, LN2G, LN2B, F2B, F1B = range(9)
LIVE = 12
PROJ = ROWS + VECS
PACKED = PROJ + WIDTH
BF16 = jnp.bfloat16
F32 = jnp.float32
ANY = pl.BlockSpec(memory_space=pl.ANY)
VMEM = pl.BlockSpec(memory_space=pltpu.VMEM)
SMEM = pl.BlockSpec(memory_space=pltpu.SMEM)


def mm(left, right):
    return jnp.dot(left, right, preferred_element_type=F32)


def mm_right_t(left, right):
    return lax.dot_general(left, right, (((1,), (1,)), ((), ())), preferred_element_type=F32)


def mm_left_t(left, right):
    return lax.dot_general(left, right, (((0,), (0,)), ((), ())), preferred_element_type=F32)


def normalise(values_in):
    centred = values_in - jnp.mean(values_in, axis=-1, keepdims=True)
    scale = lax.rsqrt(jnp.mean(centred * centred, axis=-1, keepdims=True) + EPSILON)
    return centred * scale, scale


def normalise_back(unit, scale, grad_rows, gain):
    e = grad_rows * gain
    return scale * (
        e
        - jnp.mean(e, axis=-1, keepdims=True)
        - unit * jnp.mean(e * unit, axis=-1, keepdims=True)
    )


def seq_rows(seq):
    return pl.ds(pl.multiple_of(seq * SEQ, 16), SEQ)


def column(block):
    return slice(block * WIDTH, (block + 1) * WIDTH)


def wide(part):
    return slice(part * CHUNK_FF, (part + 1) * CHUNK_FF)


def row_sum(values_in):
    return jnp.sum(values_in, axis=0, keepdims=True)


def live_flag(vec, index):
    lane = lax.broadcasted_iota(jnp.int32, (1, WIDTH), 1)
    flags = vec[LIVE : LIVE + 1, :]
    return jnp.sum(jnp.where(lane == index, flags, 0.0), axis=1, keepdims=True)


def pack_kernel(*refs):
    sources, (keep, send), held = refs[:12], refs[12:14], refs[14:26]
    rows, tail, sem = refs[26:]
    g, l, proj, vecs = held[0], held[1], held[2], held[3:]
    copies = [
        pltpu.make_async_copy(source, place, sem.at[i])
        for i, (source, place) in enumerate(zip(sources, held))
    ]
    start_all(copies)
    core = lax.axis_index("section")
    rows[...] = jnp.zeros_like(rows)
    tail[...] = jnp.zeros_like(tail)
    wait_all(copies)
    for i, vec in enumerate(vecs[:8]):
        tail[i : i + 1, :] = vec[...].astype(F32)
    for i in range(FF // WIDTH):
        tail[F1B + i : F1B + i + 1, :] = vecs[8][:, column(i)].astype(F32)
    crops = g[...].astype(F32)
    for out, half in ((keep, core), (send, 1 - core)):
        rows[:GT, :] = jnp.where(half == 0, crops[:, 0, :], crops[:, 1, :])
        for j in range(LOCALS):
            rows[SEQ + j * SLOT : SEQ + j * SLOT + LT, :] = l[half * LOCALS + j].astype(F32)
        out[:ROWS, :] = rows[...].astype(BF16)
        out[ROWS:PROJ, :] = tail[...].astype(BF16)
        out[PROJ:, :] = proj[...]


def crop_of(axis):
    dims = (SEQ, 1) if axis == 0 else (1, SEQ)
    row = lax.broadcasted_iota(jnp.int32, dims, axis)
    crop = jnp.zeros(dims, jnp.int32)
    for j in range(1, LOCALS + 1):
        crop += (row >= j * SLOT).astype(jnp.int32)
    return crop, (crop < LOCALS) & (row - crop * SLOT < LT)


def head_lanes():
    lane = lax.broadcasted_iota(jnp.int32, (SEQ, 2 * HEAD), 1)
    return (lane < HEAD, lane >= HEAD)


def only(mask, values_in):
    return jnp.where(mask, values_in, jnp.zeros_like(values_in))


def attention_forward(x, vec, masks, qkv_w, proj_w, n1, qkv, probs, mixed, middle):
    def body(seq, carry):
        rows = seq_rows(seq)
        x_rows = x[rows, :].astype(F32)
        unit, _ = normalise(x_rows)
        normed = (unit * vec[LN1G : LN1G + 1, :] + vec[LN1B : LN1B + 1, :]).astype(BF16)
        n1[rows, :] = normed
        triple = mm(normed, qkv_w[...])
        query = (triple[:, :WIDTH] + vec[QB : QB + 1, :]).astype(BF16) * BF16(HEAD**-0.5)
        qkv[rows, :WIDTH] = query
        qkv[rows, column(1)] = triple[:, column(1)].astype(BF16)
        qkv[rows, column(2)] = (triple[:, column(2)] + vec[VB : VB + 1, :]).astype(BF16)
        lanes = head_lanes()
        mask = masks[seq]
        for pair in range(3):
            q = qkv[rows, pair * 128 : pair * 128 + 128]
            k = qkv[rows, WIDTH + pair * 128 : WIDTH + pair * 128 + 128]
            v = qkv[rows, 2 * WIDTH + pair * 128 : 2 * WIDTH + pair * 128 + 128]
            total = None
            for a in range(2):
                s = mm_right_t(only(lanes[a], k), q) + mask
                e = jnp.exp(s - jnp.max(s, axis=0, keepdims=True))
                p = (e * (1.0 / jnp.sum(e, axis=0, keepdims=True))).astype(BF16)
                probs[seq * 6 + pair * 2 + a] = p
                part = mm_left_t(p, only(lanes[a], v))
                total = part if total is None else total + part
            mixed[rows, pair * 128 : pair * 128 + 128] = total.astype(BF16)
        middle[rows, :] = x_rows + (mm(mixed[rows, :], proj_w[...]) + vec[PB : PB + 1, :])
        return carry

    lax.fori_loop(0, 2, body, 0, unroll=True)


def wide_bias(vec, part):
    rows = CHUNK_FF // 128
    pieces = []
    for i in range(part * rows, (part + 1) * rows):
        row, lane = F1B + i * 128 // WIDTH, i * 128 % WIDTH
        pieces.append(vec[row : row + 1, lane : lane + 128])
    return jnp.concatenate(pieces, axis=1)


def mlp_forward(vec, fc1_w, fc2_w, middle, n2, slope, active, result):
    def body(seq, carry):
        rows = seq_rows(seq)
        unit, _ = normalise(middle[rows, :])
        normed = (unit * vec[LN2G : LN2G + 1, :] + vec[LN2B : LN2B + 1, :]).astype(BF16)
        n2[rows, :] = normed
        for part in range(FF // CHUNK_FF):
            hidden = mm(normed, fc1_w[:, wide(part)]) + wide_bias(vec, part)
            cdf = 0.5 + 0.5 * lax.erf(hidden * (0.5**0.5))
            active[rows, wide(part)] = (hidden * cdf).astype(BF16)
            density = jnp.exp(hidden * hidden * -0.5) * 0.3989422804014327
            slope[rows, wide(part)] = (cdf + hidden * density).astype(BF16)
        y = middle[rows, :] + (mm(active[rows, :], fc2_w[...]) + vec[F2B : F2B + 1, :])
        result[rows, :] = y.astype(BF16)
        return carry

    lax.fori_loop(0, 2, body, 0, unroll=True)


def mlp_backward(vec, fc1_w, fc2_w, middle, n2, slope, active, dy, dh, dmid, da, sums, emit):
    def body(seq, carry):
        rows = seq_rows(seq)
        dy_rows = dy[rows, :]
        for part in range(FF // WIDTH):
            dactive = mm_right_t(dy_rows, fc2_w[column(part), :])
            low = (slope[rows, column(part)].astype(F32) * dactive).astype(BF16)
            dh[rows, column(part)] = low
            sums[F1B + part : F1B + part + 1, :] += row_sum(low.astype(F32))
        dn2 = mm_right_t(dh[rows, :], fc1_w[...])
        unit, scale = normalise(middle[rows, :])
        dy_wide = dy_rows.astype(F32)
        grad = dy_wide + normalise_back(unit, scale, dn2, vec[LN2G : LN2G + 1, :])
        dmid[rows, :] = grad
        low = grad.astype(BF16)
        da[rows, :] = low
        sums[LN2G : LN2G + 1, :] += row_sum(dn2 * unit)
        sums[LN2B : LN2B + 1, :] += row_sum(dn2)
        sums[F2B : F2B + 1, :] += row_sum(dy_wide)
        sums[PB : PB + 1, :] += row_sum(low.astype(F32))
        return carry

    lax.fori_loop(0, 2, body, 0, unroll=True)
    for pair in range(2):
        parts = (column(2 * pair), column(2 * pair + 1))
        emit(pair, *(mm_left_t(active[:, part], dy[:ROWS, :]) for part in parts))
    for part in range(2):
        value = mm_left_t(n2[...], dh[:, part * 2 * WIDTH : (part + 1) * 2 * WIDTH])
        emit(2 + part, value[:, :WIDTH], value[:, WIDTH:])


def attention_backward(
    x, vec, qkv_w, proj_w, n1, qkv, probs, mixed, dmid, da, dt, sums, emit, result
):
    def body(seq, carry):
        rows = seq_rows(seq)
        dmixed = mm_right_t(da[rows, :], proj_w[...]).astype(BF16)
        lanes = head_lanes()
        for pair in range(3):
            q = qkv[rows, pair * 128 : pair * 128 + 128]
            k = qkv[rows, WIDTH + pair * 128 : WIDTH + pair * 128 + 128]
            v = qkv[rows, 2 * WIDTH + pair * 128 : 2 * WIDTH + pair * 128 + 128]
            dm = dmixed[:, pair * 128 : pair * 128 + 128]
            dq = dk = dv = None
            for a in range(2):
                dm_a = only(lanes[a], dm)
                p = probs[seq * 6 + pair * 2 + a]
                dp = mm_right_t(only(lanes[a], v), dm)
                p_wide = p.astype(F32)
                ds = p_wide * (dp - jnp.sum(dp * p_wide, axis=0, keepdims=True))
                ds = ds.astype(BF16)
                parts = (
                    mm_left_t(ds, only(lanes[a], k)),
                    mm(ds, only(lanes[a], q)),
                    mm(p, dm_a),
                )
                if a == 0:
                    dq, dk, dv = parts
                else:
                    dq, dk, dv = dq + parts[0], dk + parts[1], dv + parts[2]
            dq = (dq * HEAD**-0.5).astype(BF16)
            dv = dv.astype(BF16)
            here = slice(pair * 128, pair * 128 + 128)
            dt[rows, pair * 128 : pair * 128 + 128] = dq
            dt[rows, WIDTH + pair * 128 : WIDTH + pair * 128 + 128] = dk.astype(BF16)
            dt[rows, 2 * WIDTH + pair * 128 : 2 * WIDTH + pair * 128 + 128] = dv
            sums[QB : QB + 1, here] += row_sum(dq.astype(F32))
            sums[VB : VB + 1, here] += row_sum(dv.astype(F32))
        dn1 = mm_right_t(dt[rows, :], qkv_w[...])
        unit, scale = normalise(x[rows, :].astype(F32))
        grad = dmid[rows, :] + normalise_back(unit, scale, dn1, vec[LN1G : LN1G + 1, :])
        result[rows, :] = grad.astype(BF16)
        sums[LN1G : LN1G + 1, :] += row_sum(dn1 * unit)
        sums[LN1B : LN1B + 1, :] += row_sum(dn1)
        return carry

    lax.fori_loop(0, 2, body, 0, unroll=True)
    value = mm_left_t(n1[...], dt[...])
    emit(0, mm_left_t(mixed[...], da[...]), value[:, column(0)])
    emit(1, value[:, column(1)], value[:, column(2)])


def make_emit(keep, send, core):
    def emit(pair, first, second):
        rows = slice(pair * WIDTH, (pair + 1) * WIDTH)
        first, second = first.astype(BF16), second.astype(BF16)
        keep[rows, :] = jnp.where(core == 0, first, second)
        send[rows, :] = jnp.where(core == 0, second, first)

    return emit


def start_all(copies):
    for copy in copies:
        copy.start()


def wait_all(copies):
    for copy in copies:
        copy.wait()


def hold_flags(glive, llive, vec, dy):
    core = lax.axis_index("section")
    lane = lax.broadcasted_iota(jnp.int32, (1, WIDTH), 1)
    flags = jnp.zeros((1, WIDTH), F32)
    for i in range(2):
        flags = jnp.where(lane == i, glive[i].astype(F32), flags)
    for i in range(2 * LOCALS):
        flags = jnp.where(lane == 2 + i, llive[i].astype(F32), flags)
    vec[LIVE : LIVE + 1, :] = flags
    crop, _ = crop_of(0)
    live = jnp.zeros((SEQ, 1), F32)
    for j in range(LOCALS):
        live = jnp.where(crop == j, llive[core * LOCALS + j].astype(F32), live)
    dy[:SEQ, :] = (dy[:SEQ, :].astype(F32) * glive[core].astype(F32)).astype(BF16)
    dy[SEQ:ROWS, :] = (dy[SEQ:ROWS, :].astype(F32) * live).astype(BF16)


def sort_by_core(own, got, first, second):
    core = lax.axis_index("section")
    first[...] = jnp.where(core == 0, own[...], got[...])
    second[...] = jnp.where(core == 0, got[...], own[...])


def settle_kernel(_, own, got, masks, qkv_w):
    key = lax.broadcasted_iota(jnp.int32, (SEQ, SEQ), 0)
    masks[0] = jnp.where(key < GT, 0.0, MASKED)
    key_crop, true_key = crop_of(0)
    query_crop, _ = crop_of(1)
    masks[1] = jnp.where(jnp.where(true_key, key_crop, -1) == query_crop, 0.0, MASKED)
    sort_by_core(own, got, qkv_w.at[0], qkv_w.at[1])


def first_attention_kernel(*refs):
    (
        glive, llive, keep, recv, qkv_w, masks,
        pack, vec, n1, qkv, probs, mixed, middle,
    ) = refs
    sort_by_core(keep, recv, pack.at[0], pack.at[1])
    for layer in range(2):
        vec[layer] = pack[layer, ROWS:PROJ, :].astype(F32)
    hold_flags(glive, llive, vec.at[0], pack.at[1])
    attention_forward(
        pack.at[0], vec.at[0], masks, qkv_w.at[0], pack.at[0, pl.ds(PROJ, WIDTH)],
        n1, qkv, probs, mixed, middle,
    )


def forward_kernel(*refs):
    (
        fc1_own, fc2_own, fc1_got, fc2_got, pack, qkv_w, vec, masks, middle_a,
        fc1_a, fc2_a, between, result, n2_a, slope_a, active_a,
        n1_b, qkv_b, probs_b, mixed_b, dmid, da, sums, keep_out, send_out,
        fc1_b, fc2_b, middle_b, n2_b, slope_b, active_b, dh,
    ) = refs
    core = lax.axis_index("section")
    sort_by_core(fc1_own, fc1_got, fc1_a, fc1_b)
    sort_by_core(fc2_own, fc2_got, fc2_a, fc2_b)
    sums[...] = jnp.zeros_like(sums)
    mlp_forward(vec.at[0], fc1_a, fc2_a, middle_a, n2_a, slope_a, active_a, between)
    attention_forward(
        between, vec.at[1], masks, qkv_w.at[1], pack.at[1, pl.ds(PROJ, WIDTH)],
        n1_b, qkv_b, probs_b, mixed_b, middle_b,
    )
    mlp_forward(vec.at[1], fc1_b, fc2_b, middle_b, n2_b, slope_b, active_b, result)
    mlp_backward(
        vec.at[1], fc1_b, fc2_b, middle_b, n2_b, slope_b, active_b, pack.at[1], dh, dmid, da,
        sums, make_emit(keep_out, send_out, core),
    )


def attention_backward_kernel(layer, *refs):
    (
        x, pack, vec, qkv_w, n1, qkv, probs, mixed, dmid, da, sums_in,
        dx, keep_out, send_out, dt, sums,
    ) = refs
    core = lax.axis_index("section")
    sums[...] = sums_in[...]
    attention_backward(
        x, vec.at[layer], qkv_w.at[layer], pack.at[layer, pl.ds(PROJ, WIDTH)], n1, qkv, probs,
        mixed, dmid, da, dt, sums, make_emit(keep_out, send_out, core), dx,
    )
    keep_out[2 * WIDTH :, :] = sums[...].astype(BF16)
    send_out[2 * WIDTH :, :] = sums[...].astype(BF16)


def last_backward_kernel(*refs):
    pack, result, rows_keep, rows_send, dx = refs[0], refs[10], refs[11], refs[12], refs[-1]
    attention_backward_kernel(0, pack.at[0], *refs[:10], dx, *refs[13:17])
    core = lax.axis_index("section")

    rows_keep[...] = jnp.where(core == 0, dx[...], result[...])
    rows_send[...] = jnp.where(core == 0, result[...], dx[...])


def mlp_backward_kernel(*refs):
    (
        _, vec, fc1_w, fc2_w, middle, n2, slope, active, dy,
        dmid, da, sums, keep_out, send_out, dh,
    ) = refs
    core = lax.axis_index("section")
    sums[...] = jnp.zeros_like(sums)
    mlp_backward(
        vec.at[0], fc1_w, fc2_w, middle, n2, slope, active, dy, dh, dmid, da, sums, make_emit(keep_out, send_out, core),
    )


def rows_kernel(vec, keep, recv, g_out, l_out, mark, wide, g, l, sem):
    mark[...] = jnp.zeros_like(mark)
    core = lax.axis_index("section")
    globals_live = []
    for source, half in ((keep, core), (recv, 1 - core)):
        wide[...] = source[...].astype(F32)
        live = jnp.where(core == 1, live_flag(vec.at[0], half), 1.0)
        globals_live.append(wide[:GT, :] * live)
        for j in range(LOCALS):
            crop = half * LOCALS + j
            live = jnp.where(core == 1, live_flag(vec.at[0], 2 + crop), 1.0)
            piece = wide[SEQ + j * SLOT : SEQ + j * SLOT + LT, :]
            l[crop] = (piece * live).astype(BF16)
    g[:, 0, :] = jnp.where(core == 0, *globals_live).astype(BF16)
    g[:, 1, :] = jnp.where(core == 1, *globals_live).astype(BF16)
    copies = [
        pltpu.make_async_copy(g, g_out, sem.at[0]),
        pltpu.make_async_copy(l, l_out, sem.at[1]),
    ]
    start_all(copies)
    wait_all(copies)


def out_block(own, got, index):
    core = lax.axis_index("section")
    place = index // 2
    rows = slice(place * WIDTH, (place + 1) * WIDTH)
    return jnp.where(core == index % 2, own[rows, :], got[rows, :]).astype(F32)


def write_blocks(own, got, places, held, sem):
    copies = []
    for i, place in enumerate(places):
        held[i] = out_block(own, got, i)
        copies.append(pltpu.make_async_copy(held.at[i], place, sem.at[i]))
        copies[-1].start()
    return copies


def mlp_out_kernel(own, got, fc1, fc2, mark, held, sem):
    mark[...] = jnp.zeros_like(mark)
    places = [fc2.at[0, column(part), :] for part in range(4)]
    places += [fc1.at[0, :, column(part)] for part in range(4)]
    wait_all(write_blocks(own, got, places, held, sem))


def attention_out_kernel(*refs):
    (
        own, got, sums_a, sums_b,
        ln1g, ln1b, qkv, qb, vb, proj, pb, ln2g, ln2b, fc1b, fc2b, held, sem,
    ) = refs
    places = [proj.at[0]] + [qkv.at[0, :, column(part)] for part in range(3)]
    copies = write_blocks(own, got, places, held, sem)
    core = lax.axis_index("section")
    sums = jnp.where(core == 0, sums_a[...], sums_b[...])
    for out, row in (
        (ln1g, LN1G), (ln1b, LN1B), (qb, QB), (vb, VB), (pb, PB), (ln2g, LN2G), (ln2b, LN2B),
        (fc2b, F2B),
    ):
        out[...] = sums[row : row + 1, :]
    for part in range(4):
        fc1b[:, column(part)] = sums[F1B + part : F1B + part + 1, :]
    wait_all(copies)


def shape(*dims, dtype=BF16):
    return jax.ShapeDtypeStruct(dims, dtype)


MARK = shape(8, 128, dtype=F32)


class Ordered:
    def __init__(self):
        self.last = None

    def __call__(
        self, name, kernel, outs, in_specs, out_specs, scratch=(), vmem=8, cost=1, mark=0
    ):
        before = [] if self.last is None else [self.last]
        count = len(in_specs)

        def body(*refs):
            kernel(*refs[:count], *refs[count + len(before) :])

        def run(*args):
            results = pl.pallas_call(
                body,
                out_shape=outs,
                name=name,
                in_specs=list(in_specs) + [ANY] * len(before),
                out_specs=out_specs,
                scratch_shapes=list(scratch),
                compiler_params=pltpu.CompilerParams(vmem_limit_bytes=int(vmem * 1024 * 1024)),
                cost_estimate=pl.CostEstimate(
                    flops=int(COSTS.get(name, cost) * COST),
                    bytes_accessed=0,
                    transcendentals=0,
                ),
            )(*args, *before)
            self.last = results[mark]
            return results

        return run


CHUNK = 48


def add_rows(out, start_out, left, right, start, count):
    def step(i, carry):
        here = pl.ds(pl.multiple_of(start + i * CHUNK, 16), CHUNK)
        there = pl.ds(pl.multiple_of(start_out + i * CHUNK, 16), CHUNK)
        out[there, :] = (left[here, :].astype(F32) + right[here, :].astype(F32)).astype(BF16)
        return carry

    lax.fori_loop(0, count // CHUNK, step, 0, unroll=2)


def add_tail(outs, start_out, left, right, start):
    if left.shape[0] == start:
        return
    here = slice(start, start + VECS)
    tail = (left[here, :].astype(F32) + right[here, :].astype(F32)).astype(BF16)
    for out in outs:
        out[start_out : start_out + VECS, :] = tail


def bit_of(dims, step):
    dp = lax.axis_index("dp")
    core = lax.axis_index("section")
    return jnp.where(core == 0, dp >> dims[0][step] & 1, dp >> dims[1][step] & 1)


def halve_kernel(dims, step, count, keep, recv, keep_out, send_out):
    bit = bit_of(dims, step)
    half = count // 2
    add_rows(send_out, 0, keep, recv, (1 - bit) * half, half)
    add_rows(keep_out, 0, keep, recv, bit * half, half)
    add_tail((keep_out, send_out), half, keep, recv, count)


def sum_kernel(count, keep, recv, out):
    add_rows(out, 0, keep, recv, 0, count)
    add_tail((out,), count, keep, recv, count)


def total_kernel(count, own, recv, total_out, *sums_out):
    add_rows(total_out, 0, own, recv, 0, count)
    for out in sums_out:
        out[...] = own[count:, :].astype(F32) + recv[count:, :].astype(F32)


def join_rows(out, own, recv, bit):
    count = own.shape[0]
    for ref, half in ((own, bit), (recv, 1 - bit)):
        out[pl.ds(pl.multiple_of(half * count, 16), count), :] = ref[...]


def join_kernel(dims, step, own, recv, out):
    join_rows(out, own, recv, bit_of(dims, step))


def last_join_kernel(dims, own, recv, other, mine, send, whole):
    join_rows(whole, own, recv, bit_of(dims, 0))
    core = lax.axis_index("section")

    @pl.when(core == 0)
    def _():
        mine[...] = whole[...]
        send[...] = other[...]

    @pl.when(core == 1)
    def _():
        mine[...] = other[...]
        send[...] = whole[...]


def exchange(values_in, dims, step):
    pairs = [
        (core * 16 + dp, core * 16 + (dp ^ 1 << dims[core][step]))
        for core in range(2)
        for dp in range(16)
    ]
    return lax.ppermute(values_in, ("section", "dp"), pairs)


class Reduction:
    def __init__(self, name, call, dims, keep, send, count):
        self.name, self.call, self.dims = name, call, dims
        self.keep, self.recv, self.count = keep, swap(send), count
        self.steps = self.run(count, keep.shape[0] - count)

    def kernel(self, label, body, rows, *args):
        outs = [shape(n, WIDTH) for n in rows]
        return self.call(
            f"{self.name}_{label}", body, outs, [VMEM] * len(args), [VMEM] * len(outs)
        )(*args)

    def run(self, count, tail):
        keep, recv = self.keep, self.recv
        for step in range(3):
            body = functools.partial(halve_kernel, self.dims, step, count)
            count //= 2
            keep, send = self.kernel(f"halve{step}", body, [count + tail] * 2, keep, recv)
            recv = exchange(send, self.dims, step)
            yield
        body = functools.partial(sum_kernel, count)
        (own,) = self.kernel("sum", body, [count + tail], keep, recv)
        recv = exchange(own, self.dims, 3)
        yield
        whole, *sums = self.call(
            f"{self.name}_total",
            functools.partial(total_kernel, count),
            [shape(count, WIDTH)] + [shape(tail, WIDTH, dtype=F32)] * bool(tail),
            [VMEM] * 2,
            [VMEM] * (1 + bool(tail)),
        )(own, recv)
        self.sums = sums
        for step in (2, 1, 0):
            recv = exchange(whole, self.dims, step)
            self.pair = (whole, recv)
            yield
            if step:
                body = functools.partial(join_kernel, self.dims, step)
                (whole,) = self.kernel(f"join{step}", body, [2 * whole.shape[0]], whole, recv)

    def advance(self):
        next(self.steps)

    def last(self):
        assert 2 * self.pair[0].shape[0] == self.count
        body = functools.partial(join_kernel, self.dims, 0)
        (self.whole,) = self.kernel("join0", body, [self.count], *self.pair)

    def last_sorted(self, other):
        assert 2 * self.pair[0].shape[0] == self.count
        mine, send = self.call(
            f"{self.name}_last",
            functools.partial(last_join_kernel, self.dims),
            [shape(self.count, WIDTH)] * 2,
            [VMEM] * 3,
            [VMEM] * 2,
            [pltpu.VMEM((self.count, WIDTH), BF16)],
        )(*self.pair, other.whole)
        return mine, swap(send)


class PlainReduction(Reduction):
    def advance(self):
        pass

    def last(self):
        total = lax.psum(self.keep.astype(F32) + self.recv.astype(F32), "dp")
        self.whole = total[: self.count].astype(BF16)
        self.sums = [total[self.count :]] * (total.shape[0] > self.count)

    def last_sorted(self, other):
        self.last()
        leading = lax.axis_index("section") == 0
        pair = (self.whole, other.whole)
        return jnp.where(leading, *pair), swap(jnp.where(leading, *pair[::-1]))


def swap(values_in):
    return lax.ppermute(values_in, "section", [(0, 1), (1, 0)])


def on_device(dp_size, global_ends, local_ends, global_live, local_live, *weights):
    (
        ln1_gain, ln1_bias, qkv_weight, query_bias, value_bias, proj_weight, proj_bias,
        ln2_gain, ln2_bias, fc1_weight, fc1_bias, fc2_weight, fc2_bias,
    ) = weights
    qkv_own, fc1_own, fc2_own = (w[0] for w in (qkv_weight, fc1_weight, fc2_weight))
    qkv_got = swap(qkv_own)
    vectors = (
        ln1_gain, ln1_bias, query_bias, value_bias, proj_bias, ln2_gain, ln2_bias, fc2_bias,
        fc1_bias,
    )
    call = Ordered()
    packed = [global_ends[0].transpose(1, 0, 2), local_ends[0], proj_weight[0], *vectors]
    keep, send = call(
        "pack",
        pack_kernel,
        [shape(PACKED, WIDTH)] * 2,
        [ANY] * len(packed),
        [VMEM] * 2,
        [pltpu.VMEM(v.shape, BF16) for v in packed]
        + [
            pltpu.VMEM((ROWS, WIDTH), F32),
            pltpu.VMEM((VECS, WIDTH), F32),
            pltpu.SemaphoreType.DMA((len(packed),)),
        ],
        vmem=PACK_VMEM,
        cost=PACK_COST,
    )(*packed)
    recv = swap(send)
    fc1_own, fc2_own, _ = lax.optimization_barrier((fc1_own, fc2_own, send))
    fc1_got, fc2_got = swap(fc1_own), swap(fc2_own)
    rows_low, rows_wide = shape(ROWS, WIDTH), shape(ROWS, WIDTH, dtype=F32)
    hidden_low = shape(ROWS, FF)
    triple_low = shape(ROWS, 3 * WIDTH)
    weights_low = [shape(WIDTH, FF), shape(FF, WIDTH)]
    sums_shape = shape(VECS, WIDTH, dtype=F32)
    mlp_pair = [shape(4 * WIDTH, WIDTH)] * 2
    attention_pair = [shape(2 * WIDTH + VECS, WIDTH)] * 2
    attention_saved = [rows_low, triple_low, shape(12, SEQ, SEQ), rows_low]
    mlp_saved = [rows_wide, rows_low, hidden_low, hidden_low]
    masks_shape = shape(2, SEQ, SEQ, dtype=F32)
    masks, qkv_w = call(
        "settle",
        settle_kernel,
        [masks_shape, shape(2, WIDTH, 3 * WIDTH)],
        [VMEM] * 3,
        [VMEM] * 2,
    )(keep, qkv_own, qkv_got)
    outs = [shape(2, PACKED, WIDTH), shape(2, VECS, WIDTH, dtype=F32)]
    outs += attention_saved + [rows_wide]
    pack, vec, n1_a, qkv_a, probs_a, mixed_a, middle_a = call(
        "first_attention",
        first_attention_kernel,
        outs,
        [SMEM] * 2 + [VMEM] * 4,
        [VMEM] * len(outs),
        vmem=FIRST_VMEM,
        mark=1,
    )(global_live, local_live, keep, recv, qkv_w, masks)
    outs = weights_low + [rows_low] * 2 + mlp_saved[1:] + attention_saved
    outs += [rows_wide, rows_low, sums_shape] + mlp_pair
    (
        fc1_a, fc2_a, between, result, n2_a, slope_a, active_a,
        n1_b, qkv_b, probs_b, mixed_b, dmid, da, sums, keep_1, send_1,
    ) = call(
        "forward",
        forward_kernel,
        outs,
        [VMEM] * 9,
        [VMEM] * len(outs),
        [pltpu.VMEM(held.shape, held.dtype) for held in weights_low + mlp_saved]
        + [pltpu.VMEM((ROWS, FF), BF16)],
        vmem=KA_VMEM,
        mark=13,
    )(fc1_own, fc2_own, fc1_got, fc2_got, pack, qkv_w, vec, masks, middle_a)
    reduction = Reduction if dp_size == 16 else PlainReduction
    chains, held = {}, {}

    def begin(name, keep, send):
        count = PART_ROWS[name[1]]
        chains[name] = reduction(name, call, DIMS[name], keep, send, count)

    begin("bm", keep_1, send_1)
    wide_work = [pltpu.VMEM((ROWS, 3 * WIDTH), BF16), pltpu.VMEM((VECS, WIDTH), F32)]
    def back_b_attention():
        held["dx"], keep, send = call(
            "back_b_attention",
            functools.partial(attention_backward_kernel, 1),
            [rows_low] + attention_pair,
            [VMEM] * 11,
            [VMEM] * 3,
            wide_work,
            vmem=KB_VMEM,
        )(between, pack, vec, qkv_w, n1_b, qkv_b, probs_b, mixed_b, dmid, da, sums)
        begin("ba", keep, send)

    def back_a_mlp():
        *held["mlp"], keep, send = call(
            "back_a_mlp",
            mlp_backward_kernel,
            [rows_wide, rows_low, sums_shape] + mlp_pair,
            [VMEM] * 9,
            [VMEM] * 5,
            [pltpu.VMEM((ROWS, FF), BF16)],
            vmem=KB_VMEM,
        )(pack, vec, fc1_a, fc2_a, middle_a, n2_a, slope_a, active_a, held["dx"])
        begin("am", keep, send)

    def back_a_attention():
        held["rows"], rows_send, keep, send = call(
            "back_a_attention",
            last_backward_kernel,
            [rows_low] * 2 + attention_pair,
            [VMEM] * 11,
            [VMEM] * 4,
            wide_work + [pltpu.VMEM((ROWS, WIDTH), BF16)],
            vmem=KB_VMEM,
        )(pack, vec, qkv_w, n1_a, qkv_a, probs_a, mixed_a, *held["mlp"], result)
        begin("aa", keep, send)
        held["rows_got"] = swap(rows_send)

    def rows_out():
        ends = [shape(GT, global_ends.shape[1], WIDTH), shape(*local_ends.shape[1:])]
        held["rows_out"] = call(
            "rows_out",
            rows_kernel,
            ends + [MARK],
            [VMEM] * 3,
            [ANY] * 2 + [VMEM],
            [pltpu.VMEM((ROWS, WIDTH), F32)]
            + [pltpu.VMEM(end.shape, BF16) for end in ends]
            + [pltpu.SemaphoreType.DMA((2,))],
            vmem=ROWS_VMEM,
            mark=2,
        )(vec, held["rows"], held["rows_got"])

    def grad(w):
        return shape(*w.shape, dtype=F32)

    def last_sorted(part):
        held[part] = chains["a" + part].last_sorted(chains["b" + part])

    def mlp_out():
        held["mlp_out"] = call(
            "mlp_out",
            mlp_out_kernel,
            [grad(fc1_weight), grad(fc2_weight), MARK],
            [VMEM] * 2,
            [ANY] * 2 + [VMEM],
            [pltpu.VMEM((8, WIDTH, WIDTH), F32), pltpu.SemaphoreType.DMA((8,))],
            vmem=OUT_VMEM,
            mark=2,
        )(*held["m"])

    def attention_out():
        wanted = (
            ln1_gain, ln1_bias, qkv_weight, query_bias, value_bias, proj_weight,
            proj_bias, ln2_gain, ln2_bias, fc1_bias, fc2_bias,
        )
        held["attention_out"] = call(
            "attention_out",
            attention_out_kernel,
            [grad(w) for w in wanted],
            [VMEM] * 4,
            [ANY if w.ndim == 3 else VMEM for w in wanted],
            [pltpu.VMEM((4, WIDTH, WIDTH), F32), pltpu.SemaphoreType.DMA((4,))],
            vmem=LAST_VMEM,
        )(*held["a"], *chains["aa"].sums, *chains["ba"].sums)

    actions = {
        "b": back_b_attention, "c": back_a_mlp, "d": back_a_attention,
        "r": rows_out, "p": mlp_out, "q": attention_out,
        "w": lambda: chains["bm"].advance(), "x": lambda: chains["ba"].advance(),
        "y": lambda: chains["am"].advance(), "z": lambda: chains["aa"].advance(),
        "W": lambda: chains["bm"].last(), "X": lambda: chains["ba"].last(),
        "Y": lambda: last_sorted("m"), "Z": lambda: last_sorted("a"),
    }
    for name in ORDER:
        actions[name]()
    global_out, local_out, _ = held["rows_out"]
    grad_fc1, grad_fc2, _ = held["mlp_out"]
    (
        grad_ln1_gain, grad_ln1_bias, grad_qkv, grad_query_bias, grad_value_bias, grad_proj,
        grad_proj_bias, grad_ln2_gain, grad_ln2_bias, grad_fc1_bias, grad_fc2_bias,
    ) = held["attention_out"]
    return (
        global_out.transpose(1, 0, 2)[None], local_out[None],
        grad_ln1_gain, grad_ln1_bias, grad_qkv, grad_query_bias, grad_value_bias, grad_proj,
        grad_proj_bias, grad_ln2_gain, grad_ln2_bias, grad_fc1, grad_fc1_bias, grad_fc2,
        grad_fc2_bias,
    )


def solution(mesh):
    matrix, vector = P("section", None, None), P("section", None)
    weights = (
        vector, vector, matrix, vector, vector, matrix, vector,
        vector, vector, matrix, vector, matrix, vector,
    )
    rows = P("section", "dp", None, None)
    return jax.shard_map(
        functools.partial(on_device, mesh.shape["dp"]),
        mesh=mesh,
        in_specs=(rows, rows, P("dp"), P("dp")) + weights,
        out_specs=(rows, rows) + weights,
        check_vma=False,
    )
```

```python
import functools

import jax
import jax.numpy as jnp
from jax import lax
from jax.experimental import pallas as pl
from jax.experimental.pallas import tpu as pltpu
from jax.sharding import PartitionSpec as P

HEAD = 64
GT = 197
LT = 37
WIDTH = 384
FF = 1536
SEQ = 208
ROWS = 2 * SEQ
SLOT = 40
LOCALS = 5
VECS = 16
EPSILON = 1e-06
MASKED = -1e30
CHUNK_FF = 768
ORDER = "bcwxydwzxywwxzywyzwyxwzxyzWxzyxzrYXZpq"
DIMS = {
    "bm": ((0, 1, 2, 3), (1, 2, 0, 3)),
    "ba": ((1, 2, 0, 3), (2, 1, 0, 3)),
    "am": ((0, 2, 1, 3), (2, 1, 0, 3)),
    "aa": ((0, 1, 2, 3), (1, 2, 0, 3)),
}
PART_ROWS = {"m": 4 * WIDTH, "a": 2 * WIDTH}
COST = 26214400000
PACK_COST = 10
COSTS = {"bm_halve1": 0.5, "bm_sum": 0.001, "aa_halve0": 0.013, "ba_halve1": 0.002, "bm_halve2": 0.006, "back_a_attention": 0.5, "am_halve1": 0.005, "ba_halve2": 0.001, "aa_halve1": 0.5, "am_halve2": 0.025, "bm_total": 0.125, "am_sum": 0.5, "aa_halve2": 0.125, "bm_join2": 0.125, "am_total": 0.25, "ba_sum": 0.125, "bm_join1": 0.25, "aa_sum": 0.062, "ba_total": 0.02, "am_join2": 0.125, "aa_total": 0.1, "bm_join0": 0.125, "ba_join2": 0.125, "aa_join2": 0.125, "am_join1": 0.25, "ba_join1": 0.013, "aa_join1": 0.125, "back_b_attention": 0.5}
PACK_VMEM = 55
FIRST_VMEM = 8
KA_VMEM = 16
OUT_VMEM = 8
ROWS_VMEM = 8
LAST_VMEM = 8
KB_VMEM = 12
LN1G, LN1B, QB, VB, PB, LN2G, LN2B, F2B, F1B = range(9)
LIVE = 12
PROJ = ROWS + VECS
PACKED = PROJ + WIDTH
BF16 = jnp.bfloat16
F32 = jnp.float32
ANY = pl.BlockSpec(memory_space=pl.ANY)
VMEM = pl.BlockSpec(memory_space=pltpu.VMEM)
SMEM = pl.BlockSpec(memory_space=pltpu.SMEM)


def mm(left, right):
    return jnp.dot(left, right, preferred_element_type=F32)


def mm_right_t(left, right):
    return lax.dot_general(left, right, (((1,), (1,)), ((), ())), preferred_element_type=F32)


def mm_left_t(left, right):
    return lax.dot_general(left, right, (((0,), (0,)), ((), ())), preferred_element_type=F32)


def normalise(values_in):
    centred = values_in - jnp.mean(values_in, axis=-1, keepdims=True)
    scale = lax.rsqrt(jnp.mean(centred * centred, axis=-1, keepdims=True) + EPSILON)
    return centred * scale, scale


def normalise_back(unit, scale, grad_rows, gain):
    e = grad_rows * gain
    return scale * (
        e
        - jnp.mean(e, axis=-1, keepdims=True)
        - unit * jnp.mean(e * unit, axis=-1, keepdims=True)
    )


def seq_rows(seq):
    return pl.ds(pl.multiple_of(seq * SEQ, 16), SEQ)


def column(block):
    return slice(block * WIDTH, (block + 1) * WIDTH)


def wide(part):
    return slice(part * CHUNK_FF, (part + 1) * CHUNK_FF)


def row_sum(values_in):
    return jnp.sum(values_in, axis=0, keepdims=True)


def live_flag(vec, index):
    lane = lax.broadcasted_iota(jnp.int32, (1, WIDTH), 1)
    flags = vec[LIVE : LIVE + 1, :]
    return jnp.sum(jnp.where(lane == index, flags, 0.0), axis=1, keepdims=True)


def pack_kernel(*refs):
    sources, (keep, send), held = refs[:12], refs[12:14], refs[14:26]
    rows, tail, sem = refs[26:]
    g, l, proj, vecs = held[0], held[1], held[2], held[3:]
    copies = [
        pltpu.make_async_copy(source, place, sem.at[i])
        for i, (source, place) in enumerate(zip(sources, held))
    ]
    start_all(copies)
    core = lax.axis_index("section")
    rows[...] = jnp.zeros_like(rows)
    tail[...] = jnp.zeros_like(tail)
    wait_all(copies)
    for i, vec in enumerate(vecs[:8]):
        tail[i : i + 1, :] = vec[...].astype(F32)
    for i in range(FF // WIDTH):
        tail[F1B + i : F1B + i + 1, :] = vecs[8][:, column(i)].astype(F32)
    crops = g[...].astype(F32)
    for out, half in ((keep, core), (send, 1 - core)):
        rows[:GT, :] = jnp.where(half == 0, crops[:, 0, :], crops[:, 1, :])
        for j in range(LOCALS):
            rows[SEQ + j * SLOT : SEQ + j * SLOT + LT, :] = l[half * LOCALS + j].astype(F32)
        out[:ROWS, :] = rows[...].astype(BF16)
        out[ROWS:PROJ, :] = tail[...].astype(BF16)
        out[PROJ:, :] = proj[...]


def crop_of(axis):
    dims = (SEQ, 1) if axis == 0 else (1, SEQ)
    row = lax.broadcasted_iota(jnp.int32, dims, axis)
    crop = jnp.zeros(dims, jnp.int32)
    for j in range(1, LOCALS + 1):
        crop += (row >= j * SLOT).astype(jnp.int32)
    return crop, (crop < LOCALS) & (row - crop * SLOT < LT)


def head_lanes():
    lane = lax.broadcasted_iota(jnp.int32, (SEQ, 2 * HEAD), 1)
    return (lane < HEAD, lane >= HEAD)


def only(mask, values_in):
    return jnp.where(mask, values_in, jnp.zeros_like(values_in))


def attention_forward(x, vec, masks, qkv_w, proj_w, n1, qkv, probs, mixed, middle):
    def body(seq, carry):
        rows = seq_rows(seq)
        x_rows = x[rows, :].astype(F32)
        unit, _ = normalise(x_rows)
        normed = (unit * vec[LN1G : LN1G + 1, :] + vec[LN1B : LN1B + 1, :]).astype(BF16)
        n1[rows, :] = normed
        triple = mm(normed, qkv_w[...])
        query = (triple[:, :WIDTH] + vec[QB : QB + 1, :]).astype(BF16) * BF16(HEAD**-0.5)
        qkv[rows, :WIDTH] = query
        qkv[rows, column(1)] = triple[:, column(1)].astype(BF16)
        qkv[rows, column(2)] = (triple[:, column(2)] + vec[VB : VB + 1, :]).astype(BF16)
        lanes = head_lanes()
        mask = masks[seq]
        for pair in range(3):
            q = qkv[rows, pair * 128 : pair * 128 + 128]
            k = qkv[rows, WIDTH + pair * 128 : WIDTH + pair * 128 + 128]
            v = qkv[rows, 2 * WIDTH + pair * 128 : 2 * WIDTH + pair * 128 + 128]
            total = None
            for a in range(2):
                s = mm_right_t(only(lanes[a], k), q) + mask
                e = jnp.exp(s - jnp.max(s, axis=0, keepdims=True))
                p = (e * (1.0 / jnp.sum(e, axis=0, keepdims=True))).astype(BF16)
                probs[seq * 6 + pair * 2 + a] = p
                part = mm_left_t(p, only(lanes[a], v))
                total = part if total is None else total + part
            mixed[rows, pair * 128 : pair * 128 + 128] = total.astype(BF16)
        middle[rows, :] = x_rows + (mm(mixed[rows, :], proj_w[...]) + vec[PB : PB + 1, :])
        return carry

    lax.fori_loop(0, 2, body, 0, unroll=True)


def wide_bias(vec, part):
    rows = CHUNK_FF // 128
    pieces = []
    for i in range(part * rows, (part + 1) * rows):
        row, lane = F1B + i * 128 // WIDTH, i * 128 % WIDTH
        pieces.append(vec[row : row + 1, lane : lane + 128])
    return jnp.concatenate(pieces, axis=1)


def mlp_forward(vec, fc1_w, fc2_w, middle, n2, slope, active, result):
    def body(seq, carry):
        rows = seq_rows(seq)
        unit, _ = normalise(middle[rows, :])
        normed = (unit * vec[LN2G : LN2G + 1, :] + vec[LN2B : LN2B + 1, :]).astype(BF16)
        n2[rows, :] = normed
        for part in range(FF // CHUNK_FF):
            hidden = mm(normed, fc1_w[:, wide(part)]) + wide_bias(vec, part)
            cdf = 0.5 + 0.5 * lax.erf(hidden * (0.5**0.5))
            active[rows, wide(part)] = (hidden * cdf).astype(BF16)
            density = jnp.exp(hidden * hidden * -0.5) * 0.3989422804014327
            slope[rows, wide(part)] = (cdf + hidden * density).astype(BF16)
        y = middle[rows, :] + (mm(active[rows, :], fc2_w[...]) + vec[F2B : F2B + 1, :])
        result[rows, :] = y.astype(BF16)
        return carry

    lax.fori_loop(0, 2, body, 0, unroll=True)


def mlp_backward(vec, fc1_w, fc2_w, middle, n2, slope, active, dy, dh, dmid, da, sums, emit):
    def body(seq, carry):
        rows = seq_rows(seq)
        dy_rows = dy[rows, :]
        for part in range(FF // WIDTH):
            dactive = mm_right_t(dy_rows, fc2_w[column(part), :])
            low = (slope[rows, column(part)].astype(F32) * dactive).astype(BF16)
            dh[rows, column(part)] = low
            sums[F1B + part : F1B + part + 1, :] += row_sum(low.astype(F32))
        dn2 = mm_right_t(dh[rows, :], fc1_w[...])
        unit, scale = normalise(middle[rows, :])
        dy_wide = dy_rows.astype(F32)
        grad = dy_wide + normalise_back(unit, scale, dn2, vec[LN2G : LN2G + 1, :])
        dmid[rows, :] = grad
        low = grad.astype(BF16)
        da[rows, :] = low
        sums[LN2G : LN2G + 1, :] += row_sum(dn2 * unit)
        sums[LN2B : LN2B + 1, :] += row_sum(dn2)
        sums[F2B : F2B + 1, :] += row_sum(dy_wide)
        sums[PB : PB + 1, :] += row_sum(low.astype(F32))
        return carry

    lax.fori_loop(0, 2, body, 0, unroll=True)
    for pair in range(2):
        parts = (column(2 * pair), column(2 * pair + 1))
        emit(pair, *(mm_left_t(active[:, part], dy[:ROWS, :]) for part in parts))
    for part in range(2):
        value = mm_left_t(n2[...], dh[:, part * 2 * WIDTH : (part + 1) * 2 * WIDTH])
        emit(2 + part, value[:, :WIDTH], value[:, WIDTH:])


def attention_backward(
    x, vec, qkv_w, proj_w, n1, qkv, probs, mixed, dmid, da, dt, sums, emit, result
):
    def body(seq, carry):
        rows = seq_rows(seq)
        dmixed = mm_right_t(da[rows, :], proj_w[...]).astype(BF16)
        lanes = head_lanes()
        for pair in range(3):
            q = qkv[rows, pair * 128 : pair * 128 + 128]
            k = qkv[rows, WIDTH + pair * 128 : WIDTH + pair * 128 + 128]
            v = qkv[rows, 2 * WIDTH + pair * 128 : 2 * WIDTH + pair * 128 + 128]
            dm = dmixed[:, pair * 128 : pair * 128 + 128]
            dq = dk = dv = None
            for a in range(2):
                dm_a = only(lanes[a], dm)
                p = probs[seq * 6 + pair * 2 + a]
                dp = mm_right_t(only(lanes[a], v), dm)
                p_wide = p.astype(F32)
                ds = p_wide * (dp - jnp.sum(dp * p_wide, axis=0, keepdims=True))
                ds = ds.astype(BF16)
                parts = (
                    mm_left_t(ds, only(lanes[a], k)),
                    mm(ds, only(lanes[a], q)),
                    mm(p, dm_a),
                )
                if a == 0:
                    dq, dk, dv = parts
                else:
                    dq, dk, dv = dq + parts[0], dk + parts[1], dv + parts[2]
            dq = (dq * HEAD**-0.5).astype(BF16)
            dv = dv.astype(BF16)
            here = slice(pair * 128, pair * 128 + 128)
            dt[rows, pair * 128 : pair * 128 + 128] = dq
            dt[rows, WIDTH + pair * 128 : WIDTH + pair * 128 + 128] = dk.astype(BF16)
            dt[rows, 2 * WIDTH + pair * 128 : 2 * WIDTH + pair * 128 + 128] = dv
            sums[QB : QB + 1, here] += row_sum(dq.astype(F32))
            sums[VB : VB + 1, here] += row_sum(dv.astype(F32))
        dn1 = mm_right_t(dt[rows, :], qkv_w[...])
        unit, scale = normalise(x[rows, :].astype(F32))
        grad = dmid[rows, :] + normalise_back(unit, scale, dn1, vec[LN1G : LN1G + 1, :])
        result[rows, :] = grad.astype(BF16)
        sums[LN1G : LN1G + 1, :] += row_sum(dn1 * unit)
        sums[LN1B : LN1B + 1, :] += row_sum(dn1)
        return carry

    lax.fori_loop(0, 2, body, 0, unroll=True)
    value = mm_left_t(n1[...], dt[...])
    emit(0, mm_left_t(mixed[...], da[...]), value[:, column(0)])
    emit(1, value[:, column(1)], value[:, column(2)])


def make_emit(keep, send, core):
    def emit(pair, first, second):
        rows = slice(pair * WIDTH, (pair + 1) * WIDTH)
        first, second = first.astype(BF16), second.astype(BF16)
        keep[rows, :] = jnp.where(core == 0, first, second)
        send[rows, :] = jnp.where(core == 0, second, first)

    return emit


def start_all(copies):
    for copy in copies:
        copy.start()


def wait_all(copies):
    for copy in copies:
        copy.wait()


def hold_flags(glive, llive, vec, dy):
    core = lax.axis_index("section")
    lane = lax.broadcasted_iota(jnp.int32, (1, WIDTH), 1)
    flags = jnp.zeros((1, WIDTH), F32)
    for i in range(2):
        flags = jnp.where(lane == i, glive[i].astype(F32), flags)
    for i in range(2 * LOCALS):
        flags = jnp.where(lane == 2 + i, llive[i].astype(F32), flags)
    vec[LIVE : LIVE + 1, :] = flags
    crop, _ = crop_of(0)
    live = jnp.zeros((SEQ, 1), F32)
    for j in range(LOCALS):
        live = jnp.where(crop == j, llive[core * LOCALS + j].astype(F32), live)
    dy[:SEQ, :] = (dy[:SEQ, :].astype(F32) * glive[core].astype(F32)).astype(BF16)
    dy[SEQ:ROWS, :] = (dy[SEQ:ROWS, :].astype(F32) * live).astype(BF16)


def sort_by_core(own, got, first, second):
    core = lax.axis_index("section")
    first[...] = jnp.where(core == 0, own[...], got[...])
    second[...] = jnp.where(core == 0, got[...], own[...])


def settle_kernel(_, own, got, masks, qkv_w):
    key = lax.broadcasted_iota(jnp.int32, (SEQ, SEQ), 0)
    masks[0] = jnp.where(key < GT, 0.0, MASKED)
    key_crop, true_key = crop_of(0)
    query_crop, _ = crop_of(1)
    masks[1] = jnp.where(jnp.where(true_key, key_crop, -1) == query_crop, 0.0, MASKED)
    sort_by_core(own, got, qkv_w.at[0], qkv_w.at[1])


def first_attention_kernel(*refs):
    (
        glive, llive, keep, recv, qkv_w, masks,
        pack, vec, n1, qkv, probs, mixed, middle,
    ) = refs
    sort_by_core(keep, recv, pack.at[0], pack.at[1])
    for layer in range(2):
        vec[layer] = pack[layer, ROWS:PROJ, :].astype(F32)
    hold_flags(glive, llive, vec.at[0], pack.at[1])
    attention_forward(
        pack.at[0], vec.at[0], masks, qkv_w.at[0], pack.at[0, pl.ds(PROJ, WIDTH)],
        n1, qkv, probs, mixed, middle,
    )


def forward_kernel(*refs):
    (
        fc1_own, fc2_own, fc1_got, fc2_got, pack, qkv_w, vec, masks, middle_a,
        fc1_a, fc2_a, between, result, n2_a, slope_a, active_a,
        n1_b, qkv_b, probs_b, mixed_b, dmid, da, sums, keep_out, send_out,
        fc1_b, fc2_b, middle_b, n2_b, slope_b, active_b, dh,
    ) = refs
    core = lax.axis_index("section")
    sort_by_core(fc1_own, fc1_got, fc1_a, fc1_b)
    sort_by_core(fc2_own, fc2_got, fc2_a, fc2_b)
    sums[...] = jnp.zeros_like(sums)
    mlp_forward(vec.at[0], fc1_a, fc2_a, middle_a, n2_a, slope_a, active_a, between)
    attention_forward(
        between, vec.at[1], masks, qkv_w.at[1], pack.at[1, pl.ds(PROJ, WIDTH)],
        n1_b, qkv_b, probs_b, mixed_b, middle_b,
    )
    mlp_forward(vec.at[1], fc1_b, fc2_b, middle_b, n2_b, slope_b, active_b, result)
    mlp_backward(
        vec.at[1], fc1_b, fc2_b, middle_b, n2_b, slope_b, active_b, pack.at[1], dh, dmid, da,
        sums, make_emit(keep_out, send_out, core),
    )


def attention_backward_kernel(layer, *refs):
    (
        x, pack, vec, qkv_w, n1, qkv, probs, mixed, dmid, da, sums_in,
        dx, keep_out, send_out, dt, sums,
    ) = refs
    core = lax.axis_index("section")
    sums[...] = sums_in[...]
    attention_backward(
        x, vec.at[layer], qkv_w.at[layer], pack.at[layer, pl.ds(PROJ, WIDTH)], n1, qkv, probs,
        mixed, dmid, da, dt, sums, make_emit(keep_out, send_out, core), dx,
    )
    keep_out[2 * WIDTH :, :] = sums[...].astype(BF16)
    send_out[2 * WIDTH :, :] = sums[...].astype(BF16)


def last_backward_kernel(*refs):
    pack, result, rows_keep, rows_send, dx = refs[0], refs[10], refs[11], refs[12], refs[-1]
    attention_backward_kernel(0, pack.at[0], *refs[:10], dx, *refs[13:17])
    core = lax.axis_index("section")

    rows_keep[...] = jnp.where(core == 0, dx[...], result[...])
    rows_send[...] = jnp.where(core == 0, result[...], dx[...])


def mlp_backward_kernel(*refs):
    (
        _, vec, fc1_w, fc2_w, middle, n2, slope, active, dy,
        dmid, da, sums, keep_out, send_out, dh,
    ) = refs
    core = lax.axis_index("section")
    sums[...] = jnp.zeros_like(sums)
    mlp_backward(
        vec.at[0], fc1_w, fc2_w, middle, n2, slope, active, dy, dh, dmid, da, sums, make_emit(keep_out, send_out, core),
    )


def rows_kernel(vec, keep, recv, g_out, l_out, mark, wide, g, l, sem):
    mark[...] = jnp.zeros_like(mark)
    core = lax.axis_index("section")
    globals_live = []
    for source, half in ((keep, core), (recv, 1 - core)):
        wide[...] = source[...].astype(F32)
        live = jnp.where(core == 1, live_flag(vec.at[0], half), 1.0)
        globals_live.append(wide[:GT, :] * live)
        for j in range(LOCALS):
            crop = half * LOCALS + j
            live = jnp.where(core == 1, live_flag(vec.at[0], 2 + crop), 1.0)
            piece = wide[SEQ + j * SLOT : SEQ + j * SLOT + LT, :]
            l[crop] = (piece * live).astype(BF16)
    g[:, 0, :] = jnp.where(core == 0, *globals_live).astype(BF16)
    g[:, 1, :] = jnp.where(core == 1, *globals_live).astype(BF16)
    copies = [
        pltpu.make_async_copy(g, g_out, sem.at[0]),
        pltpu.make_async_copy(l, l_out, sem.at[1]),
    ]
    start_all(copies)
    wait_all(copies)


def out_block(own, got, index):
    core = lax.axis_index("section")
    place = index // 2
    rows = slice(place * WIDTH, (place + 1) * WIDTH)
    return jnp.where(core == index % 2, own[rows, :], got[rows, :]).astype(F32)


def write_blocks(own, got, places, held, sem):
    copies = []
    for i, place in enumerate(places):
        held[i] = out_block(own, got, i)
        copies.append(pltpu.make_async_copy(held.at[i], place, sem.at[i]))
        copies[-1].start()
    return copies


def mlp_out_kernel(own, got, fc1, fc2, mark, held, sem):
    mark[...] = jnp.zeros_like(mark)
    places = [fc2.at[0, column(part), :] for part in range(4)]
    places += [fc1.at[0, :, column(part)] for part in range(4)]
    wait_all(write_blocks(own, got, places, held, sem))


def attention_out_kernel(*refs):
    (
        own, got, sums_a, sums_b,
        ln1g, ln1b, qkv, qb, vb, proj, pb, ln2g, ln2b, fc1b, fc2b, held, sem,
    ) = refs
    places = [proj.at[0]] + [qkv.at[0, :, column(part)] for part in range(3)]
    copies = write_blocks(own, got, places, held, sem)
    core = lax.axis_index("section")
    sums = jnp.where(core == 0, sums_a[...], sums_b[...])
    for out, row in (
        (ln1g, LN1G), (ln1b, LN1B), (qb, QB), (vb, VB), (pb, PB), (ln2g, LN2G), (ln2b, LN2B),
        (fc2b, F2B),
    ):
        out[...] = sums[row : row + 1, :]
    for part in range(4):
        fc1b[:, column(part)] = sums[F1B + part : F1B + part + 1, :]
    wait_all(copies)


def shape(*dims, dtype=BF16):
    return jax.ShapeDtypeStruct(dims, dtype)


MARK = shape(8, 128, dtype=F32)


class Ordered:
    def __init__(self):
        self.last = None

    def __call__(
        self, name, kernel, outs, in_specs, out_specs, scratch=(), vmem=8, cost=1, mark=0
    ):
        before = [] if self.last is None else [self.last]
        count = len(in_specs)

        def body(*refs):
            kernel(*refs[:count], *refs[count + len(before) :])

        def run(*args):
            results = pl.pallas_call(
                body,
                out_shape=outs,
                name=name,
                in_specs=list(in_specs) + [ANY] * len(before),
                out_specs=out_specs,
                scratch_shapes=list(scratch),
                compiler_params=pltpu.CompilerParams(vmem_limit_bytes=int(vmem * 1024 * 1024)),
                cost_estimate=pl.CostEstimate(
                    flops=int(COSTS.get(name, cost) * COST),
                    bytes_accessed=0,
                    transcendentals=0,
                ),
            )(*args, *before)
            self.last = results[mark]
            return results

        return run


CHUNK = 48


def add_rows(out, start_out, left, right, start, count):
    def step(i, carry):
        here = pl.ds(pl.multiple_of(start + i * CHUNK, 16), CHUNK)
        there = pl.ds(pl.multiple_of(start_out + i * CHUNK, 16), CHUNK)
        out[there, :] = (left[here, :].astype(F32) + right[here, :].astype(F32)).astype(BF16)
        return carry

    lax.fori_loop(0, count // CHUNK, step, 0, unroll=2)


def add_tail(outs, start_out, left, right, start):
    if left.shape[0] == start:
        return
    here = slice(start, start + VECS)
    tail = (left[here, :].astype(F32) + right[here, :].astype(F32)).astype(BF16)
    for out in outs:
        out[start_out : start_out + VECS, :] = tail


def bit_of(dims, step):
    dp = lax.axis_index("dp")
    core = lax.axis_index("section")
    return jnp.where(core == 0, dp >> dims[0][step] & 1, dp >> dims[1][step] & 1)


def halve_kernel(dims, step, count, keep, recv, keep_out, send_out):
    bit = bit_of(dims, step)
    half = count // 2
    add_rows(send_out, 0, keep, recv, (1 - bit) * half, half)
    add_rows(keep_out, 0, keep, recv, bit * half, half)
    add_tail((keep_out, send_out), half, keep, recv, count)


def sum_kernel(count, keep, recv, out):
    add_rows(out, 0, keep, recv, 0, count)
    add_tail((out,), count, keep, recv, count)


def total_kernel(count, own, recv, total_out, *sums_out):
    add_rows(total_out, 0, own, recv, 0, count)
    for out in sums_out:
        out[...] = own[count:, :].astype(F32) + recv[count:, :].astype(F32)


def join_rows(out, own, recv, bit):
    count = own.shape[0]
    for ref, half in ((own, bit), (recv, 1 - bit)):
        out[pl.ds(pl.multiple_of(half * count, 16), count), :] = ref[...]


def join_kernel(dims, step, own, recv, out):
    join_rows(out, own, recv, bit_of(dims, step))


def last_join_kernel(dims, own, recv, other, mine, send):
    bit = bit_of(dims, 0)
    core = lax.axis_index("section")

    @pl.when(core == 0)
    def _():
        join_rows(mine, own, recv, bit)
        send[...] = other[...]

    @pl.when(core == 1)
    def _():
        join_rows(send, own, recv, bit)
        mine[...] = other[...]


def exchange(values_in, dims, step):
    pairs = [
        (core * 16 + dp, core * 16 + (dp ^ 1 << dims[core][step]))
        for core in range(2)
        for dp in range(16)
    ]
    return lax.ppermute(values_in, ("section", "dp"), pairs)


class Reduction:
    def __init__(self, name, call, dims, keep, send, count):
        self.name, self.call, self.dims = name, call, dims
        self.keep, self.recv, self.count = keep, swap(send), count
        self.steps = self.run(count, keep.shape[0] - count)

    def kernel(self, label, body, rows, *args):
        outs = [shape(n, WIDTH) for n in rows]
        return self.call(
            f"{self.name}_{label}", body, outs, [VMEM] * len(args), [VMEM] * len(outs)
        )(*args)

    def run(self, count, tail):
        keep, recv = self.keep, self.recv
        for step in range(3):
            body = functools.partial(halve_kernel, self.dims, step, count)
            count //= 2
            keep, send = self.kernel(f"halve{step}", body, [count + tail] * 2, keep, recv)
            recv = exchange(send, self.dims, step)
            yield
        body = functools.partial(sum_kernel, count)
        (own,) = self.kernel("sum", body, [count + tail], keep, recv)
        recv = exchange(own, self.dims, 3)
        yield
        whole, *sums = self.call(
            f"{self.name}_total",
            functools.partial(total_kernel, count),
            [shape(count, WIDTH)] + [shape(tail, WIDTH, dtype=F32)] * bool(tail),
            [VMEM] * 2,
            [VMEM] * (1 + bool(tail)),
        )(own, recv)
        self.sums = sums
        for step in (2, 1, 0):
            recv = exchange(whole, self.dims, step)
            self.pair = (whole, recv)
            yield
            if step:
                body = functools.partial(join_kernel, self.dims, step)
                (whole,) = self.kernel(f"join{step}", body, [2 * whole.shape[0]], whole, recv)

    def advance(self):
        next(self.steps)

    def last(self):
        assert 2 * self.pair[0].shape[0] == self.count
        body = functools.partial(join_kernel, self.dims, 0)
        (self.whole,) = self.kernel("join0", body, [self.count], *self.pair)

    def last_sorted(self, other):
        assert 2 * self.pair[0].shape[0] == self.count
        mine, send = self.call(
            f"{self.name}_last",
            functools.partial(last_join_kernel, self.dims),
            [shape(self.count, WIDTH)] * 2,
            [VMEM] * 3,
            [VMEM] * 2,
        )(*self.pair, other.whole)
        return mine, swap(send)


class PlainReduction(Reduction):
    def advance(self):
        pass

    def last(self):
        total = lax.psum(self.keep.astype(F32) + self.recv.astype(F32), "dp")
        self.whole = total[: self.count].astype(BF16)
        self.sums = [total[self.count :]] * (total.shape[0] > self.count)

    def last_sorted(self, other):
        self.last()
        leading = lax.axis_index("section") == 0
        pair = (self.whole, other.whole)
        return jnp.where(leading, *pair), swap(jnp.where(leading, *pair[::-1]))


def swap(values_in):
    return lax.ppermute(values_in, "section", [(0, 1), (1, 0)])


def on_device(dp_size, global_ends, local_ends, global_live, local_live, *weights):
    (
        ln1_gain, ln1_bias, qkv_weight, query_bias, value_bias, proj_weight, proj_bias,
        ln2_gain, ln2_bias, fc1_weight, fc1_bias, fc2_weight, fc2_bias,
    ) = weights
    qkv_own, fc1_own, fc2_own = (w[0] for w in (qkv_weight, fc1_weight, fc2_weight))
    qkv_got = swap(qkv_own)
    vectors = (
        ln1_gain, ln1_bias, query_bias, value_bias, proj_bias, ln2_gain, ln2_bias, fc2_bias,
        fc1_bias,
    )
    call = Ordered()
    packed = [global_ends[0].transpose(1, 0, 2), local_ends[0], proj_weight[0], *vectors]
    keep, send = call(
        "pack",
        pack_kernel,
        [shape(PACKED, WIDTH)] * 2,
        [ANY] * len(packed),
        [VMEM] * 2,
        [pltpu.VMEM(v.shape, BF16) for v in packed]
        + [
            pltpu.VMEM((ROWS, WIDTH), F32),
            pltpu.VMEM((VECS, WIDTH), F32),
            pltpu.SemaphoreType.DMA((len(packed),)),
        ],
        vmem=PACK_VMEM,
        cost=PACK_COST,
    )(*packed)
    recv = swap(send)
    fc1_own, fc2_own, _ = lax.optimization_barrier((fc1_own, fc2_own, send))
    fc1_got, fc2_got = swap(fc1_own), swap(fc2_own)
    rows_low, rows_wide = shape(ROWS, WIDTH), shape(ROWS, WIDTH, dtype=F32)
    hidden_low = shape(ROWS, FF)
    triple_low = shape(ROWS, 3 * WIDTH)
    weights_low = [shape(WIDTH, FF), shape(FF, WIDTH)]
    sums_shape = shape(VECS, WIDTH, dtype=F32)
    mlp_pair = [shape(4 * WIDTH, WIDTH)] * 2
    attention_pair = [shape(2 * WIDTH + VECS, WIDTH)] * 2
    attention_saved = [rows_low, triple_low, shape(12, SEQ, SEQ), rows_low]
    mlp_saved = [rows_wide, rows_low, hidden_low, hidden_low]
    masks_shape = shape(2, SEQ, SEQ, dtype=F32)
    masks, qkv_w = call(
        "settle",
        settle_kernel,
        [masks_shape, shape(2, WIDTH, 3 * WIDTH)],
        [VMEM] * 3,
        [VMEM] * 2,
    )(keep, qkv_own, qkv_got)
    outs = [shape(2, PACKED, WIDTH), shape(2, VECS, WIDTH, dtype=F32)]
    outs += attention_saved + [rows_wide]
    pack, vec, n1_a, qkv_a, probs_a, mixed_a, middle_a = call(
        "first_attention",
        first_attention_kernel,
        outs,
        [SMEM] * 2 + [VMEM] * 4,
        [VMEM] * len(outs),
        vmem=FIRST_VMEM,
        mark=1,
    )(global_live, local_live, keep, recv, qkv_w, masks)
    outs = weights_low + [rows_low] * 2 + mlp_saved[1:] + attention_saved
    outs += [rows_wide, rows_low, sums_shape] + mlp_pair
    (
        fc1_a, fc2_a, between, result, n2_a, slope_a, active_a,
        n1_b, qkv_b, probs_b, mixed_b, dmid, da, sums, keep_1, send_1,
    ) = call(
        "forward",
        forward_kernel,
        outs,
        [VMEM] * 9,
        [VMEM] * len(outs),
        [pltpu.VMEM(held.shape, held.dtype) for held in weights_low + mlp_saved]
        + [pltpu.VMEM((ROWS, FF), BF16)],
        vmem=KA_VMEM,
        mark=13,
    )(fc1_own, fc2_own, fc1_got, fc2_got, pack, qkv_w, vec, masks, middle_a)
    reduction = Reduction if dp_size == 16 else PlainReduction
    chains, held = {}, {}

    def begin(name, keep, send):
        count = PART_ROWS[name[1]]
        chains[name] = reduction(name, call, DIMS[name], keep, send, count)

    begin("bm", keep_1, send_1)
    wide_work = [pltpu.VMEM((ROWS, 3 * WIDTH), BF16), pltpu.VMEM((VECS, WIDTH), F32)]
    def back_b_attention():
        held["dx"], keep, send = call(
            "back_b_attention",
            functools.partial(attention_backward_kernel, 1),
            [rows_low] + attention_pair,
            [VMEM] * 11,
            [VMEM] * 3,
            wide_work,
            vmem=KB_VMEM,
        )(between, pack, vec, qkv_w, n1_b, qkv_b, probs_b, mixed_b, dmid, da, sums)
        begin("ba", keep, send)

    def back_a_mlp():
        *held["mlp"], keep, send = call(
            "back_a_mlp",
            mlp_backward_kernel,
            [rows_wide, rows_low, sums_shape] + mlp_pair,
            [VMEM] * 9,
            [VMEM] * 5,
            [pltpu.VMEM((ROWS, FF), BF16)],
            vmem=KB_VMEM,
        )(pack, vec, fc1_a, fc2_a, middle_a, n2_a, slope_a, active_a, held["dx"])
        begin("am", keep, send)

    def back_a_attention():
        held["rows"], rows_send, keep, send = call(
            "back_a_attention",
            last_backward_kernel,
            [rows_low] * 2 + attention_pair,
            [VMEM] * 11,
            [VMEM] * 4,
            wide_work + [pltpu.VMEM((ROWS, WIDTH), BF16)],
            vmem=KB_VMEM,
        )(pack, vec, qkv_w, n1_a, qkv_a, probs_a, mixed_a, *held["mlp"], result)
        begin("aa", keep, send)
        held["rows_got"] = swap(rows_send)

    def rows_out():
        ends = [shape(GT, global_ends.shape[1], WIDTH), shape(*local_ends.shape[1:])]
        held["rows_out"] = call(
            "rows_out",
            rows_kernel,
            ends + [MARK],
            [VMEM] * 3,
            [ANY] * 2 + [VMEM],
            [pltpu.VMEM((ROWS, WIDTH), F32)]
            + [pltpu.VMEM(end.shape, BF16) for end in ends]
            + [pltpu.SemaphoreType.DMA((2,))],
            vmem=ROWS_VMEM,
            mark=2,
        )(vec, held["rows"], held["rows_got"])

    def grad(w):
        return shape(*w.shape, dtype=F32)

    def last_sorted(part):
        held[part] = chains["a" + part].last_sorted(chains["b" + part])

    def mlp_out():
        held["mlp_out"] = call(
            "mlp_out",
            mlp_out_kernel,
            [grad(fc1_weight), grad(fc2_weight), MARK],
            [VMEM] * 2,
            [ANY] * 2 + [VMEM],
            [pltpu.VMEM((8, WIDTH, WIDTH), F32), pltpu.SemaphoreType.DMA((8,))],
            vmem=OUT_VMEM,
            mark=2,
        )(*held["m"])

    def attention_out():
        wanted = (
            ln1_gain, ln1_bias, qkv_weight, query_bias, value_bias, proj_weight,
            proj_bias, ln2_gain, ln2_bias, fc1_bias, fc2_bias,
        )
        held["attention_out"] = call(
            "attention_out",
            attention_out_kernel,
            [grad(w) for w in wanted],
            [VMEM] * 4,
            [ANY if w.ndim == 3 else VMEM for w in wanted],
            [pltpu.VMEM((4, WIDTH, WIDTH), F32), pltpu.SemaphoreType.DMA((4,))],
            vmem=LAST_VMEM,
        )(*held["a"], *chains["aa"].sums, *chains["ba"].sums)

    actions = {
        "b": back_b_attention, "c": back_a_mlp, "d": back_a_attention,
        "r": rows_out, "p": mlp_out, "q": attention_out,
        "w": lambda: chains["bm"].advance(), "x": lambda: chains["ba"].advance(),
        "y": lambda: chains["am"].advance(), "z": lambda: chains["aa"].advance(),
        "W": lambda: chains["bm"].last(), "X": lambda: chains["ba"].last(),
        "Y": lambda: last_sorted("m"), "Z": lambda: last_sorted("a"),
    }
    for name in ORDER:
        actions[name]()
    global_out, local_out, _ = held["rows_out"]
    grad_fc1, grad_fc2, _ = held["mlp_out"]
    (
        grad_ln1_gain, grad_ln1_bias, grad_qkv, grad_query_bias, grad_value_bias, grad_proj,
        grad_proj_bias, grad_ln2_gain, grad_ln2_bias, grad_fc1_bias, grad_fc2_bias,
    ) = held["attention_out"]
    return (
        global_out.transpose(1, 0, 2)[None], local_out[None],
        grad_ln1_gain, grad_ln1_bias, grad_qkv, grad_query_bias, grad_value_bias, grad_proj,
        grad_proj_bias, grad_ln2_gain, grad_ln2_bias, grad_fc1, grad_fc1_bias, grad_fc2,
        grad_fc2_bias,
    )


def solution(mesh):
    matrix, vector = P("section", None, None), P("section", None)
    weights = (
        vector, vector, matrix, vector, vector, matrix, vector,
        vector, vector, matrix, vector, matrix, vector,
    )
    rows = P("section", "dp", None, None)
    return jax.shard_map(
        functools.partial(on_device, mesh.shape["dp"]),
        mesh=mesh,
        in_specs=(rows, rows, P("dp"), P("dp")) + weights,
        out_specs=(rows, rows) + weights,
        check_vma=False,
    )
```
